32 devices in a mesh: band: 8 (over z, core), img: 4 (over y, x).
Axes of the slice: x: 2, y: 2, z: 4, core: 2. Of those that a mesh axis runs over, the one named last changes fastest.
Arguments:
- x_small: bfloat16 [16, 24, 16, 512], P('img', 'band'), may hold values from -6 to 6
- x_medium: bfloat16 [24, 32, 24, 512], P('img', 'band'), may hold values from -6 to 6
- x_large: bfloat16 [8, 48, 32, 512], P('img', 'band'), may hold values from -6 to 6
- cot_small: bfloat16 [16, 24, 16, 512], P('img', 'band'), may hold values from -6 to 6
- cot_medium: bfloat16 [24, 32, 24, 512], P('img', 'band'), may hold values from -6 to 6
- cot_large: bfloat16 [8, 48, 32, 512], P('img', 'band'), may hold values from -6 to 6
- band_rows: int32 [3, 8], replicated, may hold values from 1 to 6, as said below
- params: float32 [11296, 512], P(('band', 'img'))
- first_moment: float32 [11296, 512], P(('band', 'img')), may hold values from -640 to 640
- second_moment: float32 [11296, 512], P(('band', 'img')), may hold values from 1000 to 100000
- step: int32 [1], replicated, may hold values from 1 to 9
- rate: float32 [1], replicated, may hold values from 0.001 to 0.01
Outputs:
- out_small: bfloat16 [16, 24, 16, 512], P('img', 'band')
- out_medium: bfloat16 [24, 32, 24, 512], P('img', 'band')
- out_large: bfloat16 [8, 48, 32, 512], P('img', 'band')
- again_small: bfloat16 [16, 24, 16, 512], P('img', 'band')
- again_medium: bfloat16 [24, 32, 24, 512], P('img', 'band')
- again_large: bfloat16 [8, 48, 32, 512], P('img', 'band')
- grad_small: bfloat16 [16, 24, 16, 512], P('img', 'band')
- grad_medium: bfloat16 [24, 32, 24, 512], P('img', 'band')
- grad_large: bfloat16 [8, 48, 32, 512], P('img', 'band')
- weight_update: float32 [11296, 512], P(('band', 'img'))
- new_first: float32 [11296, 512], P(('band', 'img'))
- new_second: float32 [11296, 512], P(('band', 'img'))
The draws below stay inside these ranges and needn't reach their ends.
Inputs may be any that keep to these rules, and one draw needn't show every extreme that they name: Row s of band_rows belongs to the side in (16, 24, 32); its entries sum to that side and its largest entry is exactly (3, 4, 6) for that side, every entry at least 1.
All inputs are finite; a program needn't handle non-finite values.
Results may differ from the reference program's by a relative error of at most 0.017.
Values may be sent and summed in bfloat16 or wider, within the bound.
No kernel may reach another device: no remote copies, remote signals or barrier semaphores. Data moves between devices by JAX's collectives and lax.ppermute only.
A program may use at most 192 MiB of HBM per device.

```python
import math
import jax
import jax.numpy as jnp
from jax import lax

C = 512
GROUPS = 32
SIDE_S = 16
SIDE_M = 24
SIDE_L = 32
CAP_S = 3
CAP_M = 4
CAP_L = 6
BATCH_S = 16
BATCH_M = 24
BATCH_L = 8
ROWS_S = 24
ROWS_M = 32
ROWS_L = 48
PROWS = 11296
N_BAND = 8


def band_lengths(key, side, slots):
    order = jax.random.permutation(key, N_BAND).astype(jnp.int32)
    placing = jnp.zeros((N_BAND,), jnp.int32).at[order].set(jnp.arange(N_BAND, dtype=jnp.int32))
    leftover = side - N_BAND - (slots - 1)
    extra = jnp.clip(leftover - (slots - 1) * (placing - 1), 0, slots - 1)
    extra = jnp.where(placing == 0, slots - 1, extra)
    return (1 + extra).astype(jnp.int32)


def draw_band_rows(key, part):
    key = jax.random.fold_in(key, 5)
    subkeys = jax.random.split(key, 3)
    return jnp.stack([band_lengths(subkeys[0], SIDE_S, CAP_S), band_lengths(subkeys[1], SIDE_M, CAP_M), band_lengths(subkeys[2], SIDE_L, CAP_L)]).astype(jnp.int32)


def draw_params(key, part):
    key = jax.random.fold_in(key, 11)
    subkeys = jax.random.split(key, 2)
    base = jax.random.normal(subkeys[0], (PROWS, C), jnp.float32)
    row_ids = jnp.arange(PROWS, dtype=jnp.int32)
    small_ids = row_ids - 22 * C
    scaling = jnp.where(row_ids < 18 * C, (9.0 * C) ** (-0.5), jnp.where(row_ids < 21 * C, C ** (-0.5), jnp.where(row_ids < 22 * C, 12.0 * C ** (-0.5), 0.5)))
    values = base * scaling[:, None]
    gains = jax.random.uniform(subkeys[1], (PROWS, C), jnp.float32, 0.5, 1.5)
    gain_rows = (small_ids == 0) | (small_ids == 3) | (small_ids == 6)
    values = jnp.where(gain_rows[:, None], gains, values)
    return jnp.where((row_ids < 22 * C + 11)[:, None], values, 0.0).astype(jnp.float32)


def level_of(stream_key, shape, shards, smallest, high):
    level, own = 1.0, jax.random.fold_in(stream_key, 6)
    for axis_at, parts in shards:
        steps = jnp.exp(jax.random.uniform(jax.random.fold_in(own, axis_at), (parts,), jnp.float32, smallest / len(shards), high / len(shards)))
        level = level * jnp.repeat(steps, shape[axis_at] // parts).reshape([-1 if axis == axis_at else 1 for axis in range(len(shape))])
    return level


def gaussian(stream_key, extent, scale, limit, cuts=(), held_as=jnp.bfloat16):
    factor_of = level_of(stream_key, extent, cuts, -0.22, 0.18) if cuts else 1.0
    entries = jax.random.normal(stream_key, extent, jnp.float32) * scale * factor_of
    return jnp.minimum(jnp.maximum(entries, -limit), limit).astype(held_as)


def setup_inputs(seed: int = 0) -> dict:
    arg_keys = jax.random.split(jax.random.key(seed), 13)
    x_small = gaussian(arg_keys[0], (BATCH_S, ROWS_S, SIDE_S, C), 1.0, 6.0, ((0, 4), (1, 8)))
    x_medium = gaussian(arg_keys[1], (BATCH_M, ROWS_M, SIDE_M, C), 1.0, 6.0, ((0, 4), (1, 8)))
    x_large = gaussian(arg_keys[2], (BATCH_L, ROWS_L, SIDE_L, C), 1.0, 6.0, ((0, 4), (1, 8)))
    cot_small = gaussian(arg_keys[3], (BATCH_S, ROWS_S, SIDE_S, C), 1.0, 6.0, ((0, 4), (1, 8)))
    cot_medium = gaussian(arg_keys[4], (BATCH_M, ROWS_M, SIDE_M, C), 1.0, 6.0, ((0, 4), (1, 8)))
    cot_large = gaussian(arg_keys[5], (BATCH_L, ROWS_L, SIDE_L, C), 1.0, 6.0, ((0, 4), (1, 8)))
    band_rows = draw_band_rows(jax.random.fold_in(arg_keys[12], 71), 0)
    params = draw_params(jax.random.fold_in(arg_keys[12], 71), 0)
    first_moment = gaussian(arg_keys[8], (PROWS, C), 100.0, 640.0, ((0, 32),), jnp.float32)
    second_moment = jnp.clip(jnp.exp(math.log(100000.0) - 4.6051702 * jax.random.uniform(arg_keys[9], (PROWS, C), jnp.float32) ** level_of(arg_keys[9], (PROWS, C), ((0, 32),), -0.2, 0.2)), 1000.0, 100000.0)
    step = jax.random.randint(arg_keys[10], (1,), 1, 10).astype(jnp.int32)
    rate = jnp.clip(jnp.exp(jax.random.uniform(arg_keys[11], (1,), jnp.float32, math.log(0.001), math.log(0.01))), 0.001, 0.01)
    return {"x_small": x_small, "x_medium": x_medium, "x_large": x_large, "cot_small": cot_small, "cot_medium": cot_medium, "cot_large": cot_large, "band_rows": band_rows, "params": params, "first_moment": first_moment, "second_moment": second_moment, "step": step, "rate": rate}


EPSILON = 1e-05
ADAM_EPSILON = 1e-08
HIGHEST_PRECISION = lax.Precision.HIGHEST

@jax.custom_vjp
def lowered_input(v):
    return lax.optimization_barrier(v.astype(jnp.bfloat16)).astype(jnp.float32)

@jax.custom_vjp
def lowered_gradient(v):
    return v

def low_keep(v):
    return (lowered_input(v), None)

def low_pass(kept, grad):
    return (grad,)

def back_keep(v):
    return (v, None)

def back_low(kept, grad):
    return (lowered_input(grad),)
lowered_input.defvjp(low_keep, low_pass)
lowered_gradient.defvjp(back_keep, back_low)

def band_layout(lengths, slots):
    starts = (jnp.cumsum(lengths) - lengths).astype(jnp.int32)
    slot_rows = jnp.arange(lengths.shape[0] * slots, dtype=jnp.int32)
    which_band = (slot_rows // slots).astype(jnp.int32)
    within = (slot_rows - which_band * slots).astype(jnp.int32)
    in_image = within < lengths[which_band]
    return ((starts[which_band] + within).astype(jnp.int32), in_image)

def to_image(slotted, lengths, slots, side):
    starts = (jnp.cumsum(lengths) - lengths).astype(jnp.int32)
    height = jnp.arange(side, dtype=jnp.int32)
    which_band = (lax.optimization_barrier(jnp.sum((starts[None, :] <= height[:, None]).astype(jnp.int32), axis=1)) - 1).astype(jnp.int32)
    source = (which_band * slots + height - starts[which_band]).astype(jnp.int32)
    return jnp.take(slotted, source, axis=1)

def to_slots(picture, lengths, slots):
    source, in_image = band_layout(lengths, slots)
    picked = jnp.take(picture, jnp.clip(source, 0, picture.shape[1] - 1).astype(jnp.int32), axis=1)
    return jnp.where(in_image[None, :, None, None], picked, jnp.zeros_like(picked))

def swish(value):
    return value * jax.nn.sigmoid(value)

def group_norm(feature, gain_row, shift_row):
    num_img, height, num_cols, channel_count = feature.shape
    grouped = feature.reshape(num_img, height * num_cols, GROUPS, channel_count // GROUPS)
    center = lax.optimization_barrier(jnp.mean(grouped, axis=(1, 3), keepdims=True))
    spread = lax.optimization_barrier(jnp.mean((grouped - center) ** 2, axis=(1, 3), keepdims=True))
    normed = ((grouped - center) * lax.rsqrt(spread + EPSILON)).reshape(feature.shape)
    return normed * gain_row + shift_row

def convolve(feature, kernel):
    height, num_cols = (feature.shape[1], feature.shape[2])
    padded = jnp.pad(feature, ((0, 0), (1, 1), (1, 1), (0, 0)))
    summed = jnp.zeros(feature.shape[:3] + (kernel.shape[2],), jnp.float32)
    for offset in range(9):
        row_shift, col_shift = (offset // 3, offset % 3)
        window = padded[:, row_shift:row_shift + height, col_shift:col_shift + num_cols]
        summed = summed + jnp.einsum('bhwc,cd->bhwd', window, kernel[offset], precision=HIGHEST_PRECISION)
    return summed

def attention(normed, project, small_band_rows):
    query_w, key_w, value_w, output_weight = project
    num_img, height, num_cols, channel_count = normed.shape
    flat_rows = normed.reshape(num_img, height * num_cols, channel_count)
    query_block = lowered_input(lowered_gradient(jnp.einsum('bnc,cd->bnd', flat_rows, query_w, precision=HIGHEST_PRECISION) + small_band_rows[8]))
    key_row_block = lowered_input(lowered_gradient(jnp.einsum('bnc,cd->bnd', flat_rows, key_w, precision=HIGHEST_PRECISION)))
    value_row_block = lowered_input(lowered_gradient(jnp.einsum('bnc,cd->bnd', flat_rows, value_w, precision=HIGHEST_PRECISION) + small_band_rows[9]))
    attention_scores = lowered_gradient(jnp.einsum('zrn,zgn->zrg', query_block, key_row_block, precision=HIGHEST_PRECISION) * channel_count ** (-0.5))
    top = lax.optimization_barrier(jnp.max(attention_scores, axis=-1, keepdims=True))
    expo = jnp.exp(attention_scores - top)
    attention_probabilities = expo / lax.optimization_barrier(jnp.sum(expo, axis=-1, keepdims=True))
    attended_values = lowered_input(lowered_gradient(jnp.einsum('adv,avt->adt', lowered_input(attention_probabilities), value_row_block, precision=HIGHEST_PRECISION)))
    projected_output = jnp.einsum('utm,ml->utl', attended_values, output_weight, precision=HIGHEST_PRECISION) + small_band_rows[10]
    return projected_output.reshape(normed.shape)

def unpack(flat_params):
    channel_count = flat_params.shape[1]
    conv_one = flat_params[:9 * channel_count].reshape(9, channel_count, channel_count)
    conv_two = flat_params[9 * channel_count:18 * channel_count].reshape(9, channel_count, channel_count)
    project = [flat_params[(18 + offset) * channel_count:(19 + offset) * channel_count] for offset in range(4)]
    small_band_rows = flat_params[22 * channel_count:22 * channel_count + 11]
    return (conv_one, conv_two, project, small_band_rows)

def forward(flat_params, pictures):
    conv_one, conv_two, project, small_band_rows = unpack(lowered_input(flat_params))
    results = []
    for picture in pictures:
        activated = swish(group_norm(picture, small_band_rows[0], small_band_rows[1]))
        branch = lowered_gradient(convolve(lowered_input(activated), conv_one) + small_band_rows[2])
        activated = swish(group_norm(branch, small_band_rows[3], small_band_rows[4]))
        branch = lowered_gradient(convolve(lowered_input(activated), conv_two) + small_band_rows[5])
        middle = picture + branch
        normed = lowered_input(group_norm(middle, small_band_rows[6], small_band_rows[7]))
        results.append(middle + attention(normed, project, small_band_rows))
    return tuple(results)

def reference(x_small, x_medium, x_large, cot_small, cot_medium, cot_large, band_rows, params, first_moment, second_moment, step, rate):
    slot_counts = (CAP_S, CAP_M, CAP_L)
    sides = (SIDE_S, SIDE_M, SIDE_L)
    raw_inputs = (x_small, x_medium, x_large)
    raw_cots = (cot_small, cot_medium, cot_large)
    pictures = tuple((to_image(raw_inputs[member].astype(jnp.float32), band_rows[member], slot_counts[member], sides[member]) for member in range(3)))
    cotangents = tuple((to_image(raw_cots[member].astype(jnp.float32), band_rows[member], slot_counts[member], sides[member]) for member in range(3)))
    outputs, pullback = jax.vjp(forward, params, pictures)
    grads, picture_grads = pullback(cotangents)
    step_count = step[0].astype(jnp.float32)
    moment_one = 0.5 * first_moment + 0.5 * grads
    moment_two = 0.9 * second_moment + 0.1 * grads * grads
    weight_update = rate[0] * (moment_one / (1.0 - jnp.power(0.5, step_count))) / (jnp.sqrt(moment_two / (1.0 - jnp.power(0.9, step_count))) + ADAM_EPSILON)
    updated = params - weight_update
    again = forward(updated, pictures)
    first_out = [to_slots(outputs[member], band_rows[member], slot_counts[member]).astype(jnp.bfloat16) for member in range(3)]
    second_out = [to_slots(again[member], band_rows[member], slot_counts[member]).astype(jnp.bfloat16) for member in range(3)]
    input_grads = [to_slots(picture_grads[member], band_rows[member], slot_counts[member]).astype(jnp.bfloat16) for member in range(3)]
    return (first_out[0], first_out[1], first_out[2], second_out[0], second_out[1], second_out[2], input_grads[0], input_grads[1], input_grads[2], weight_update, moment_one, moment_two)
```

```python
import functools

import jax
import jax.numpy as jnp
import numpy as np
from jax import lax
from jax.experimental import pallas as pl
from jax.experimental.pallas import tpu as pltpu
from jax.sharding import PartitionSpec as P

GROUPS = 32
EPSILON = 1e-05
ADAM_EPSILON = 1e-08
C = 512
AXES = ("band", "img")
VMEM_BYTES = 58 * 1024 * 1024
F32, BF16 = jnp.float32, jnp.bfloat16

PIX = 1024
SEG_LINES = ((0, 24), (24, 32))
BUF_LINES = 36


class Plan:
    def __init__(self, shapes, n_band):
        (self.n_s, self.cap_s, self.side_s, _), (self.n_m, self.cap_m, self.side_m, _), (
            self.n_l,
            self.cap_l,
            self.side_l,
            _,
        ) = shapes
        assert (self.side_s, self.side_m, self.side_l) == (16, 24, 32)
        self.n_band = n_band
        self.n_chip = n_band // 2
        self.r_s, self.r_m, self.r_l = (
            self.cap_s * self.side_s,
            self.cap_m * self.side_m,
            self.cap_l * self.side_l,
        )
        holders = [dict() for _ in range(n_band)]
        for i in range(self.n_l):
            holders[2 * i]["l"] = i
        free = [b for b in range(n_band) if "l" not in holders[b]]
        for i in range(self.n_m):
            holders[free[i]]["m"] = i
        spots = [b for b in free if b >= 2 * self.n_l]
        for i in range(self.n_s):
            holders[spots[i]]["s"] = i
        self.holders = holders
        self.sizes = [
            (self.r_l if "l" in h else 0)
            + (self.r_m if "m" in h else 0)
            + (self.r_s if "s" in h else 0)
            for h in holders
        ]
        self.block = max(self.sizes[2 * j] + self.sizes[2 * j + 1] for j in range(self.n_chip))
        self.piece = max(self.sizes)
        self.offs = [0 if b % 2 == 0 else self.piece - self.sizes[b] for b in range(n_band)]
        self.is_l = np.array([int("l" in h) for h in holders], np.int32)
        self.has_m = np.array([int("m" in h) for h in holders], np.int32)
        self.has_s = np.array([int("s" in h) for h in holders], np.int32)
        self.off = np.array(self.offs, np.int32)


def pick(table, index):
    return lax.dynamic_index_in_dim(jnp.asarray(table), index, 0, keepdims=False)


def make_tables(plan, band_rows, position):
    nz = plan.n_chip
    z, core = position // 2, position % 2
    is_l, has_m, has_s, off = (pick(t, position) for t in (plan.is_l, plan.has_m, plan.has_s, plan.off))
    starts = jnp.cumsum(band_rows, axis=1) - band_rows
    zero_in = plan.n_band * plan.piece // 8

    def band_of(member, rows):
        return jnp.sum((starts[member][None, :] <= rows[:, None]).astype(jnp.int32), axis=1) - 1

    def place(member, rows):
        band = band_of(member, rows)
        onehot = band[:, None] == jnp.arange(plan.n_band)[None, :]
        start = jnp.sum(jnp.where(onehot, starts[member][None, :], 0), axis=1)
        k = (z - band // 2) % nz
        pos = jnp.where(band % 2 == core, k, nz + k)
        return pos * plan.piece + off, rows - start

    q = np.arange(128)
    base, r = place(2, jnp.asarray(q // 4, jnp.int32))
    src_l = (base + r * 32) // 8 + jnp.asarray(q % 4, jnp.int32)
    base, r = place(1, jnp.asarray(np.minimum(q // 4, 23), jnp.int32))
    src_m = (base + r * 24) // 8 + jnp.asarray(q % 4, jnp.int32)
    ok_m = jnp.asarray((q < 96) & (q % 4 < 3)) & (has_m == 1)
    line = np.clip((q - 96) // 4, 0, 7)
    base, r = place(0, jnp.asarray(line + 8 * (q % 4 // 2), jnp.int32))
    src_s = (base + has_m * plan.r_m + r * 16) // 8 + jnp.asarray(q % 2, jnp.int32)
    ok_s = jnp.asarray(q >= 96) & (has_s == 1)
    gather = jnp.where(
        is_l == 1, src_l, jnp.where(ok_m, src_m, jnp.where(ok_s, src_s, zero_in))
    ).astype(jnp.int32)

    per = plan.piece // 8
    p, t = np.divmod(np.arange(plan.n_band * per), per)
    k = jnp.asarray(p % nz, jnp.int32)
    c_src = jnp.where(jnp.asarray(p < nz), core, 1 - core)
    band = 2 * ((z - k) % nz) + c_src
    onehot = band[:, None] == jnp.arange(plan.n_band)[None, :]

    def of_band(row):
        return jnp.sum(jnp.where(onehot, row[None, :], 0), axis=1)

    within = jnp.asarray(t * 8, jnp.int32) - off
    wl = jnp.maximum(within, 0)
    r = wl // 32
    ok_l = (within >= 0) & (r < of_band(band_rows[2]))
    out_l = (of_band(starts[2]) + r) * 4 + wl % 32 // 8
    r = wl // 24
    in_m = (has_m == 1) & (wl < plan.r_m)
    ok_m = (within >= 0) & in_m & (r < of_band(band_rows[1]))
    out_m = (of_band(starts[1]) + r) * 4 + wl % 24 // 8
    ws = jnp.maximum(wl - has_m * plan.r_m, 0)
    r = ws // 16
    h = of_band(starts[0]) + r
    ok_s = (within >= 0) & (has_s == 1) & ~in_m & (r < of_band(band_rows[0]))
    out_s = 96 + (h % 8) * 4 + (h // 8) * 2 + ws % 16 // 8
    scatter = jnp.where(
        is_l == 1,
        jnp.where(ok_l, out_l, 128),
        jnp.where(ok_m, out_m, jnp.where(ok_s, out_s, 128)),
    ).astype(jnp.int32)
    flags = jnp.stack(
        [
            is_l,
            jnp.where(is_l == 1, 32, 24 * has_m),
            jnp.where(is_l == 1, 32, 32 * has_s),
            jnp.where(is_l == 1, 0, 16),
        ]
    ).astype(jnp.int32)
    return gather, scatter, flags


class Scalars:
    def __init__(self, flags):
        self.is_l = flags[0]
        self.lims = (flags[1], flags[2])
        self.split = flags[3]
        self.l_f = flags[0].astype(F32)
        large = flags[0] == 1
        self.inv = (
            jnp.where(large, 1.0 / (1024 * 16), 1.0 / (576 * 16)).astype(F32),
            jnp.where(large, 1.0 / (1024 * 16), 1.0 / (256 * 16)).astype(F32),
        )


def dot(a, b):
    return jnp.dot(a, b, preferred_element_type=F32)


def dot_nt(a, b):
    return lax.dot_general(a, b, (((1,), (1,)), ((), ())), preferred_element_type=F32)


def dot_tn(a, b):
    return lax.dot_general(a, b, (((0,), (0,)), ((), ())), preferred_element_type=F32)


def line_rows(line):
    return pl.ds(pl.multiple_of(line * 32, 32), 32)


def line_loop(body, carries, unroll=2):
    results = []
    for seg, (low, high) in enumerate(SEG_LINES):
        results.append(
            lax.fori_loop(
                low, high, lambda line, carry, seg=seg: body(seg, line, carry), carries[seg], unroll=unroll
            )
        )
    return results


def fold(value):
    return value.reshape(4, 8, C).sum(axis=0)


def columns():
    return lax.broadcasted_iota(jnp.int32, (32, C), 0)


def fill_group_matrix(gm_ref):
    row = lax.broadcasted_iota(jnp.int32, (C, C), 0) // (C // GROUPS)
    col = lax.broadcasted_iota(jnp.int32, (C, C), 1) // (C // GROUPS)
    gm_ref[...] = (row == col).astype(F32).astype(BF16)


def group_totals(gm_ref, scal, per_seg):
    stacked = jnp.concatenate(list(per_seg) + [jnp.zeros((8 - len(per_seg), C), F32)], axis=0)
    hi = stacked.astype(BF16)
    rest = stacked - hi.astype(F32)
    mid = rest.astype(BF16)
    low = (rest - mid.astype(F32)).astype(BF16)
    both = dot(jnp.concatenate([hi, mid, low, jnp.zeros((8, C), BF16)], axis=0), gm_ref[...])
    total = both[0:8] + both[8:16] + both[16:24]
    out = []
    for i in range(0, len(per_seg), 2):
        first, second = total[i : i + 1], total[i + 1 : i + 2]
        out.append((first + scal.l_f * second, second + scal.l_f * first))
    return out


def norm_stats(read, gm_ref, scal):
    zero = jnp.zeros((8, C), F32)
    sums = line_loop(lambda seg, line, acc: acc + fold(read(line)), (zero, zero))
    sums = [s.sum(axis=0, keepdims=True) for s in sums]
    (totals,) = group_totals(gm_ref, scal, sums)
    means = [totals[seg] * scal.inv[seg] for seg in range(2)]
    col = columns()

    def squares(seg, line, acc):
        dev = jnp.where(col < scal.lims[seg], read(line) - means[seg], 0.0)
        return acc + fold(dev * dev)

    sums = line_loop(squares, (zero, zero))
    sums = [s.sum(axis=0, keepdims=True) for s in sums]
    (totals,) = group_totals(gm_ref, scal, sums)
    rstds = [lax.rsqrt(totals[seg] * scal.inv[seg] + EPSILON) for seg in range(2)]
    return means, rstds


def store_shifted(buf_ref, scal, seg, line, value16):
    col = columns()
    value = value16.astype(F32)
    keep_left, keep_right = col != 0, col != 31
    if seg == 1:
        keep_left &= col != scal.split
        keep_right &= col != scal.split - 1
    left = jnp.where(keep_left, pltpu.roll(value, 1, 0), 0.0).astype(BF16)
    right = jnp.where(keep_right, pltpu.roll(value, 31, 0), 0.0).astype(BF16)
    at = line_rows(line + (1 if seg == 0 else 3))
    buf_ref[at, 0:C] = left
    buf_ref[at, C : 2 * C] = value16
    buf_ref[at, 2 * C : 3 * C] = right


def fill_halos(buf_ref, scal):
    zero = jnp.zeros((32, 3 * C), BF16)
    buf_ref[0:32, :] = zero
    buf_ref[25 * 32 : 26 * 32, :] = zero
    buf_ref[26 * 32 : 27 * 32, :] = zero
    buf_ref[35 * 32 : 36 * 32, :] = zero

    @pl.when(scal.is_l == 1)
    def _():
        buf_ref[25 * 32 : 26 * 32, :] = buf_ref[27 * 32 : 28 * 32, :]
        buf_ref[26 * 32 : 27 * 32, :] = buf_ref[24 * 32 : 25 * 32, :]

    @pl.when(scal.is_l == 0)
    def _():
        buf_ref[26 * 32 + 16 : 27 * 32, :] = buf_ref[34 * 32 : 34 * 32 + 16, :]
        buf_ref[35 * 32 : 35 * 32 + 16, :] = buf_ref[27 * 32 + 16 : 28 * 32, :]


def tile_rows(tile, shift):
    line = (8 * tile if tile < 3 else 26) + shift
    return slice(line * 32, line * 32 + 256)


def conv_tiles(buf_ref, w_ref, write):
    for tile in range(4):
        acc = None
        for shift in range(3):
            term = dot(buf_ref[tile_rows(tile, shift), :], w_ref[shift * 3 * C : (shift + 1) * 3 * C, :])
            acc = term if acc is None else acc + term
        write(tile, acc)


def gather_pieces(table_ref, src_ref, dst_ref, count):
    def step(i, carry):
        at = pl.multiple_of(table_ref[i] * 8, 8)
        dst_ref[pl.ds(pl.multiple_of(i * 8, 8), 8), :] = src_ref[pl.ds(at, 8), :]
        return carry

    lax.fori_loop(0, count, step, 0, unroll=4)


def slots_to_image(table_ref, own_ref, got_ref, slots_ref, image_ref):
    half = own_ref.shape[0]
    slots_ref[0:half, :] = own_ref[...].astype(F32)
    slots_ref[half : 2 * half, :] = got_ref[...].astype(F32)
    slots_ref[2 * half : 2 * half + 8, :] = jnp.zeros((8, C), F32)
    gather_pieces(table_ref, slots_ref, image_ref, 128)


def image_to_slots(table_ref, image_ref, slots_ref, own_ref, oth_ref):
    half = own_ref.shape[0]
    gather_pieces(table_ref, image_ref, slots_ref, 2 * half // 8)
    own_ref[...] = slots_ref[0:half, :].astype(BF16)
    oth_ref[...] = slots_ref[half : 2 * half, :].astype(BF16)


def swish_slope(value):
    sigma = jax.nn.sigmoid(value)
    return sigma * (1.0 + value * (1.0 - sigma))


def features_kernel(
    first,
    gather,
    flags,
    own,
    got,
    small,
    weights,
    *refs,
):
    if first:
        x_out, a1_out, h1_out, a2_out, y_out, z_out, q_out, k_out, v_out, stats_out = refs[:10]
        scratch = refs[10:]
    else:
        y_out, q_out, k_out, v_out = refs[:4]
        scratch = refs[4:]
    slots, x_ref, h_ref, z_ref, buf, w1, w2, wp, gm, sems = scratch
    copies = [
        pltpu.make_async_copy(weights.at[pl.ds(0, 9 * C)], w1, sems.at[0]),
        pltpu.make_async_copy(weights.at[pl.ds(9 * C, 9 * C)], w2, sems.at[1]),
        pltpu.make_async_copy(weights.at[pl.ds(18 * C, 3 * C)], wp, sems.at[2]),
    ]
    for copy in copies:
        copy.start()
    scal = Scalars(flags)
    fill_group_matrix(gm)
    slots_to_image(gather, own, got, slots, x_ref)
    col = columns()

    def row(i):
        return small[i : i + 1, :]

    def activate(read, means, rstds, gain, shift, keep):
        def body(seg, line, carry):
            normed = (read(line) - means[seg]) * rstds[seg] * gain + shift
            act = jnp.where(col < scal.lims[seg], normed * jax.nn.sigmoid(normed), 0.0).astype(BF16)
            if keep is not None:
                keep[line_rows(line), :] = act
            store_shifted(buf, scal, seg, line, act)
            return carry

        line_loop(body, (0, 0))
        fill_halos(buf, scal)

    def read_x(line):
        return x_ref[line_rows(line), :]

    means1, rstds1 = norm_stats(read_x, gm, scal)
    activate(read_x, means1, rstds1, row(0), row(1), a1_out if first else None)
    if first:

        def keep_x(seg, line, carry):
            x_out[line_rows(line), :] = read_x(line).astype(BF16)
            return carry

        line_loop(keep_x, (0, 0))

    copies[0].wait()

    def write_h(tile, acc):
        h_ref[tile * 256 : (tile + 1) * 256, :] = acc

    conv_tiles(buf, w1, write_h)

    def finish_h(seg, line, carry):
        value = jnp.where(col < scal.lims[seg], h_ref[line_rows(line), :] + row(2), 0.0)
        h_ref[line_rows(line), :] = value
        if first:
            h1_out[line_rows(line), :] = value
        return carry

    line_loop(finish_h, (0, 0))

    def read_h(line):
        return h_ref[line_rows(line), :]

    means2, rstds2 = norm_stats(read_h, gm, scal)
    activate(read_h, means2, rstds2, row(3), row(4), a2_out if first else None)
    copies[1].wait()
    conv_tiles(buf, w2, write_h)

    def finish_y(seg, line, carry):
        value = jnp.where(
            col < scal.lims[seg], read_x(line) + (h_ref[line_rows(line), :] + row(5)), 0.0
        )
        y_out[line_rows(line), :] = value
        return carry

    line_loop(finish_y, (0, 0))

    def read_y(line):
        return y_out[line_rows(line), :]

    means3, rstds3 = norm_stats(read_y, gm, scal)

    def third(seg, line, carry):
        normed = (read_y(line) - means3[seg]) * rstds3[seg] * row(6) + row(7)
        value = jnp.where(col < scal.lims[seg], normed, 0.0).astype(BF16)
        z_ref[line_rows(line), :] = value
        if first:
            z_out[line_rows(line), :] = value
        return carry

    line_loop(third, (0, 0))
    copies[2].wait()
    for tile in range(4):
        at = slice(tile * 256, (tile + 1) * 256)
        rows = z_ref[at, :]
        q_out[at, :] = (dot(rows, wp[0:C, :]) + row(8)).astype(BF16)
        k_out[at, :] = dot(rows, wp[C : 2 * C, :]).astype(BF16)
        v_out[at, :] = (dot(rows, wp[2 * C : 3 * C, :]) + row(9)).astype(BF16)
    if first:
        for i, pair in enumerate((means1, rstds1, means2, rstds2, means3, rstds3)):
            stats_out[2 * i : 2 * i + 1, :] = pair[0]
            stats_out[2 * i + 1 : 2 * i + 2, :] = pair[1]


def key_bias(scal):
    key = lax.broadcasted_iota(jnp.int32, (1, PIX), 1)
    column = key % 32
    in0 = key < 768
    ok0 = in0 & (column < scal.lims[0])
    ok1 = (~in0) & (column < scal.lims[1])
    large = scal.is_l == 1
    row0 = jnp.where(ok0 | (ok1 & large), 0.0, -1e30).astype(F32)
    row1 = jnp.where(ok1 | (ok0 & large), 0.0, -1e30).astype(F32)
    return row0, row1


def probabilities(q, k_ref, bias):
    scores = dot_nt(q, k_ref[...]) * (C**-0.5) + bias
    top = jnp.max(scores, axis=1, keepdims=True)
    expo = jnp.exp(scores - top)
    return expo * (1.0 / jnp.sum(expo, axis=1, keepdims=True))


def attend_kernel(scatter, flags, q, k, v, y, small, weights, own_out, oth_out, image, slots, wo, sems):
    copy = pltpu.make_async_copy(weights.at[pl.ds(21 * C, C)], wo, sems.at[0])
    copy.start()
    scal = Scalars(flags)
    biases = key_bias(scal)
    copy.wait()
    for tile in range(4):
        at = slice(tile * 256, (tile + 1) * 256)
        prob = probabilities(q[at, :], k, biases[tile // 3]).astype(BF16)
        mixed = dot(prob, v[...]).astype(BF16)
        image[at, :] = y[at, :] + (dot(mixed, wo[...]) + small[10:11, :])
    image[PIX : PIX + 8, :] = jnp.zeros((8, C), F32)
    image_to_slots(scatter, image, slots, own_out, oth_out)


def attend_both_kernel(
    gather,
    scatter,
    flags,
    q,
    k,
    v,
    y,
    z,
    cot_own,
    cot_got,
    stats,
    small,
    weights,
    own_out,
    oth_out,
    dy_out,
    dy16_out,
    grads_out,
    sums_out,
    image,
    slots,
    g_ref,
    o_ref,
    d_ref,
    dk_acc,
    dv_acc,
    wp,
    gm,
    sems,
):
    copy = pltpu.make_async_copy(weights.at[pl.ds(18 * C, 4 * C)], wp, sems.at[0])
    copy.start()
    scal = Scalars(flags)
    fill_group_matrix(gm)
    biases = key_bias(scal)
    slots_to_image(gather, cot_own, cot_got, slots, g_ref)
    copy.wait()
    scaling = C**-0.5
    for tile in range(4):
        at = slice(tile * 256, (tile + 1) * 256)
        q_t = q[at, :]
        prob = probabilities(q_t, k, biases[tile // 3])
        prob16 = prob.astype(BF16)
        mixed = dot(prob16, v[...]).astype(BF16)
        o_ref[at, :] = mixed
        image[at, :] = y[at, :] + (dot(mixed, wp[3 * C : 4 * C, :]) + small[10:11, :])
        d_mixed = dot_nt(g_ref[at, :].astype(BF16), wp[3 * C : 4 * C, :]).astype(BF16)
        d_prob = dot_nt(d_mixed, v[...])
        inner = jnp.sum(prob * d_prob, axis=1, keepdims=True)
        d_score = (prob * (d_prob - inner)).astype(BF16)
        d_ref[at, 0:C] = (scaling * dot(d_score, k[...])).astype(BF16)
        dk = dot_tn(d_score, q_t)
        dv = dot_tn(prob16, d_mixed)
        if tile == 0:
            dk_acc[...] = dk
            dv_acc[...] = dv
        else:
            dk_acc[...] += dk
            dv_acc[...] += dv
    d_ref[:, C : 2 * C] = (scaling * dk_acc[...]).astype(BF16)
    d_ref[:, 2 * C : 3 * C] = dv_acc[...].astype(BF16)
    image[PIX : PIX + 8, :] = jnp.zeros((8, C), F32)
    image_to_slots(scatter, image, slots, own_out, oth_out)
    for part in range(3):
        grads_out[part * C : (part + 1) * C, :] = dot_tn(
            z[...], d_ref[:, part * C : (part + 1) * C]
        ).astype(BF16)
    grads_out[3 * C : 4 * C, :] = dot_tn(o_ref[...], g_ref[...].astype(BF16)).astype(BF16)
    for tile in range(4):
        at = slice(tile * 256, (tile + 1) * 256)
        acc = dot_nt(d_ref[at, 0:C], wp[0:C, :])
        acc = acc + dot_nt(d_ref[at, C : 2 * C], wp[C : 2 * C, :])
        image[at, :] = acc + dot_nt(d_ref[at, 2 * C : 3 * C], wp[2 * C : 3 * C, :])
    col = columns()
    means = (stats[8:9, :], stats[9:10, :])
    rstds = (stats[10:11, :], stats[11:12, :])
    zero = jnp.zeros((8, C), F32)

    def sums(seg, line, acc):
        at = line_rows(line)
        d_norm = image[at, :]
        unit = (y[at, :] - means[seg]) * rstds[seg]
        d_all = d_ref[at, :].astype(F32)
        return (
            acc[0] + fold(d_norm),
            acc[1] + fold(d_norm * unit),
            acc[2] + fold(d_all[:, 0:C]),
            acc[3] + fold(d_all[:, 2 * C : 3 * C]),
            acc[4] + fold(g_ref[at, :]),
        )

    got = line_loop(sums, ((zero,) * 5, (zero,) * 5), unroll=1)
    got = [[part.sum(axis=0, keepdims=True) for part in seg] for seg in got]
    gain = small[6:7, :]
    ones, cross = group_totals(
        gm, scal, [got[0][0] * gain, got[1][0] * gain, got[0][1] * gain, got[1][1] * gain]
    )
    for i, part in enumerate((1, 0, 2, 3, 4)):
        sums_out[i : i + 1, :] = got[0][part] + got[1][part]
    sums_out[5:8, :] = jnp.zeros((3, C), F32)

    def back(seg, line, carry):
        at = line_rows(line)
        unit = (y[at, :] - means[seg]) * rstds[seg]
        d_in = rstds[seg] * (
            image[at, :] * gain - ones[seg] * scal.inv[seg] - unit * (cross[seg] * scal.inv[seg])
        )
        value = g_ref[at, :] + jnp.where(col < scal.lims[seg], d_in, 0.0)
        dy_out[at, :] = value
        dy16_out[at, :] = value.astype(BF16)
        return carry

    line_loop(back, (0, 0))


def fill_gradient_buffer(buf, scal, grad_ref):
    def body(seg, line, carry):
        store_shifted(buf, scal, seg, line, grad_ref[line_rows(line), :])
        return carry

    line_loop(body, (0, 0))
    fill_halos(buf, scal)


def weight_grad_kernel(flags, act, grad, w_out, sums_out, buf, act_t):
    scal = Scalars(flags)
    fill_gradient_buffer(buf, scal, grad)
    for tile in range(4):
        at = slice(tile * 256, (tile + 1) * 256)
        act_t[:, at] = act[at, :].T
    for shift in range(3):
        seg0 = slice(shift * 32, shift * 32 + 768)
        seg1 = slice((26 + shift) * 32, (26 + shift) * 32 + 256)
        for part in range(3):
            cols = slice(part * C, (part + 1) * C)
            value = dot(act_t[:, 0:768], buf[seg0, cols]) + dot(act_t[:, 768:1024], buf[seg1, cols])
            tap = 3 * (2 - shift) + (2 - part)
            w_out[tap * C : (tap + 1) * C, :] = value.astype(BF16)
    zero = jnp.zeros((8, C), F32)
    got = line_loop(
        lambda seg, line, acc: acc + fold(grad[line_rows(line), :].astype(F32)), (zero, zero)
    )
    sums_out[...] = jnp.zeros((8, C), F32)
    sums_out[0:1, :] = (got[0] + got[1]).sum(axis=0, keepdims=True)


def data_grad_kernel(last, conv, *refs):
    if last:
        scatter, flags, grad, feat, dy, stats, small, weights, own_out, oth_out, sums_out = refs[:11]
        dn, slots, buf, w, gm, sems = refs[11:]
    else:
        flags, grad, feat, stats, small, weights, grad_out, sums_out = refs[:8]
        dn, buf, w, gm, sems = refs[8:]
    copy = pltpu.make_async_copy(weights.at[pl.ds(conv * 9 * C, 9 * C)], w, sems.at[0])
    copy.start()
    scal = Scalars(flags)
    fill_group_matrix(gm)
    fill_gradient_buffer(buf, scal, grad)
    copy.wait()
    for tile in range(4):
        acc = None
        for shift in range(3):
            for part in range(3):
                tap = 3 * (2 - shift) + (2 - part)
                term = dot_nt(
                    buf[tile_rows(tile, shift), part * C : (part + 1) * C], w[tap * C : (tap + 1) * C, :]
                )
                acc = term if acc is None else acc + term
        dn[tile * 256 : (tile + 1) * 256, :] = acc
    base = 4 * conv
    means = (stats[base : base + 1, :], stats[base + 1 : base + 2, :])
    rstds = (stats[base + 2 : base + 3, :], stats[base + 3 : base + 4, :])
    gain, shift_row = small[3 * conv : 3 * conv + 1, :], small[3 * conv + 1 : 3 * conv + 2, :]
    col = columns()
    zero = jnp.zeros((8, C), F32)

    def sums(seg, line, acc):
        at = line_rows(line)
        unit = (feat[at, :].astype(F32) - means[seg]) * rstds[seg]
        value = dn[at, :] * swish_slope(unit * gain + shift_row)
        value = jnp.where(col < scal.lims[seg], value, 0.0)
        dn[at, :] = value
        return (acc[0] + fold(value), acc[1] + fold(value * unit))

    got = line_loop(sums, ((zero, zero), (zero, zero)))
    got = [[part.sum(axis=0, keepdims=True) for part in seg] for seg in got]
    ones, cross = group_totals(
        gm, scal, [got[0][0] * gain, got[1][0] * gain, got[0][1] * gain, got[1][1] * gain]
    )
    sums_out[...] = jnp.zeros((8, C), F32)
    sums_out[0:1, :] = got[0][1] + got[1][1]
    sums_out[1:2, :] = got[0][0] + got[1][0]

    def back(seg, line, carry):
        at = line_rows(line)
        unit = (feat[at, :].astype(F32) - means[seg]) * rstds[seg]
        value = rstds[seg] * (
            dn[at, :] * gain - ones[seg] * scal.inv[seg] - unit * (cross[seg] * scal.inv[seg])
        )
        value = jnp.where(col < scal.lims[seg], value, 0.0)
        if last:
            dn[at, :] = value + dy[at, :]
        else:
            grad_out[at, :] = value.astype(BF16)
        return carry

    line_loop(back, (0, 0))
    if last:
        dn[PIX : PIX + 8, :] = jnp.zeros((8, C), F32)
        image_to_slots(scatter, dn, slots, own_out, oth_out)


SMEM = pl.BlockSpec(memory_space=pltpu.SMEM)
VMEM = pl.BlockSpec(memory_space=pltpu.VMEM)
ANY = pl.BlockSpec(memory_space=pl.ANY)


def call(kernel, name, in_specs, outs, scratch, flops, args):
    moved = sum(int(np.prod(a.shape)) * a.dtype.itemsize for a in args)
    moved += sum(int(np.prod(s)) * jnp.dtype(d).itemsize for s, d in outs)
    return pl.pallas_call(
        kernel,
        name=name,
        out_shape=[jax.ShapeDtypeStruct(s, d) for s, d in outs],
        in_specs=in_specs,
        out_specs=[VMEM] * len(outs),
        scratch_shapes=scratch,
        compiler_params=pltpu.CompilerParams(vmem_limit_bytes=VMEM_BYTES),
        cost_estimate=pl.CostEstimate(flops=int(flops), bytes_accessed=moved, transcendentals=0),
    )(*args)


MAP, SLOT_PAD = (PIX, C), 8
CONV_FLOPS = 2 * PIX * 9 * C * C
PROJ_FLOPS = 2 * PIX * C * C
PAIR_FLOPS = 2 * PIX * PIX * C
BUF = pltpu.VMEM((BUF_LINES * 32, 3 * C), BF16)


def run_features(first, tables, slots_in, small, weights):
    gather, _, flags = tables
    rows = 2 * slots_in[0].shape[0] + SLOT_PAD
    outs = [(MAP, F32), (MAP, BF16), (MAP, BF16), (MAP, BF16)]
    if first:
        outs = [
            (MAP, BF16),
            (MAP, BF16),
            (MAP, F32),
            (MAP, BF16),
            (MAP, F32),
            (MAP, BF16),
            (MAP, BF16),
            (MAP, BF16),
            (MAP, BF16),
            ((16, C), F32),
        ]
    return call(
        functools.partial(features_kernel, first),
        "features_first" if first else "features_again",
        [SMEM, SMEM, VMEM, VMEM, VMEM, ANY],
        outs,
        [
            pltpu.VMEM((rows, C), F32),
            pltpu.VMEM(MAP, F32),
            pltpu.VMEM(MAP, F32),
            pltpu.VMEM(MAP, BF16),
            BUF,
            pltpu.VMEM((9 * C, C), BF16),
            pltpu.VMEM((9 * C, C), BF16),
            pltpu.VMEM((3 * C, C), BF16),
            pltpu.VMEM((C, C), BF16),
            pltpu.SemaphoreType.DMA((3,)),
        ],
        2 * CONV_FLOPS + 3 * PROJ_FLOPS,
        (gather, flags, slots_in[0], slots_in[1], small, weights),
    )


def run_attend(tables, q, k, v, y, small, weights, half):
    _, scatter, flags = tables
    return call(
        attend_kernel,
        "attend_again",
        [SMEM, SMEM, VMEM, VMEM, VMEM, VMEM, VMEM, ANY],
        [((half, C), BF16)] * 2,
        [
            pltpu.VMEM((PIX + 8, C), F32),
            pltpu.VMEM((2 * half, C), F32),
            pltpu.VMEM((C, C), BF16),
            pltpu.SemaphoreType.DMA((1,)),
        ],
        2 * PAIR_FLOPS + PROJ_FLOPS,
        (scatter, flags, q, k, v, y, small, weights),
    )


def run_attend_both(tables, q, k, v, y, z, cot, stats, small, weights):
    gather, scatter, flags = tables
    half = cot[0].shape[0]
    return call(
        attend_both_kernel,
        "attend_both",
        [SMEM, SMEM, SMEM] + [VMEM] * 9 + [ANY],
        [
            ((half, C), BF16),
            ((half, C), BF16),
            (MAP, F32),
            (MAP, BF16),
            ((4 * C, C), BF16),
            ((8, C), F32),
        ],
        [
            pltpu.VMEM((PIX + 8, C), F32),
            pltpu.VMEM((2 * half + SLOT_PAD, C), F32),
            pltpu.VMEM(MAP, F32),
            pltpu.VMEM(MAP, BF16),
            pltpu.VMEM((PIX, 3 * C), BF16),
            pltpu.VMEM(MAP, F32),
            pltpu.VMEM(MAP, F32),
            pltpu.VMEM((4 * C, C), BF16),
            pltpu.VMEM((C, C), BF16),
            pltpu.SemaphoreType.DMA((1,)),
        ],
        7 * PAIR_FLOPS + 9 * PROJ_FLOPS,
        (gather, scatter, flags, q, k, v, y, z, cot[0], cot[1], stats, small, weights),
    )


def run_weight_grad(tables, act, grad, name):
    return call(
        weight_grad_kernel,
        name,
        [SMEM, VMEM, VMEM],
        [((9 * C, C), BF16), ((8, C), F32)],
        [BUF, pltpu.VMEM((C, PIX), BF16)],
        CONV_FLOPS,
        (tables[2], act, grad),
    )


def run_data_grad(tables, conv, grad, feat, stats, small, weights, dy=None, half=None):
    last = dy is not None
    scratch = [BUF, pltpu.VMEM((9 * C, C), BF16), pltpu.VMEM((C, C), BF16), pltpu.SemaphoreType.DMA((1,))]
    if last:
        outs = [((half, C), BF16)] * 2
        scratch = [pltpu.VMEM((PIX + 8, C), F32), pltpu.VMEM((2 * half, C), F32)] + scratch
        args = (tables[1], tables[2], grad, feat, dy, stats, small, weights)
        specs = [SMEM, SMEM] + [VMEM] * 5 + [ANY]
    else:
        outs = [(MAP, BF16)]
        scratch = [pltpu.VMEM(MAP, F32)] + scratch
        args = (tables[2], grad, feat, stats, small, weights)
        specs = [SMEM] + [VMEM] * 4 + [ANY]
    return call(
        functools.partial(data_grad_kernel, last, conv),
        "data_grad_one" if conv == 0 else "data_grad_two",
        specs,
        outs + [((8, C), F32)],
        scratch,
        CONV_FLOPS,
        args,
    )


def z_shift(value, nz, k):
    return lax.ppermute(value, "band", [(2 * z + c, 2 * ((z + k) % nz) + c) for z in range(nz) for c in range(2)])


def core_swap(value, n_band):
    return lax.ppermute(value, "band", [(b, b ^ 1) for b in range(n_band)])


def to_holders(plan, position, arrays):
    z, core = position // 2, position % 2
    flat = [a.reshape(a.shape[0], -1, C) for a in arrays]
    blocks = []
    for chip in range(plan.n_chip):
        parts = []
        for c in range(2):
            h = plan.holders[2 * chip + c]
            mine = [flat[m][h[name]] for m, name in ((2, "l"), (1, "m"), (0, "s")) if name in h]
            if c == 1:
                used = plan.sizes[2 * chip] + plan.sizes[2 * chip + 1]
                if used < plan.block:
                    parts.append(jnp.zeros((plan.block - used, C), BF16))
            parts += mine
        blocks.append(jnp.concatenate(parts, axis=0))
    sent = jnp.stack(blocks)
    nz = plan.n_chip
    received = []
    for k in range(nz):
        block = lax.dynamic_index_in_dim(sent, (z + k) % nz, 0, keepdims=False)
        received.append(block if k == 0 else z_shift(block, nz, k))
    received = jnp.stack(received)
    slack = plan.block - plan.piece
    own = lax.dynamic_slice_in_dim(received, slack * core, plan.piece, 1)
    other = lax.dynamic_slice_in_dim(received, slack * (1 - core), plan.piece, 1)
    got = core_swap(other, plan.n_band)
    return own.reshape(-1, C), got.reshape(-1, C)


def from_holders(plan, position, own, other):
    z, core = position // 2, position % 2
    nz, slack = plan.n_chip, plan.block - plan.piece
    got = core_swap(other, plan.n_band).reshape(nz, plan.piece, C)
    own = own.reshape(nz, plan.piece, C)
    first, second = jnp.where(core == 0, own, got), jnp.where(core == 0, got, own)
    blocks = jnp.pad(first, ((0, 0), (0, slack), (0, 0))) + jnp.pad(second, ((0, 0), (slack, 0), (0, 0)))
    received = [blocks[0]] + [z_shift(blocks[k], nz, -k) for k in range(1, nz)]
    received = jnp.stack(received)
    images = [[None] * plan.n_s, [None] * plan.n_m, [None] * plan.n_l]
    for b, h in enumerate(plan.holders):
        chip = b // 2
        if not h:
            continue
        block = lax.dynamic_index_in_dim(received, (chip - z) % nz, 0, keepdims=False)
        at = plan.offs[b] + (slack if b % 2 else 0)
        for member, name, size in ((2, "l", plan.r_l), (1, "m", plan.r_m), (0, "s", plan.r_s)):
            if name in h:
                images[member][h[name]] = block[at : at + size]
                at += size
    sides = (plan.side_s, plan.side_m, plan.side_l)
    return [
        jnp.stack(images[m]).reshape(len(images[m]), -1, sides[m], C) for m in range(3)
    ]


def fetch_weights(shard):
    full = lax.all_gather(shard.astype(BF16), AXES, axis=0, tiled=True)
    small = full[22 * C : 22 * C + 16].astype(F32)
    return full, small


def swap_axis(value, n_band, which):
    if which == "core":
        return core_swap(value, n_band)
    bit = 1 if which == "x" else 2
    return lax.ppermute(value, "img", [(i, i ^ bit) for i in range(4)])


def reduce_pair(position, img, top, small):
    core, y, x = position % 2, img // 2, img % 2
    rows = top.shape[3]
    kept = lax.dynamic_index_in_dim(top, core, 1, keepdims=False)
    sent = lax.dynamic_index_in_dim(top, 1 - core, 1, keepdims=False)
    got = core_swap(sent, lax.axis_size("band"))
    both = (kept.astype(F32) + got.astype(F32)).astype(BF16).reshape(2, 2, 2, rows, C)

    def halve(value, axis, mine, which):
        keep = lax.dynamic_index_in_dim(value, mine, axis, keepdims=False)
        send = lax.dynamic_index_in_dim(value, 1 - mine, axis, keepdims=False)
        arrived = swap_axis(send, None, which)
        return (keep.astype(F32) + arrived.astype(F32)).astype(BF16)

    a = halve(both[0], 1, x, "x")
    b = halve(both[1], 0, y, "y")
    a = halve(a, 0, y, "y")
    b = halve(b, 0, x, "x")
    return a, b


def reduce_grads(position, img, high, low):
    z = position // 2
    planes = list(reduce_pair(position, img, low, None)) + list(reduce_pair(position, img, high, None))
    stacked = jnp.stack(planes)
    total = lax.dynamic_index_in_dim(stacked, z, 0, keepdims=False).astype(F32)
    for k in range(1, 4):
        sent = lax.dynamic_index_in_dim(stacked, (z + k) % 4, 0, keepdims=False)
        total = total + z_shift(sent, 4, k).astype(F32)
    return total


def shard_of_grads(position, img, w1, w2, proj, small_rows, rows):
    n_band, n_img = lax.axis_size("band"), lax.axis_size("img")
    count = n_band * n_img
    small_rows = jnp.pad(small_rows, ((0, rows * count - 22 * C - small_rows.shape[0]), (0, 0)))
    if n_band != 8 or n_img != 4:
        full = jnp.concatenate([w1, w2, proj, small_rows.astype(BF16)], axis=0)
        return lax.psum_scatter(full, AXES, scatter_dimension=0, tiled=True).astype(F32)
    block = 22 * C // count
    high = jnp.concatenate([w2[2 * C :], proj], axis=0).reshape(2, 2, 4, block, C)
    low = jnp.concatenate([w1, w2[: 2 * C]], axis=0).reshape(2, 2, 4, block, C)
    mine = reduce_grads(position, img, high, low)
    small_sum = lax.psum(small_rows, AXES)
    owner = position * n_img + img
    after = lax.ppermute(mine[:count], AXES, [(o, o - 1) for o in range(1, count)])
    after = jnp.where(owner == count - 1, small_sum, after)
    return lax.dynamic_slice_in_dim(jnp.concatenate([mine, after], axis=0), owner, rows, 0)


def body(
    x_small,
    x_medium,
    x_large,
    cot_small,
    cot_medium,
    cot_large,
    band_rows,
    params,
    first_moment,
    second_moment,
    step,
    rate,
):
    n_band = lax.axis_size("band")
    position, img = lax.axis_index("band"), lax.axis_index("img")
    plan = Plan([x_small.shape, x_medium.shape, x_large.shape], n_band)
    tables = make_tables(plan, band_rows, position)
    half = n_band // 2 * plan.piece

    x_slots = to_holders(plan, position, (x_small, x_medium, x_large))
    weights, small = fetch_weights(params)
    cot_slots = to_holders(plan, position, (cot_small, cot_medium, cot_large))
    x_img, a1, h1, a2, y, z, q, k, v, stats = run_features(True, tables, x_slots, small, weights)
    out_own, out_oth, dy, dy16, g_proj, sums3 = run_attend_both(
        tables, q, k, v, y, z, cot_slots, stats, small, weights
    )
    first_out = from_holders(plan, position, out_own, out_oth)
    g_w2, sums_b2 = run_weight_grad(tables, a2, dy16, "weight_grad_two")
    dh1, sums_n2 = run_data_grad(tables, 1, dy16, h1, stats, small, weights)
    g_w1, sums_b1 = run_weight_grad(tables, a1, dh1, "weight_grad_one")
    dx_own, dx_oth, sums_n1 = run_data_grad(
        tables, 0, dh1, x_img, stats, small, weights, dy=dy, half=half
    )
    input_grads = from_holders(plan, position, dx_own, dx_oth)
    small_rows = jnp.concatenate(
        [sums_n1[0:2], sums_b1[0:1], sums_n2[0:2], sums_b2[0:1], sums3[0:5]], axis=0
    )
    grad = shard_of_grads(position, img, g_w1, g_w2, g_proj, small_rows, params.shape[0])

    step_count = step[0].astype(F32)
    new_first = 0.5 * first_moment + 0.5 * grad
    new_second = 0.9 * second_moment + 0.1 * grad * grad
    weight_update = (
        rate[0]
        * (new_first / (1.0 - jnp.power(0.5, step_count)))
        / (jnp.sqrt(new_second / (1.0 - jnp.power(0.9, step_count))) + ADAM_EPSILON)
    )
    new_weights, new_small = fetch_weights(params - weight_update)
    y2, q2, k2, v2 = run_features(False, tables, x_slots, new_small, new_weights)
    again_own, again_oth = run_attend(tables, q2, k2, v2, y2, new_small, new_weights, half)
    second_out = from_holders(plan, position, again_own, again_oth)
    return (*first_out, *second_out, *input_grads, weight_update, new_first, new_second)


def solution(mesh):
    image = P("img", "band", None, None)
    shard = P(("band", "img"), None)
    return jax.shard_map(
        body,
        mesh=mesh,
        in_specs=(image,) * 6 + (P(),) + (shard,) * 3 + (P(), P()),
        out_specs=(image,) * 9 + (shard,) * 3,
        check_vma=False,
    )
```

```python
import functools

import jax
import jax.numpy as jnp
import numpy as np
from jax import lax
from jax.experimental import pallas as pl
from jax.experimental.pallas import tpu as pltpu
from jax.sharding import PartitionSpec as P

GROUPS = 32
EPSILON = 1e-05
ADAM_EPSILON = 1e-08
C = 512
AXES = ("band", "img")
VMEM_BYTES = 58 * 1024 * 1024
F32, BF16 = jnp.float32, jnp.bfloat16

PIX = 1024
SEG_LINES = ((0, 24), (24, 32))
BUF_LINES = 36


class Plan:
    def __init__(self, shapes, n_band):
        (self.n_s, self.cap_s, self.side_s, _), (self.n_m, self.cap_m, self.side_m, _), (
            self.n_l,
            self.cap_l,
            self.side_l,
            _,
        ) = shapes
        assert (self.side_s, self.side_m, self.side_l) == (16, 24, 32)
        self.n_band = n_band
        self.n_chip = n_band // 2
        self.r_s, self.r_m, self.r_l = (
            self.cap_s * self.side_s,
            self.cap_m * self.side_m,
            self.cap_l * self.side_l,
        )
        holders = [dict() for _ in range(n_band)]
        for i in range(self.n_l):
            holders[2 * i]["l"] = i
        free = [b for b in range(n_band) if "l" not in holders[b]]
        for i in range(self.n_m):
            holders[free[i]]["m"] = i
        spots = [b for b in free if b >= 2 * self.n_l]
        for i in range(self.n_s):
            holders[spots[i]]["s"] = i
        self.holders = holders
        self.sizes = [
            (self.r_l if "l" in h else 0)
            + (self.r_m if "m" in h else 0)
            + (self.r_s if "s" in h else 0)
            for h in holders
        ]
        self.block = max(self.sizes[2 * j] + self.sizes[2 * j + 1] for j in range(self.n_chip))
        self.piece = max(self.sizes)
        self.offs = [0 if b % 2 == 0 else self.piece - self.sizes[b] for b in range(n_band)]
        self.is_l = np.array([int("l" in h) for h in holders], np.int32)
        self.has_m = np.array([int("m" in h) for h in holders], np.int32)
        self.has_s = np.array([int("s" in h) for h in holders], np.int32)
        self.off = np.array(self.offs, np.int32)


def pick(table, index):
    return lax.dynamic_index_in_dim(jnp.asarray(table), index, 0, keepdims=False)


def make_tables(plan, band_rows, position):
    nz = plan.n_chip
    z, core = position // 2, position % 2
    is_l, has_m, has_s, off = (pick(t, position) for t in (plan.is_l, plan.has_m, plan.has_s, plan.off))
    starts = jnp.cumsum(band_rows, axis=1) - band_rows
    zero_in = plan.n_band * plan.piece // 8

    def band_of(member, rows):
        return jnp.sum((starts[member][None, :] <= rows[:, None]).astype(jnp.int32), axis=1) - 1

    def place(member, rows):
        band = band_of(member, rows)
        onehot = band[:, None] == jnp.arange(plan.n_band)[None, :]
        start = jnp.sum(jnp.where(onehot, starts[member][None, :], 0), axis=1)
        k = (z - band // 2) % nz
        pos = jnp.where(band % 2 == core, k, nz + k)
        return pos * plan.piece + off, rows - start

    q = np.arange(128)
    base, r = place(2, jnp.asarray(q // 4, jnp.int32))
    src_l = (base + r * 32) // 8 + jnp.asarray(q % 4, jnp.int32)
    base, r = place(1, jnp.asarray(np.minimum(q // 4, 23), jnp.int32))
    src_m = (base + r * 24) // 8 + jnp.asarray(q % 4, jnp.int32)
    ok_m = jnp.asarray((q < 96) & (q % 4 < 3)) & (has_m == 1)
    line = np.clip((q - 96) // 4, 0, 7)
    base, r = place(0, jnp.asarray(line + 8 * (q % 4 // 2), jnp.int32))
    src_s = (base + has_m * plan.r_m + r * 16) // 8 + jnp.asarray(q % 2, jnp.int32)
    ok_s = jnp.asarray(q >= 96) & (has_s == 1)
    gather = jnp.where(
        is_l == 1, src_l, jnp.where(ok_m, src_m, jnp.where(ok_s, src_s, zero_in))
    ).astype(jnp.int32)

    per = plan.piece // 8
    p, t = np.divmod(np.arange(plan.n_band * per), per)
    k = jnp.asarray(p % nz, jnp.int32)
    c_src = jnp.where(jnp.asarray(p < nz), core, 1 - core)
    band = 2 * ((z - k) % nz) + c_src
    onehot = band[:, None] == jnp.arange(plan.n_band)[None, :]

    def of_band(row):
        return jnp.sum(jnp.where(onehot, row[None, :], 0), axis=1)

    within = jnp.asarray(t * 8, jnp.int32) - off
    wl = jnp.maximum(within, 0)
    r = wl // 32
    ok_l = (within >= 0) & (r < of_band(band_rows[2]))
    out_l = (of_band(starts[2]) + r) * 4 + wl % 32 // 8
    r = wl // 24
    in_m = (has_m == 1) & (wl < plan.r_m)
    ok_m = (within >= 0) & in_m & (r < of_band(band_rows[1]))
    out_m = (of_band(starts[1]) + r) * 4 + wl % 24 // 8
    ws = jnp.maximum(wl - has_m * plan.r_m, 0)
    r = ws // 16
    h = of_band(starts[0]) + r
    ok_s = (within >= 0) & (has_s == 1) & ~in_m & (r < of_band(band_rows[0]))
    out_s = 96 + (h % 8) * 4 + (h // 8) * 2 + ws % 16 // 8
    scatter = jnp.where(
        is_l == 1,
        jnp.where(ok_l, out_l, 128),
        jnp.where(ok_m, out_m, jnp.where(ok_s, out_s, 128)),
    ).astype(jnp.int32)
    flags = jnp.stack(
        [
            is_l,
            jnp.where(is_l == 1, 32, 24 * has_m),
            jnp.where(is_l == 1, 32, 32 * has_s),
            jnp.where(is_l == 1, 0, 16),
            core,
        ]
    ).astype(jnp.int32)
    return gather, scatter, flags


class Scalars:
    def __init__(self, flags):
        self.is_l = flags[0]
        self.lims = (flags[1], flags[2])
        self.split = flags[3]
        self.core = flags[4]
        self.l_f = flags[0].astype(F32)
        large = flags[0] == 1
        self.inv = (
            jnp.where(large, 1.0 / (1024 * 16), 1.0 / (576 * 16)).astype(F32),
            jnp.where(large, 1.0 / (1024 * 16), 1.0 / (256 * 16)).astype(F32),
        )


def dot(a, b):
    return jnp.dot(a, b, preferred_element_type=F32)


def dot_nt(a, b):
    return lax.dot_general(a, b, (((1,), (1,)), ((), ())), preferred_element_type=F32)


def dot_tn(a, b):
    return lax.dot_general(a, b, (((0,), (0,)), ((), ())), preferred_element_type=F32)


def line_rows(line):
    return pl.ds(pl.multiple_of(line * 32, 32), 32)


def line_loop(body, carries, unroll=2):
    results = []
    for seg, (low, high) in enumerate(SEG_LINES):
        results.append(
            lax.fori_loop(
                low, high, lambda line, carry, seg=seg: body(seg, line, carry), carries[seg], unroll=unroll
            )
        )
    return results


def fold(value):
    return value.reshape(4, 8, C).sum(axis=0)


def columns():
    return lax.broadcasted_iota(jnp.int32, (32, C), 0)


def fill_group_matrix(gm_ref):
    row = lax.broadcasted_iota(jnp.int32, (C, C), 0) // (C // GROUPS)
    col = lax.broadcasted_iota(jnp.int32, (C, C), 1) // (C // GROUPS)
    gm_ref[...] = (row == col).astype(F32).astype(BF16)


def group_totals(gm_ref, scal, per_seg):
    stacked = jnp.concatenate(list(per_seg) + [jnp.zeros((8 - len(per_seg), C), F32)], axis=0)
    hi = stacked.astype(BF16)
    rest = stacked - hi.astype(F32)
    mid = rest.astype(BF16)
    low = (rest - mid.astype(F32)).astype(BF16)
    both = dot(jnp.concatenate([hi, mid, low, jnp.zeros((8, C), BF16)], axis=0), gm_ref[...])
    total = both[0:8] + both[8:16] + both[16:24]
    out = []
    for i in range(0, len(per_seg), 2):
        first, second = total[i : i + 1], total[i + 1 : i + 2]
        out.append((first + scal.l_f * second, second + scal.l_f * first))
    return out


def norm_stats(read, gm_ref, scal):
    zero = jnp.zeros((8, C), F32)
    sums = line_loop(lambda seg, line, acc: acc + fold(read(line)), (zero, zero))
    sums = [s.sum(axis=0, keepdims=True) for s in sums]
    (totals,) = group_totals(gm_ref, scal, sums)
    means = [totals[seg] * scal.inv[seg] for seg in range(2)]
    col = columns()

    def squares(seg, line, acc):
        dev = jnp.where(col < scal.lims[seg], read(line) - means[seg], 0.0)
        return acc + fold(dev * dev)

    sums = line_loop(squares, (zero, zero))
    sums = [s.sum(axis=0, keepdims=True) for s in sums]
    (totals,) = group_totals(gm_ref, scal, sums)
    rstds = [lax.rsqrt(totals[seg] * scal.inv[seg] + EPSILON) for seg in range(2)]
    return means, rstds


def store_shifted(buf_ref, scal, seg, line, value16):
    col = columns()
    value = value16.astype(F32)
    keep_left, keep_right = col != 0, col != 31
    if seg == 1:
        keep_left &= col != scal.split
        keep_right &= col != scal.split - 1
    left = jnp.where(keep_left, pltpu.roll(value, 1, 0), 0.0).astype(BF16)
    right = jnp.where(keep_right, pltpu.roll(value, 31, 0), 0.0).astype(BF16)
    at = line_rows(line + (1 if seg == 0 else 3))
    buf_ref[at, 0:C] = left
    buf_ref[at, C : 2 * C] = value16
    buf_ref[at, 2 * C : 3 * C] = right


def fill_halos(buf_ref, scal):
    zero = jnp.zeros((32, 3 * C), BF16)
    buf_ref[0:32, :] = zero
    buf_ref[25 * 32 : 26 * 32, :] = zero
    buf_ref[26 * 32 : 27 * 32, :] = zero
    buf_ref[35 * 32 : 36 * 32, :] = zero

    @pl.when(scal.is_l == 1)
    def _():
        buf_ref[25 * 32 : 26 * 32, :] = buf_ref[27 * 32 : 28 * 32, :]
        buf_ref[26 * 32 : 27 * 32, :] = buf_ref[24 * 32 : 25 * 32, :]

    @pl.when(scal.is_l == 0)
    def _():
        buf_ref[26 * 32 + 16 : 27 * 32, :] = buf_ref[34 * 32 : 34 * 32 + 16, :]
        buf_ref[35 * 32 : 35 * 32 + 16, :] = buf_ref[27 * 32 + 16 : 28 * 32, :]


def tile_rows(tile, shift):
    line = (8 * tile if tile < 3 else 26) + shift
    return slice(line * 32, line * 32 + 256)


def conv_tiles(buf_ref, w_ref, write):
    for tile in range(4):
        acc = None
        for shift in range(3):
            term = dot(buf_ref[tile_rows(tile, shift), :], w_ref[shift * 3 * C : (shift + 1) * 3 * C, :])
            acc = term if acc is None else acc + term
        write(tile, acc)


def gather_pieces(table_ref, src_ref, dst_ref, count):
    def step(i, carry):
        at = pl.multiple_of(table_ref[i] * 8, 8)
        dst_ref[pl.ds(pl.multiple_of(i * 8, 8), 8), :] = src_ref[pl.ds(at, 8), :]
        return carry

    lax.fori_loop(0, count, step, 0, unroll=4)


def slots_to_image(table_ref, scal, blocks, slots_ref, image_ref):
    piece = (slots_ref.shape[0] - 8) // len(blocks)
    start = pl.multiple_of((blocks[0].shape[0] - piece) * scal.core, 16)
    for i, block in enumerate(blocks):
        slots_ref[i * piece : (i + 1) * piece, :] = block[pl.ds(start, piece), :].astype(F32)
    slots_ref[len(blocks) * piece :, :] = jnp.zeros((8, C), F32)
    gather_pieces(table_ref, slots_ref, image_ref, 128)


def image_to_slots(table_ref, image_ref, slots_ref, own_ref, oth_ref):
    half = own_ref.shape[0]
    gather_pieces(table_ref, image_ref, slots_ref, 2 * half // 8)
    own_ref[...] = slots_ref[0:half, :].astype(BF16)
    oth_ref[...] = slots_ref[half : 2 * half, :].astype(BF16)


def swish_slope(value):
    sigma = jax.nn.sigmoid(value)
    return sigma * (1.0 + value * (1.0 - sigma))


def load_weights(pieces, parts, table, w, small16, sems):
    copies, last = [], len(parts) * len(pieces)
    if len(pieces) == 1:
        copies.append(pltpu.make_async_copy(pieces[0].at[pl.ds(0, 22 * C)], w, sems.at[0]))
        copy = pltpu.make_async_copy(pieces[0].at[pl.ds(22 * C, 16)], small16, sems.at[1])
        copies[0].start()
        copy.start()
        copy.wait()
    else:
        for i, piece in enumerate(pieces):
            for start, count in parts:
                e = len(copies)
                at = pl.multiple_of(table[e] * 16, 16)
                copy = pltpu.make_async_copy(
                    piece.at[pl.ds(start, count)], w.at[pl.ds(at, count)], sems.at[e]
                )
                copy.start()
                copies.append(copy)

            @pl.when(table[last] == i)
            def _():
                copy = pltpu.make_async_copy(
                    piece.at[pl.ds(parts[-1][0] + parts[-1][1], 16)], small16, sems.at[last]
                )
                copy.start()
                copy.wait()

    def wait():
        for copy in copies:
            copy.wait()

    return wait


def features_kernel(first, sources, count, parts, *refs):
    if first:
        gather, flags, table = refs[:3]
        blocks, refs = refs[3 : 3 + sources], refs[3 + sources :]
        pieces, refs = refs[:count], refs[count:]
        (
            x_out,
            a1_out,
            h1_out,
            a2_out,
            y_ref,
            z_out,
            q_ref,
            k_ref,
            v_ref,
            stats_out,
            small,
            w_out,
        ) = refs[:12]
        slots, x_ref, h_ref, z_ref, buf, w, gm, sems, small16 = refs[12:]
    else:
        gather, scatter, flags, table = refs[:4]
        blocks, refs = refs[4 : 4 + sources], refs[4 + sources :]
        pieces, refs = refs[:count], refs[count:]
        own_out, oth_out = refs[:2]
        slots, x_ref, h_ref, z_ref, buf, w, gm, sems, small16, small, y_ref, q_ref, k_ref, v_ref = refs[2:]
    wait_weights = load_weights(pieces, parts, table, w, small16, sems)
    scal = Scalars(flags)
    fill_group_matrix(gm)
    slots_to_image(gather, scal, blocks, slots, x_ref)
    small[...] = small16[...].astype(F32)
    col = columns()

    def row(i):
        return small[i : i + 1, :]

    def activate(read, means, rstds, gain, shift, keep):
        def body(seg, line, carry):
            normed = (read(line) - means[seg]) * rstds[seg] * gain + shift
            act = jnp.where(col < scal.lims[seg], normed * jax.nn.sigmoid(normed), 0.0).astype(BF16)
            if keep is not None:
                keep[line_rows(line), :] = act
            store_shifted(buf, scal, seg, line, act)
            return carry

        line_loop(body, (0, 0))
        fill_halos(buf, scal)

    def read_x(line):
        return x_ref[line_rows(line), :]

    means1, rstds1 = norm_stats(read_x, gm, scal)
    activate(read_x, means1, rstds1, row(0), row(1), a1_out if first else None)
    if first:

        def keep_x(seg, line, carry):
            x_out[line_rows(line), :] = read_x(line).astype(BF16)
            return carry

        line_loop(keep_x, (0, 0))

    wait_weights()
    if first:
        save = pltpu.make_async_copy(w, w_out, sems.at[0])
        save.start()

    def write_h(tile, acc):
        h_ref[tile * 256 : (tile + 1) * 256, :] = acc

    conv_tiles(buf, w.at[0 : 9 * C], write_h)

    def finish_h(seg, line, carry):
        value = jnp.where(col < scal.lims[seg], h_ref[line_rows(line), :] + row(2), 0.0)
        h_ref[line_rows(line), :] = value
        if first:
            h1_out[line_rows(line), :] = value
        return carry

    line_loop(finish_h, (0, 0))

    def read_h(line):
        return h_ref[line_rows(line), :]

    means2, rstds2 = norm_stats(read_h, gm, scal)
    activate(read_h, means2, rstds2, row(3), row(4), a2_out if first else None)
    conv_tiles(buf, w.at[9 * C : 18 * C], write_h)

    def finish_y(seg, line, carry):
        value = jnp.where(
            col < scal.lims[seg], read_x(line) + (h_ref[line_rows(line), :] + row(5)), 0.0
        )
        y_ref[line_rows(line), :] = value
        return carry

    line_loop(finish_y, (0, 0))

    def read_y(line):
        return y_ref[line_rows(line), :]

    means3, rstds3 = norm_stats(read_y, gm, scal)

    def third(seg, line, carry):
        normed = (read_y(line) - means3[seg]) * rstds3[seg] * row(6) + row(7)
        value = jnp.where(col < scal.lims[seg], normed, 0.0).astype(BF16)
        z_ref[line_rows(line), :] = value
        if first:
            z_out[line_rows(line), :] = value
        return carry

    line_loop(third, (0, 0))
    for tile in range(4):
        at = slice(tile * 256, (tile + 1) * 256)
        rows = z_ref[at, :]
        q_ref[at, :] = (dot(rows, w[18 * C : 19 * C, :]) + row(8)).astype(BF16)
        k_ref[at, :] = dot(rows, w[19 * C : 20 * C, :]).astype(BF16)
        v_ref[at, :] = (dot(rows, w[20 * C : 21 * C, :]) + row(9)).astype(BF16)
    if first:
        for i, pair in enumerate((means1, rstds1, means2, rstds2, means3, rstds3)):
            stats_out[2 * i : 2 * i + 1, :] = pair[0]
            stats_out[2 * i + 1 : 2 * i + 2, :] = pair[1]
        stats_out[12:16, :] = jnp.zeros((4, C), F32)
        save.wait()
        return
    biases = key_bias(scal)
    for tile in range(4):
        at = slice(tile * 256, (tile + 1) * 256)
        prob = probabilities(q_ref[at, :], k_ref, biases[tile // 3]).astype(BF16)
        mixed = dot(prob, v_ref[...]).astype(BF16)
        y_ref[at, :] = y_ref[at, :] + (dot(mixed, w[21 * C : 22 * C, :]) + row(10))
    y_ref[PIX : PIX + 8, :] = jnp.zeros((8, C), F32)
    image_to_slots(scatter, y_ref, slots, own_out, oth_out)


def key_bias(scal):
    key = lax.broadcasted_iota(jnp.int32, (1, PIX), 1)
    column = key % 32
    in0 = key < 768
    ok0 = in0 & (column < scal.lims[0])
    ok1 = (~in0) & (column < scal.lims[1])
    large = scal.is_l == 1
    row0 = jnp.where(ok0 | (ok1 & large), 0.0, -1e30).astype(F32)
    row1 = jnp.where(ok1 | (ok0 & large), 0.0, -1e30).astype(F32)
    return row0, row1


def probabilities(q, k_ref, bias):
    scores = dot_nt(q, k_ref[...]) * (C**-0.5) + bias
    top = jnp.max(scores, axis=1, keepdims=True)
    expo = jnp.exp(scores - top)
    return expo * (1.0 / jnp.sum(expo, axis=1, keepdims=True))


def attend_both_kernel(
    gather,
    scatter,
    flags,
    q,
    k,
    v,
    y,
    z,
    stats,
    small,
    weights,
    *refs,
):
    blocks = refs[:-16]
    own_out, oth_out, dy_out, dy16_out, grads_out, sums_out = refs[-16:-10]
    image, slots, g_ref, o_ref, d_ref, dk_acc, dv_acc, wp, gm, sems = refs[-10:]
    copy = pltpu.make_async_copy(weights.at[pl.ds(18 * C, 4 * C)], wp, sems.at[0])
    copy.start()
    scal = Scalars(flags)
    fill_group_matrix(gm)
    biases = key_bias(scal)
    slots_to_image(gather, scal, blocks, slots, g_ref)
    copy.wait()
    scaling = C**-0.5
    for tile in range(4):
        at = slice(tile * 256, (tile + 1) * 256)
        q_t = q[at, :]
        prob = probabilities(q_t, k, biases[tile // 3])
        prob16 = prob.astype(BF16)
        mixed = dot(prob16, v[...]).astype(BF16)
        o_ref[at, :] = mixed
        image[at, :] = y[at, :] + (dot(mixed, wp[3 * C : 4 * C, :]) + small[10:11, :])
        d_mixed = dot_nt(g_ref[at, :].astype(BF16), wp[3 * C : 4 * C, :]).astype(BF16)
        d_prob = dot_nt(d_mixed, v[...])
        inner = jnp.sum(prob * d_prob, axis=1, keepdims=True)
        d_score = (prob * (d_prob - inner)).astype(BF16)
        d_ref[at, 0:C] = (scaling * dot(d_score, k[...])).astype(BF16)
        dk = dot_tn(d_score, q_t)
        dv = dot_tn(prob16, d_mixed)
        if tile == 0:
            dk_acc[...] = dk
            dv_acc[...] = dv
        else:
            dk_acc[...] += dk
            dv_acc[...] += dv
    d_ref[:, C : 2 * C] = (scaling * dk_acc[...]).astype(BF16)
    d_ref[:, 2 * C : 3 * C] = dv_acc[...].astype(BF16)
    image[PIX : PIX + 8, :] = jnp.zeros((8, C), F32)
    image_to_slots(scatter, image, slots, own_out, oth_out)
    for part in range(3):
        grads_out[part * C : (part + 1) * C, :] = dot_tn(
            z[...], d_ref[:, part * C : (part + 1) * C]
        ).astype(BF16)
    grads_out[3 * C : 4 * C, :] = dot_tn(o_ref[...], g_ref[...].astype(BF16)).astype(BF16)
    for tile in range(4):
        at = slice(tile * 256, (tile + 1) * 256)
        acc = dot_nt(d_ref[at, 0:C], wp[0:C, :])
        acc = acc + dot_nt(d_ref[at, C : 2 * C], wp[C : 2 * C, :])
        image[at, :] = acc + dot_nt(d_ref[at, 2 * C : 3 * C], wp[2 * C : 3 * C, :])
    col = columns()
    means = (stats[8:9, :], stats[9:10, :])
    rstds = (stats[10:11, :], stats[11:12, :])
    zero = jnp.zeros((8, C), F32)

    def sums(seg, line, acc):
        at = line_rows(line)
        d_norm = image[at, :]
        unit = (y[at, :] - means[seg]) * rstds[seg]
        d_all = d_ref[at, :].astype(F32)
        return (
            acc[0] + fold(d_norm),
            acc[1] + fold(d_norm * unit),
            acc[2] + fold(d_all[:, 0:C]),
            acc[3] + fold(d_all[:, 2 * C : 3 * C]),
            acc[4] + fold(g_ref[at, :]),
        )

    got = line_loop(sums, ((zero,) * 5, (zero,) * 5), unroll=1)
    got = [[part.sum(axis=0, keepdims=True) for part in seg] for seg in got]
    gain = small[6:7, :]
    ones, cross = group_totals(
        gm, scal, [got[0][0] * gain, got[1][0] * gain, got[0][1] * gain, got[1][1] * gain]
    )
    for i, part in enumerate((1, 0, 2, 3, 4)):
        sums_out[i : i + 1, :] = got[0][part] + got[1][part]
    sums_out[5:8, :] = jnp.zeros((3, C), F32)

    def back(seg, line, carry):
        at = line_rows(line)
        unit = (y[at, :] - means[seg]) * rstds[seg]
        d_in = rstds[seg] * (
            image[at, :] * gain - ones[seg] * scal.inv[seg] - unit * (cross[seg] * scal.inv[seg])
        )
        value = g_ref[at, :] + jnp.where(col < scal.lims[seg], d_in, 0.0)
        dy_out[at, :] = value
        dy16_out[at, :] = value.astype(BF16)
        return carry

    line_loop(back, (0, 0))


def fill_gradient_buffer(buf, scal, grad_ref):
    def body(seg, line, carry):
        store_shifted(buf, scal, seg, line, grad_ref[line_rows(line), :])
        return carry

    line_loop(body, (0, 0))
    fill_halos(buf, scal)


def weight_grad_kernel(conv, split, *refs):
    if not split:
        flags, act, grad, w_out, sums_out, buf, act_t = refs
    elif conv == 1:
        flags, act, grad, proj, kept, sent, early, sums_out, buf, act_t = refs
    else:
        flags, act, grad, early, kept, sent, sums_out, buf, act_t = refs
    scal = Scalars(flags)

    def put(unit, value16):
        if split and conv == 1 and unit < 44:
            early[(unit - 36) * 128 : (unit - 35) * 128, :] = value16
            return
        if not split:
            unit -= 36 * conv
            w_out[unit * 128 : (unit + 1) * 128, :] = value16
            return
        row = (unit // 22 % 2) * 1408 + unit % 11 * 128
        mine = scal.core == unit % 22 // 11

        @pl.when(mine)
        def _():
            kept[row : row + 128, :] = value16

        @pl.when(jnp.logical_not(mine))
        def _():
            sent[row : row + 128, :] = value16

    if split and conv == 1:
        for i in range(16):
            put(72 + i, proj[i * 128 : (i + 1) * 128, :])
    elif split:
        for i in range(8):
            put(36 + i, early[i * 128 : (i + 1) * 128, :])
    fill_gradient_buffer(buf, scal, grad)
    for tile in range(4):
        at = slice(tile * 256, (tile + 1) * 256)
        act_t[:, at] = act[at, :].T
    for shift in range(3):
        seg0 = slice(shift * 32, shift * 32 + 768)
        seg1 = slice((26 + shift) * 32, (26 + shift) * 32 + 256)
        for part in range(3):
            cols = slice(part * C, (part + 1) * C)
            tap = 3 * (2 - shift) + (2 - part)
            value = dot(act_t[:, 0:768], buf[seg0, cols]) + dot(act_t[:, 768:1024], buf[seg1, cols])
            value16 = value.astype(BF16)
            for i in range(4):
                put(36 * conv + 4 * tap + i, value16[i * 128 : (i + 1) * 128])
    zero = jnp.zeros((8, C), F32)
    got = line_loop(
        lambda seg, line, acc: acc + fold(grad[line_rows(line), :].astype(F32)), (zero, zero)
    )
    sums_out[...] = jnp.zeros((8, C), F32)
    sums_out[0:1, :] = (got[0] + got[1]).sum(axis=0, keepdims=True)


def data_grad_kernel(last, conv, *refs):
    if last:
        scatter, flags, grad, feat, dy, stats, small, weights, own_out, oth_out, sums_out = refs[:11]
        dn, slots, buf, w, gm, sems = refs[11:]
    else:
        flags, grad, feat, stats, small, weights, grad_out, sums_out = refs[:8]
        dn, buf, w, gm, sems = refs[8:]
    copy = pltpu.make_async_copy(weights.at[pl.ds(conv * 9 * C, 9 * C)], w, sems.at[0])
    copy.start()
    scal = Scalars(flags)
    fill_group_matrix(gm)
    fill_gradient_buffer(buf, scal, grad)
    copy.wait()
    for tile in range(4):
        acc = None
        for shift in range(3):
            for part in range(3):
                tap = 3 * (2 - shift) + (2 - part)
                term = dot_nt(
                    buf[tile_rows(tile, shift), part * C : (part + 1) * C], w[tap * C : (tap + 1) * C, :]
                )
                acc = term if acc is None else acc + term
        dn[tile * 256 : (tile + 1) * 256, :] = acc
    base = 4 * conv
    means = (stats[base : base + 1, :], stats[base + 1 : base + 2, :])
    rstds = (stats[base + 2 : base + 3, :], stats[base + 3 : base + 4, :])
    gain, shift_row = small[3 * conv : 3 * conv + 1, :], small[3 * conv + 1 : 3 * conv + 2, :]
    col = columns()
    zero = jnp.zeros((8, C), F32)

    def sums(seg, line, acc):
        at = line_rows(line)
        unit = (feat[at, :].astype(F32) - means[seg]) * rstds[seg]
        value = dn[at, :] * swish_slope(unit * gain + shift_row)
        value = jnp.where(col < scal.lims[seg], value, 0.0)
        dn[at, :] = value
        return (acc[0] + fold(value), acc[1] + fold(value * unit))

    got = line_loop(sums, ((zero, zero), (zero, zero)))
    got = [[part.sum(axis=0, keepdims=True) for part in seg] for seg in got]
    ones, cross = group_totals(
        gm, scal, [got[0][0] * gain, got[1][0] * gain, got[0][1] * gain, got[1][1] * gain]
    )
    sums_out[...] = jnp.zeros((8, C), F32)
    sums_out[0:1, :] = got[0][1] + got[1][1]
    sums_out[1:2, :] = got[0][0] + got[1][0]

    def back(seg, line, carry):
        at = line_rows(line)
        unit = (feat[at, :].astype(F32) - means[seg]) * rstds[seg]
        value = rstds[seg] * (
            dn[at, :] * gain - ones[seg] * scal.inv[seg] - unit * (cross[seg] * scal.inv[seg])
        )
        value = jnp.where(col < scal.lims[seg], value, 0.0)
        if last:
            dn[at, :] = value + dy[at, :]
        else:
            grad_out[at, :] = value.astype(BF16)
        return carry

    line_loop(back, (0, 0))
    if last:
        dn[PIX : PIX + 8, :] = jnp.zeros((8, C), F32)
        image_to_slots(scatter, dn, slots, own_out, oth_out)


SMEM = pl.BlockSpec(memory_space=pltpu.SMEM)
VMEM = pl.BlockSpec(memory_space=pltpu.VMEM)
ANY = pl.BlockSpec(memory_space=pl.ANY)


def call(kernel, name, in_specs, outs, scratch, flops, args, out_specs=None):
    moved = sum(int(np.prod(a.shape)) * a.dtype.itemsize for a in args)
    moved += sum(int(np.prod(s)) * jnp.dtype(d).itemsize for s, d in outs)
    return pl.pallas_call(
        kernel,
        name=name,
        out_shape=[jax.ShapeDtypeStruct(s, d) for s, d in outs],
        in_specs=in_specs,
        out_specs=out_specs or [VMEM] * len(outs),
        scratch_shapes=scratch,
        compiler_params=pltpu.CompilerParams(vmem_limit_bytes=VMEM_BYTES),
        cost_estimate=pl.CostEstimate(flops=int(flops), bytes_accessed=moved, transcendentals=0),
    )(*args)


MAP, SLOT_PAD = (PIX, C), 8
MICROSECOND = 1_100_000_000
BUF = pltpu.VMEM((BUF_LINES * 32, 3 * C), BF16)


def run_features(first, plan, tables, blocks, pieces, parts, table):
    gather, scatter, flags = tables
    slot_rows = plan.n_band * plan.piece
    scratch = [
        pltpu.VMEM((slot_rows + SLOT_PAD, C), F32),
        pltpu.VMEM(MAP, F32),
        pltpu.VMEM(MAP, F32),
        pltpu.VMEM(MAP, BF16),
        BUF,
        pltpu.VMEM((22 * C, C), BF16),
        pltpu.VMEM((C, C), BF16),
        pltpu.SemaphoreType.DMA((len(parts) * len(pieces) + 1,)),
        pltpu.VMEM((16, C), BF16),
    ]
    count = len(pieces)
    if first:
        outs = [
            (MAP, BF16),
            (MAP, BF16),
            (MAP, F32),
            (MAP, BF16),
            (MAP, F32),
            (MAP, BF16),
            (MAP, BF16),
            (MAP, BF16),
            (MAP, BF16),
            ((16, C), F32),
            ((16, C), F32),
            ((22 * C, C), BF16),
        ]
        return call(
            functools.partial(features_kernel, True, len(blocks), count, parts),
            "features_first",
            [SMEM] * 3 + [VMEM] * len(blocks) + [ANY] * count,
            outs,
            scratch,
            26 * MICROSECOND,
            (gather, flags, table, *blocks, *pieces),
            out_specs=[VMEM] * 11 + [ANY],
        )
    return call(
        functools.partial(features_kernel, False, len(blocks), count, parts),
        "forward_again",
        [SMEM] * 4 + [VMEM] * len(blocks) + [ANY] * count,
        [((slot_rows // 2, C), BF16)] * 2,
        scratch
        + [
            pltpu.VMEM((16, C), F32),
            pltpu.VMEM((PIX + 8, C), F32),
            pltpu.VMEM(MAP, BF16),
            pltpu.VMEM(MAP, BF16),
            pltpu.VMEM(MAP, BF16),
        ],
        28 * MICROSECOND,
        (gather, scatter, flags, table, *blocks, *pieces),
    )


def run_attend_both(plan, tables, q, k, v, y, z, blocks, stats, small, weights):
    gather, scatter, flags = tables
    slot_rows = plan.n_band * plan.piece
    return call(
        attend_both_kernel,
        "attend_both",
        [SMEM] * 3 + [VMEM] * 7 + [ANY] + [VMEM] * len(blocks),
        [
            ((slot_rows // 2, C), BF16),
            ((slot_rows // 2, C), BF16),
            (MAP, F32),
            (MAP, BF16),
            ((4 * C, C), BF16),
            ((8, C), F32),
        ],
        [
            pltpu.VMEM((PIX + 8, C), F32),
            pltpu.VMEM((slot_rows + SLOT_PAD, C), F32),
            pltpu.VMEM(MAP, F32),
            pltpu.VMEM(MAP, BF16),
            pltpu.VMEM((PIX, 3 * C), BF16),
            pltpu.VMEM(MAP, F32),
            pltpu.VMEM(MAP, F32),
            pltpu.VMEM((4 * C, C), BF16),
            pltpu.VMEM((C, C), BF16),
            pltpu.SemaphoreType.DMA((1,)),
        ],
        24 * MICROSECOND,
        (gather, scatter, flags, q, k, v, y, z, stats, small, weights, *blocks),
    )


def run_weight_grad(tables, conv, act, grad, more=None):
    split = more is not None
    outs = [((2816, C), BF16)] * 2 if split else [((9 * C, C), BF16)]
    if split and conv == 1:
        outs.append(((2 * C, C), BF16))
    return call(
        functools.partial(weight_grad_kernel, conv, split),
        "weight_grad_one" if conv == 0 else "weight_grad_two",
        [SMEM, VMEM, VMEM] + [VMEM] * split,
        outs + [((8, C), F32)],
        [BUF, pltpu.VMEM((C, PIX), BF16)],
        12 * MICROSECOND,
        (tables[2], act, grad) + ((more,) if split else ()),
    )


def run_data_grad(tables, conv, grad, feat, stats, small, weights, dy=None, half=None):
    last = dy is not None
    scratch = [BUF, pltpu.VMEM((9 * C, C), BF16), pltpu.VMEM((C, C), BF16), pltpu.SemaphoreType.DMA((1,))]
    if last:
        outs = [((half, C), BF16)] * 2
        scratch = [pltpu.VMEM((PIX + 8, C), F32), pltpu.VMEM((2 * half, C), F32)] + scratch
        args = (tables[1], tables[2], grad, feat, dy, stats, small, weights)
        specs = [SMEM, SMEM] + [VMEM] * 5 + [ANY]
    else:
        outs = [(MAP, BF16)]
        scratch = [pltpu.VMEM(MAP, F32)] + scratch
        args = (tables[2], grad, feat, stats, small, weights)
        specs = [SMEM] + [VMEM] * 4 + [ANY]
    return call(
        functools.partial(data_grad_kernel, last, conv),
        "data_grad_one" if conv == 0 else "data_grad_two",
        specs,
        outs + [((8, C), F32)],
        scratch,
        12 * MICROSECOND,
        args,
    )


def z_shift(value, nz, k):
    return lax.ppermute(value, "band", [(2 * z + c, 2 * ((z + k) % nz) + c) for z in range(nz) for c in range(2)])


def core_swap(value, n_band):
    return lax.ppermute(value, "band", [(b, b ^ 1) for b in range(n_band)])


def stage(values):
    return lax.optimization_barrier(values)


def pack_slots(plan, arrays):
    flat = [a.reshape(a.shape[0], -1, C) for a in arrays]
    blocks = []
    for chip in range(plan.n_chip):
        parts = []
        for c in range(2):
            h = plan.holders[2 * chip + c]
            mine = [flat[m][h[name]] for m, name in ((2, "l"), (1, "m"), (0, "s")) if name in h]
            if c == 1:
                used = plan.sizes[2 * chip] + plan.sizes[2 * chip + 1]
                if used < plan.block:
                    parts.append(jnp.zeros((plan.block - used, C), BF16))
            parts += mine
        blocks.append(jnp.concatenate(parts, axis=0))
    return jnp.stack(blocks)


def chip_blocks(plan, position, arrays):
    z, nz = position // 2, plan.n_chip
    sent = pack_slots(plan, arrays)
    return [lax.dynamic_index_in_dim(sent, (z + k) % nz, 0, keepdims=False) for k in range(nz)]


def to_chips(plan, blocks):
    return [blocks[0]] + [z_shift(blocks[k], plan.n_chip, k) for k in range(1, plan.n_chip)]


def to_cores(plan, received):
    return [*received, *[core_swap(block, plan.n_band) for block in received]]


def merge_cores(plan, position, own, got):
    core, nz, slack = position % 2, plan.n_chip, plan.block - plan.piece
    own, got = own.reshape(nz, plan.piece, C), got.reshape(nz, plan.piece, C)
    first, second = jnp.where(core == 0, own, got), jnp.where(core == 0, got, own)
    return jnp.pad(first, ((0, 0), (0, slack), (0, 0))) + jnp.pad(second, ((0, 0), (slack, 0), (0, 0)))


def from_chips(plan, blocks):
    return [blocks[0]] + [z_shift(blocks[k], plan.n_chip, -k) for k in range(1, plan.n_chip)]


def to_bands(plan, position, received):
    z, nz, slack = position // 2, plan.n_chip, plan.block - plan.piece
    received = jnp.stack(received)
    images = [[None] * plan.n_s, [None] * plan.n_m, [None] * plan.n_l]
    for b, h in enumerate(plan.holders):
        chip = b // 2
        if not h:
            continue
        block = lax.dynamic_index_in_dim(received, (chip - z) % nz, 0, keepdims=False)
        at = plan.offs[b] + (slack if b % 2 else 0)
        for member, name, size in ((2, "l", plan.r_l), (1, "m", plan.r_m), (0, "s", plan.r_s)):
            if name in h:
                images[member][h[name]] = block[at : at + size]
                at += size
    sides = (plan.side_s, plan.side_m, plan.side_l)
    return [
        jnp.stack(images[m]).reshape(len(images[m]), -1, sides[m], C) for m in range(3)
    ]


class Place:
    def __init__(self):
        self.n_band, self.n_img = lax.axis_size("band"), lax.axis_size("img")
        self.count = self.n_band * self.n_img
        self.position, self.img = lax.axis_index("band"), lax.axis_index("img")
        self.owner = self.position * self.n_img + self.img
        self.z, self.core = self.position // 2, self.position % 2
        self.y, self.x = self.img // 2, self.img % 2
        self.planes = self.n_band == 8 and self.n_img == 4


def over_core(value):
    return core_swap(value, lax.axis_size("band"))


def over_x(value):
    return lax.ppermute(value, "img", [(i, i ^ 1) for i in range(4)])


def over_y(value):
    return lax.ppermute(value, "img", [(i, i ^ 2) for i in range(4)])


def along_z(value, pairs):
    return lax.ppermute(value, "band", [(2 * a + c, 2 * b + c) for a, b in pairs for c in range(2)])


def over_corner(value):
    return lax.ppermute(value, "img", [(i, i ^ 3) for i in range(4)])


class Gather:
    def __init__(self, block):
        self.block = block

    def beside(self):
        return [self.block, over_x(self.block), over_y(self.block)]

    def first(self, got=None):
        block, x0, y0 = got or self.beside()
        return [block, x0, y0, over_corner(block), z_shift(block, 4, 1), z_shift(block, 4, 3)]

    def second(self, values):
        block, x0, y0, d0, up, down = values
        across = z_shift(block, 4, 2)
        return values + [over_x(up), over_y(up), over_x(down), over_y(down), across]

    def third(self, values):
        d0, up, down, x1, y1, x3, y3, across = values[3:]
        return values + [over_x(across), over_y(across), z_shift(d0, 4, 2), over_y(x1), over_x(y3)]

    def others(self, values, count):
        return [over_core(value) for value in values[:count]]

    def pieces(self, values, others):
        def ordered(v):
            block, x0, y0, d0, up, down, x1, y1, x3, y3, across, x2, y2, d2, c1, c3 = v
            return [block, x0, y0, d0, up, x1, y1, c1, across, x2, y2, d2, down, x3, y3, c3]

        return ordered(values) + ordered(others)


GATHERED = [(side, k, flip) for side in range(2) for k in (0, 1, 2, 3) for flip in range(4)]


def gather_table(here, block_rows):
    side, k, flip = np.array(GATHERED, np.int32).T
    core, z, img = here.core ^ side, (here.z - k) % 4, here.img ^ flip
    last = (core == 1) & (z == 3) & (img == 3)
    rows = jnp.stack(block_rows(z, 4 * core + img), axis=1).reshape(-1)
    return jnp.concatenate([rows, jnp.argmax(last)[None]]).astype(jnp.int32)


def part(value, axis, index):
    return lax.dynamic_index_in_dim(value, index, axis, keepdims=False)


def planes_of(rows):
    return rows.reshape(2, 2, 2, 352, C)


def add_part(kept, got, plane, axis, index):
    both = part(planes_of(kept)[plane], axis, index).astype(F32)
    return (both + part(planes_of(got)[plane], axis, index).astype(F32)).astype(BF16)


def send_halves(here, kept, got):
    return over_x(add_part(kept, got, 0, 1, 1 - here.x)), over_y(add_part(kept, got, 1, 0, 1 - here.y))


def add_halves(here, kept, got, got_a, got_b):
    a = add_part(kept, got, 0, 1, here.x).astype(F32) + got_a.astype(F32)
    b = add_part(kept, got, 1, 0, here.y).astype(F32) + got_b.astype(F32)
    return a.astype(BF16), b.astype(BF16)


def quarters_to_send(here, a, b):
    return part(a, 0, 1 - here.y), part(b, 0, 1 - here.x)


def send_quarters(a, b):
    return over_y(a), over_x(b)


def add_quarters(here, a, b, got_a, got_b):
    return (
        part(a, 0, here.y).astype(F32) + got_a.astype(F32),
        part(b, 0, here.x).astype(F32) + got_b.astype(F32),
    )


def by_plane(low_planes, first, second):
    halves = [first[:176], second[:176], first[176:], second[176:]]
    return jnp.stack(halves if low_planes else halves[2:] + halves[:2])


def send_planes(here, planes, more=None):
    planes16 = planes.astype(BF16)
    sent = [part(planes16, 0, (here.z + k) % 4) for k in (1, 3, 2)]
    if more is not None:
        sent = [jnp.concatenate([value, more.astype(BF16)], axis=0) for value in sent]
    return [z_shift(value, 4, k) for value, k in zip(sent, (1, 3, 2))]


def add_planes(here, planes, got, more=None):
    total = part(planes, 0, here.z)
    if more is not None:
        total = jnp.concatenate([total, more], axis=0)
    for value in got:
        total = total + value.astype(F32)
    return total


def over_two_planes(value):
    return along_z(value, [(0, 2), (2, 0), (1, 3), (3, 1)])


def sum_over_plane(value):
    value = value + over_core(value)
    value = value + over_x(value)
    return value + over_y(value)


def adam(params, first, second, grad, step_count, rate):
    new_first = 0.5 * first + 0.5 * grad
    new_second = 0.9 * second + 0.1 * grad * grad
    update = (
        rate
        * (new_first / (1.0 - jnp.power(0.5, step_count)))
        / (jnp.sqrt(new_second / (1.0 - jnp.power(0.9, step_count))) + ADAM_EPSILON)
    )
    return update, new_first, new_second


def body(
    x_small,
    x_medium,
    x_large,
    cot_small,
    cot_medium,
    cot_large,
    band_rows,
    params,
    first_moment,
    second_moment,
    step,
    rate,
):
    here = Place()
    n_band, position = here.n_band, here.position
    plan = Plan([x_small.shape, x_medium.shape, x_large.shape], n_band)
    tables = make_tables(plan, band_rows, position)
    half = n_band // 2 * plan.piece
    rows, count = params.shape[0], here.count
    step_count, step_rate = step[0].astype(F32), rate[0]
    last = count - 1
    singles = 22 * C - last * rows

    images, cots = (x_small, x_medium, x_large), (cot_small, cot_medium, cot_large)
    if here.planes:
        shard16 = params.astype(BF16)
        before = lax.ppermute(shard16[rows - count :], AXES, [(o, o + 1) for o in range(last)])

        def aligned(head, shard, size):
            both = jnp.concatenate([head, shard], axis=0)
            return lax.dynamic_slice_in_dim(both, count - here.owner, size, 0)

        gather = Gather(jnp.concatenate([aligned(before, shard16, rows - 1), shard16[singles : singles + 16]], axis=0))
        x_got = to_chips(plan, chip_blocks(plan, position, images))
        values, x_got, band_rows, cots = stage((gather.beside(), x_got, band_rows, cots))
        tables = make_tables(plan, band_rows, position)
        cot_sent = chip_blocks(plan, position, cots)
        table = gather_table(here, lambda z, place: [(8 * z + place) * 22])
        values, x_blocks, cot_sent, tables, table = stage(
            (gather.first(values), to_cores(plan, x_got), cot_sent, tables, table)
        )
        state = (params, first_moment, second_moment)
        far = [lax.dynamic_slice_in_dim(rows_of, 176 - here.owner, 176, 0).astype(BF16) for rows_of in state]
        values, far = stage((gather.second(values), jnp.concatenate(far, axis=1)))
        values, others = stage((gather.third(values), gather.others(values, 4)))
        cot_sent, values = stage((cot_sent, values))
        cot_got = to_chips(plan, cot_sent)
        pieces, parts = gather.pieces(values, others + gather.others(values[4:], 12)), ((0, rows - 1),)
        pieces, x_blocks = stage((pieces, x_blocks))
    else:
        pieces, parts = [lax.all_gather(params.astype(BF16), AXES, axis=0, tiled=True)], ((0, rows),)
        table = jnp.zeros((2,), jnp.int32)
        tables = make_tables(plan, band_rows, position)
        x_blocks = to_cores(plan, to_chips(plan, chip_blocks(plan, position, images)))
        cot_got = to_chips(plan, chip_blocks(plan, position, cots))
    x_img, a1, h1, a2, y, z, q, k, v, stats, small, weights = run_features(
        True, plan, tables, x_blocks, pieces, parts, table
    )
    cot_got, y = stage((cot_got, y))
    cot_blocks = to_cores(plan, cot_got)
    if here.planes:
        cot_blocks, far = stage((cot_blocks, far))
        far = over_two_planes(far)
    out_own, out_oth, dy, dy16, g_proj, sums3 = run_attend_both(
        plan, tables, q, k, v, y, z, cot_blocks, stats, small, weights
    )
    if here.planes:

        def stepped(state, grad):
            update, _, _ = adam(*state, grad, step_count, step_rate)
            return (state[0] - update).astype(BF16)

        dy16, far, out_oth = stage((dy16, far, out_oth))
        out_got = over_core(out_oth)
        kept, sent, early, sums_b2 = run_weight_grad(tables, 1, a2, dy16, g_proj)
        dy16, kept, sent, out_got = stage((dy16, kept, sent, out_got))
        got = over_core(sent)
        out_got = from_chips(plan, merge_cores(plan, position, out_own, out_got))
        dh1, sums_n2 = run_data_grad(tables, 1, dy16, h1, stats, small, weights)
        dh1, kept, got = stage((dh1, kept, got))
        halves = send_halves(here, kept, got)
        high = kept, got
        kept, sent, sums_b1 = run_weight_grad(tables, 0, a1, dh1, early)
        kept, sent, high, halves, out_got = stage((kept, sent, high, halves, out_got))
        got = over_core(sent)
        high = add_halves(here, *high, *halves)
        quarters = send_quarters(*quarters_to_send(here, *high))
        kept, got, high = stage((kept, got, high))
        low = kept, got
        halves = send_halves(here, *low)
        high, quarters, dh1 = stage((high, quarters, dh1))
        high = by_plane(False, *add_quarters(here, *high, *quarters))
        high, dh1, head = stage((high, dh1, [rows_of[rows - count :] for rows_of in state]))
        high_got = send_planes(here, high)
        dx_own, dx_oth, sums_n1 = run_data_grad(
            tables, 0, dh1, x_img, stats, small, weights, dy=dy, half=out_own.shape[0]
        )
        low, halves, high, high_got, sums_n1, head = stage((low, halves, high, high_got, sums_n1, head))
        low = add_halves(here, *low, *halves)
        low, low_sent, sums_n1, head = stage((low, quarters_to_send(here, *low), sums_n1, head))
        quarters = send_quarters(*low_sent)
        before = lax.ppermute(jnp.concatenate(head, axis=1), AXES, [(o, o + 1) for o in range(last)])
        small_rows = jnp.concatenate(
            [sums_n1[0:2], sums_b1[0:1], sums_n2[0:2], sums_b2[0:1], sums3[0:5]], axis=0
        )
        small_sum = sum_over_plane(jnp.pad(small_rows, ((0, 5), (0, 0))))
        low, quarters, small_sum, before = stage((low, quarters, small_sum, before))
        low = by_plane(True, *add_quarters(here, *low, *quarters))
        low_got = send_planes(here, low, small_sum)
        low, low_got, before, far, high, high_got = stage((low, low_got, before, far, high, high_got))
        low, high = add_planes(here, low, low_got, small_sum), add_planes(here, high, high_got)
        low, small_sum = low[:176], low[176:]
        own = [
            aligned(before[:, i * C : (i + 1) * C], rows_of[:176], 176) for i, rows_of in enumerate(state)
        ]
        far = [far[:, i * C : (i + 1) * C].astype(F32) for i in range(3)]
        first_two = here.z < 2
        block = [
            stepped([jnp.where(first_two, a, b) for a, b in zip(own, far)], low),
            stepped([jnp.where(first_two, b, a) for a, b in zip(own, far)], high),
            stepped([rows_of[singles : singles + 16] for rows_of in state], small_sum),
        ]
        gather = Gather(jnp.concatenate(block, axis=0))
        values = stage(gather.first())
        values, others, dx_oth = stage((gather.second(values), gather.others(values, 4), dx_oth))
        values, more, dx_got = stage((gather.third(values), gather.others(values[4:], 6), over_core(dx_oth)))
        others = others + more
        dx_sent = merge_cores(plan, position, dx_own, dx_got)
        pieces = gather.pieces(values, others + gather.others(values[10:], 6))
        pieces, dx_sent = stage((pieces, dx_sent))
        dx_got = from_chips(plan, dx_sent)
        far = over_two_planes(jnp.where(here.z < 2, high, low).astype(BF16))
        table = gather_table(
            here,
            lambda z, place: [
                (8 * (z & 1) + place) * 22 + jnp.where(z < 2, 0, 11),
                (8 * (z | 2) + place) * 22 + jnp.where(z < 2, 11, 0),
            ],
        )
        parts = ((0, 176), (176, 176))
    else:
        out_got = from_chips(plan, merge_cores(plan, position, out_own, over_core(out_oth)))
        g_w2, sums_b2 = run_weight_grad(tables, 1, a2, dy16)
        dh1, sums_n2 = run_data_grad(tables, 1, dy16, h1, stats, small, weights)
        g_w1, sums_b1 = run_weight_grad(tables, 0, a1, dh1)
        dx_own, dx_oth, sums_n1 = run_data_grad(
            tables, 0, dh1, x_img, stats, small, weights, dy=dy, half=out_own.shape[0]
        )
        dx_got = from_chips(plan, merge_cores(plan, position, dx_own, over_core(dx_oth)))
        small_rows = jnp.concatenate(
            [sums_n1[0:2], sums_b1[0:1], sums_n2[0:2], sums_b2[0:1], sums3[0:5]], axis=0
        )
        full = jnp.concatenate([g_w1, g_w2, g_proj, small_rows.astype(BF16)], axis=0)
        full = jnp.pad(full, ((0, rows * count - full.shape[0]), (0, 0)))
        grad = lax.psum_scatter(full, AXES, scatter_dimension=0, tiled=True).astype(F32)
        weight_update, new_first, new_second = adam(
            params, first_moment, second_moment, grad, step_count, step_rate
        )
        pieces = [lax.all_gather((params - weight_update).astype(BF16), AXES, axis=0, tiled=True)]
    again_own, again_oth = run_features(False, plan, tables, x_blocks, pieces, parts, table)
    if here.planes:
        again_own, again_oth, out_got, dx_got, far = stage((again_own, again_oth, out_got, dx_got, far))
    again = from_chips(plan, merge_cores(plan, position, again_own, over_core(again_oth)))
    if here.planes:
        mine = jnp.concatenate([jnp.where(here.z < 2, low, high), far.astype(F32)], axis=0)
        follow = lax.ppermute(mine[:count], AXES, [(o, o - 1) for o in range(1, count)])
        follow, dx_got, out_got = stage((follow, dx_got, out_got))
        follow = jnp.where(here.owner == last, jnp.pad(small_sum, ((0, count - 16), (0, 0))), follow)
        grad = lax.dynamic_slice_in_dim(jnp.concatenate([mine, follow], axis=0), here.owner, rows, 0)
        weight_update, new_first, new_second = adam(
            params, first_moment, second_moment, grad, step_count, step_rate
        )
    first_out = to_bands(plan, position, out_got)
    input_grads = to_bands(plan, position, dx_got)
    second_out = to_bands(plan, position, again)
    return (*first_out, *second_out, *input_grads, weight_update, new_first, new_second)


def solution(mesh):
    image = P("img", "band", None, None)
    shard = P(("band", "img"), None)
    return jax.shard_map(
        body,
        mesh=mesh,
        in_specs=(image,) * 6 + (P(),) + (shard,) * 3 + (P(), P()),
        out_specs=(image,) * 9 + (shard,) * 3,
        check_vma=False,
    )
```

```python
import functools

import jax
import jax.numpy as jnp
import numpy as np
from jax import lax
from jax.experimental import pallas as pl
from jax.experimental.pallas import tpu as pltpu
from jax.sharding import PartitionSpec as P

GROUPS = 32
EPSILON = 1e-05
ADAM_EPSILON = 1e-08
C = 512
AXES = ("band", "img")
VMEM_MARGIN = 6 * 1024 * 1024
VMEM_MOST = 58 * 1024 * 1024
F32, BF16 = jnp.float32, jnp.bfloat16

PIX = 1024
SEG_LINES = ((0, 24), (24, 32))
BUF_LINES = 36


class Plan:
    def __init__(self, shapes, n_band):
        (self.n_s, self.cap_s, self.side_s, _), (self.n_m, self.cap_m, self.side_m, _), (
            self.n_l,
            self.cap_l,
            self.side_l,
            _,
        ) = shapes
        assert (self.side_s, self.side_m, self.side_l) == (16, 24, 32)
        self.n_band = n_band
        self.n_chip = n_band // 2
        self.r_s, self.r_m, self.r_l = (
            self.cap_s * self.side_s,
            self.cap_m * self.side_m,
            self.cap_l * self.side_l,
        )
        holders = [dict() for _ in range(n_band)]
        for i in range(self.n_l):
            holders[2 * i]["l"] = i
        free = [b for b in range(n_band) if "l" not in holders[b]]
        for i in range(self.n_m):
            holders[free[i]]["m"] = i
        spots = [b for b in free if b >= 2 * self.n_l]
        for i in range(self.n_s):
            holders[spots[i]]["s"] = i
        self.holders = holders
        self.sizes = [
            (self.r_l if "l" in h else 0)
            + (self.r_m if "m" in h else 0)
            + (self.r_s if "s" in h else 0)
            for h in holders
        ]
        self.block = max(self.sizes[2 * j] + self.sizes[2 * j + 1] for j in range(self.n_chip))
        self.piece = max(self.sizes)
        self.offs = [0 if b % 2 == 0 else self.piece - self.sizes[b] for b in range(n_band)]
        self.is_l = np.array([int("l" in h) for h in holders], np.int32)
        self.has_m = np.array([int("m" in h) for h in holders], np.int32)
        self.has_s = np.array([int("s" in h) for h in holders], np.int32)
        self.off = np.array(self.offs, np.int32)


def pick(table, index):
    return lax.dynamic_index_in_dim(jnp.asarray(table), index, 0, keepdims=False)


def make_tables(plan, band_rows, position):
    nz = plan.n_chip
    z, core = position // 2, position % 2
    is_l, has_m, has_s, off = (pick(t, position) for t in (plan.is_l, plan.has_m, plan.has_s, plan.off))
    starts = jnp.cumsum(band_rows, axis=1) - band_rows
    zero_in = plan.n_band * plan.piece // 8

    def band_of(member, rows):
        return jnp.sum((starts[member][None, :] <= rows[:, None]).astype(jnp.int32), axis=1) - 1

    def place(member, rows):
        band = band_of(member, rows)
        onehot = band[:, None] == jnp.arange(plan.n_band)[None, :]
        start = jnp.sum(jnp.where(onehot, starts[member][None, :], 0), axis=1)
        k = (z - band // 2) % nz
        pos = jnp.where(band % 2 == core, k, nz + k)
        return pos * plan.piece + off, rows - start

    q = np.arange(128)
    base, r = place(2, jnp.asarray(q // 4, jnp.int32))
    src_l = (base + r * 32) // 8 + jnp.asarray(q % 4, jnp.int32)
    base, r = place(1, jnp.asarray(np.minimum(q // 4, 23), jnp.int32))
    src_m = (base + r * 24) // 8 + jnp.asarray(q % 4, jnp.int32)
    ok_m = jnp.asarray((q < 96) & (q % 4 < 3)) & (has_m == 1)
    line = np.clip((q - 96) // 4, 0, 7)
    base, r = place(0, jnp.asarray(line + 8 * (q % 4 // 2), jnp.int32))
    src_s = (base + has_m * plan.r_m + r * 16) // 8 + jnp.asarray(q % 2, jnp.int32)
    ok_s = jnp.asarray(q >= 96) & (has_s == 1)
    gather = jnp.where(
        is_l == 1, src_l, jnp.where(ok_m, src_m, jnp.where(ok_s, src_s, zero_in))
    ).astype(jnp.int32)

    per = plan.piece // 8
    p, t = np.divmod(np.arange(plan.n_band * per), per)
    k = jnp.asarray(p % nz, jnp.int32)
    c_src = jnp.where(jnp.asarray(p < nz), core, 1 - core)
    band = 2 * ((z - k) % nz) + c_src
    onehot = band[:, None] == jnp.arange(plan.n_band)[None, :]

    def of_band(row):
        return jnp.sum(jnp.where(onehot, row[None, :], 0), axis=1)

    within = jnp.asarray(t * 8, jnp.int32) - off
    wl = jnp.maximum(within, 0)
    r = wl // 32
    ok_l = (within >= 0) & (r < of_band(band_rows[2]))
    out_l = (of_band(starts[2]) + r) * 4 + wl % 32 // 8
    r = wl // 24
    in_m = (has_m == 1) & (wl < plan.r_m)
    ok_m = (within >= 0) & in_m & (r < of_band(band_rows[1]))
    out_m = (of_band(starts[1]) + r) * 4 + wl % 24 // 8
    ws = jnp.maximum(wl - has_m * plan.r_m, 0)
    r = ws // 16
    h = of_band(starts[0]) + r
    ok_s = (within >= 0) & (has_s == 1) & ~in_m & (r < of_band(band_rows[0]))
    out_s = 96 + (h % 8) * 4 + (h // 8) * 2 + ws % 16 // 8
    scatter = jnp.where(
        is_l == 1,
        jnp.where(ok_l, out_l, 128),
        jnp.where(ok_m, out_m, jnp.where(ok_s, out_s, 128)),
    ).astype(jnp.int32)
    flags = jnp.stack(
        [
            is_l,
            jnp.where(is_l == 1, 32, 24 * has_m),
            jnp.where(is_l == 1, 32, 32 * has_s),
            jnp.where(is_l == 1, 0, 16),
            core,
        ]
    ).astype(jnp.int32)
    return gather, scatter, flags


class Scalars:
    def __init__(self, flags):
        self.is_l = flags[0]
        self.lims = (flags[1], flags[2])
        self.split = flags[3]
        self.core = flags[4]
        self.l_f = flags[0].astype(F32)
        large = flags[0] == 1
        self.inv = (
            jnp.where(large, 1.0 / (1024 * 16), 1.0 / (576 * 16)).astype(F32),
            jnp.where(large, 1.0 / (1024 * 16), 1.0 / (256 * 16)).astype(F32),
        )


def dot(a, b):
    return jnp.dot(a, b, preferred_element_type=F32)


def dot_nt(a, b):
    return lax.dot_general(a, b, (((1,), (1,)), ((), ())), preferred_element_type=F32)


def dot_tn(a, b):
    return lax.dot_general(a, b, (((0,), (0,)), ((), ())), preferred_element_type=F32)


def line_rows(line):
    return pl.ds(pl.multiple_of(line * 32, 32), 32)


def line_loop(body, carries, unroll=2):
    results = []
    for seg, (low, high) in enumerate(SEG_LINES):
        results.append(
            lax.fori_loop(
                low, high, lambda line, carry, seg=seg: body(seg, line, carry), carries[seg], unroll=unroll
            )
        )
    return results


def fold(value):
    return value.reshape(4, 8, C).sum(axis=0)


def columns():
    return lax.broadcasted_iota(jnp.int32, (32, C), 0)


def fill_group_matrix(gm_ref):
    row = lax.broadcasted_iota(jnp.int32, (C, C), 0) // (C // GROUPS)
    col = lax.broadcasted_iota(jnp.int32, (C, C), 1) // (C // GROUPS)
    gm_ref[...] = (row == col).astype(F32).astype(BF16)


def group_totals(gm_ref, scal, per_seg):
    stacked = jnp.concatenate(list(per_seg) + [jnp.zeros((8 - len(per_seg), C), F32)], axis=0)
    hi = stacked.astype(BF16)
    rest = stacked - hi.astype(F32)
    mid = rest.astype(BF16)
    low = (rest - mid.astype(F32)).astype(BF16)
    both = dot(jnp.concatenate([hi, mid, low, jnp.zeros((8, C), BF16)], axis=0), gm_ref[...])
    total = both[0:8] + both[8:16] + both[16:24]
    out = []
    for i in range(0, len(per_seg), 2):
        first, second = total[i : i + 1], total[i + 1 : i + 2]
        out.append((first + scal.l_f * second, second + scal.l_f * first))
    return out


def norm_stats(read, gm_ref, scal, sums=None):
    zero = jnp.zeros((8, C), F32)
    if sums is None:
        sums = line_loop(lambda seg, line, acc: acc + fold(read(line)), (zero, zero))
    sums = [s.sum(axis=0, keepdims=True) for s in sums]
    (totals,) = group_totals(gm_ref, scal, sums)
    means = [totals[seg] * scal.inv[seg] for seg in range(2)]
    col = columns()

    def squares(seg, line, acc):
        dev = jnp.where(col < scal.lims[seg], read(line) - means[seg], 0.0)
        return acc + fold(dev * dev)

    sums = line_loop(squares, (zero, zero))
    sums = [s.sum(axis=0, keepdims=True) for s in sums]
    (totals,) = group_totals(gm_ref, scal, sums)
    rstds = [lax.rsqrt(totals[seg] * scal.inv[seg] + EPSILON) for seg in range(2)]
    return means, rstds


def store_shifted(buf_ref, scal, seg, line, value16):
    col = columns()
    value = value16.astype(F32)
    keep_left, keep_right = col != 0, col != 31
    if seg == 1:
        keep_left &= col != scal.split
        keep_right &= col != scal.split - 1
    left = jnp.where(keep_left, pltpu.roll(value, 1, 0), 0.0).astype(BF16)
    right = jnp.where(keep_right, pltpu.roll(value, 31, 0), 0.0).astype(BF16)
    at = line_rows(line + (1 if seg == 0 else 3))
    buf_ref[at, 0:C] = left
    buf_ref[at, C : 2 * C] = value16
    buf_ref[at, 2 * C : 3 * C] = right


def fill_halos(buf_ref, scal):
    zero = jnp.zeros((32, 3 * C), BF16)
    buf_ref[0:32, :] = zero
    buf_ref[25 * 32 : 26 * 32, :] = zero
    buf_ref[26 * 32 : 27 * 32, :] = zero
    buf_ref[35 * 32 : 36 * 32, :] = zero

    @pl.when(scal.is_l == 1)
    def _():
        buf_ref[25 * 32 : 26 * 32, :] = buf_ref[27 * 32 : 28 * 32, :]
        buf_ref[26 * 32 : 27 * 32, :] = buf_ref[24 * 32 : 25 * 32, :]

    @pl.when(scal.is_l == 0)
    def _():
        buf_ref[26 * 32 + 16 : 27 * 32, :] = buf_ref[34 * 32 : 34 * 32 + 16, :]
        buf_ref[35 * 32 : 35 * 32 + 16, :] = buf_ref[27 * 32 + 16 : 28 * 32, :]


def tile_at(tile):
    return pl.ds(pl.multiple_of(tile * 256, 256), 256)


def tile_rows(tile, shift):
    line = 8 * tile + jnp.where(tile == 3, 2, 0) + shift
    return pl.ds(pl.multiple_of(line * 32, 32), 256)


def tile_loop(body):
    def step(tile, carry):
        body(tile)
        return carry

    lax.fori_loop(0, 4, step, 0)


def conv_tiles(buf_ref, w_ref, out_ref):
    def body(tile):
        acc = None
        for shift in range(3):
            term = dot(buf_ref[tile_rows(tile, shift), :], w_ref[shift * 3 * C : (shift + 1) * 3 * C, :])
            acc = term if acc is None else acc + term
        out_ref[tile_at(tile), :] = acc

    tile_loop(body)


def gather_pieces(table_ref, src_ref, dst_ref, count):
    def step(i, carry):
        at = pl.multiple_of(table_ref[i] * 8, 8)
        dst_ref[pl.ds(pl.multiple_of(i * 8, 8), 8), :] = src_ref[pl.ds(at, 8), :]
        return carry

    lax.fori_loop(0, count, step, 0, unroll=4)


def slots_to_image(table_ref, scal, blocks, slots_ref, image_ref):
    piece = (slots_ref.shape[0] - 8) // len(blocks)
    start = pl.multiple_of((blocks[0].shape[0] - piece) * scal.core, 16)
    for i, block in enumerate(blocks):
        slots_ref[i * piece : (i + 1) * piece, :] = block[pl.ds(start, piece), :].astype(F32)
    slots_ref[len(blocks) * piece :, :] = jnp.zeros((8, C), F32)
    gather_pieces(table_ref, slots_ref, image_ref, 128)


def image_to_slots(table_ref, image_ref, slots_ref, own_ref, oth_ref):
    half = own_ref.shape[0]
    gather_pieces(table_ref, image_ref, slots_ref, 2 * half // 8)
    own_ref[...] = slots_ref[0:half, :].astype(BF16)
    oth_ref[...] = slots_ref[half : 2 * half, :].astype(BF16)


def swish_slope(value):
    sigma = jax.nn.sigmoid(value)
    return sigma * (1.0 + value * (1.0 - sigma))


def load_weights(pieces, parts, table, w, small16, sems):
    last = len(parts) * len(pieces)
    if len(pieces) == 1:
        copies = [[pltpu.make_async_copy(pieces[0].at[pl.ds(0, 22 * C)], w, sems.at[0])]]
        copy = pltpu.make_async_copy(pieces[0].at[pl.ds(22 * C, 16)], small16, sems.at[1])
        copy.start()
        copies[0][0].start()
        copy.wait()
    else:
        for i, piece in enumerate(pieces):

            @pl.when(table[last] == i)
            def _():
                pltpu.make_async_copy(
                    piece.at[pl.ds(parts[-1][0] + parts[-1][1], 16)], small16, sems.at[last]
                ).start()

        copies = []
        for p, (start, count) in enumerate(parts):
            copies.append([])
            for i, piece in enumerate(pieces):
                e = i * len(parts) + p
                at = pl.multiple_of(table[e] * 16, 16)
                copy = pltpu.make_async_copy(
                    piece.at[pl.ds(start, count)], w.at[pl.ds(at, count)], sems.at[e]
                )
                copy.start()
                copies[p].append(copy)
        pltpu.make_async_copy(pieces[0].at[pl.ds(0, 16)], small16, sems.at[last]).wait()

    def wait(p):
        if p < len(copies):
            for copy in copies[p]:
                copy.wait()

    return wait


def features_kernel(first, sources, count, parts, *refs):
    if first:
        gather, flags, table = refs[:3]
        blocks, refs = refs[3 : 3 + sources], refs[3 + sources :]
        pieces, refs = refs[:count], refs[count:]
        x_out, a1_out, h1_out, a2_out, y_ref, z_out, q_ref, k_ref, v_ref, stats, small, w_out = refs[:12]
        slots, x_ref, h_ref, z_ref, buf, w, gm, sems, small16, a1, h1, a2, x16, out_sems = refs[12:]
    else:
        scatter, flags, table, x_in, stats = refs[:5]
        pieces, refs = refs[5 : 5 + count], refs[5 + count :]
        own_out, oth_out = refs[:2]
        slots, x_ref, h_ref, z_ref, buf, w, gm, sems, small16, small, y_ref, q_ref, k_ref, v_ref = refs[2:]
    wait_weights = load_weights(pieces, parts, table, w, small16, sems)
    scal = Scalars(flags)
    fill_group_matrix(gm)
    small[...] = small16[...].astype(F32)
    col = columns()
    saves = []

    def save(value, out):
        if first:
            copy = pltpu.make_async_copy(value, out, out_sems.at[len(saves)])
            copy.start()
            saves.append(copy)

    def row(i):
        return small[i : i + 1, :]

    def activate(read, means, rstds, gain, shift, keep):
        def body(seg, line, carry):
            normed = (read(line) - means[seg]) * rstds[seg] * gain + shift
            act = jnp.where(col < scal.lims[seg], normed * jax.nn.sigmoid(normed), 0.0).astype(BF16)
            if keep is not None:
                keep[line_rows(line), :] = act
            store_shifted(buf, scal, seg, line, act)
            return carry

        line_loop(body, (0, 0))
        fill_halos(buf, scal)

    def read_x(line):
        return x_ref[line_rows(line), :]

    if first:
        slots_to_image(gather, scal, blocks, slots, x_ref)
        means1, rstds1 = norm_stats(read_x, gm, scal)

        def keep_x(seg, line, carry):
            x16[line_rows(line), :] = read_x(line).astype(BF16)
            return carry

        line_loop(keep_x, (0, 0))
        save(x16, x_out)
    else:

        def widen_x(seg, line, carry):
            x_ref[line_rows(line), :] = x_in[line_rows(line), :].astype(F32)
            return carry

        line_loop(widen_x, (0, 0))
        means1, rstds1 = [stats[0:1, :], stats[1:2, :]], [stats[2:3, :], stats[3:4, :]]
    activate(read_x, means1, rstds1, row(0), row(1), a1 if first else None)
    if first:
        save(a1, a1_out)
    wait_weights(0)
    if first:
        save(w, w_out)

    conv_tiles(buf, w.at[0 : 9 * C], h_ref)

    def finish_h(seg, line, carry):
        value = jnp.where(col < scal.lims[seg], h_ref[line_rows(line), :] + row(2), 0.0)
        h_ref[line_rows(line), :] = value
        if first:
            h1[line_rows(line), :] = value
        return carry + fold(value)

    zero = jnp.zeros((8, C), F32)

    def read_h(line):
        return h_ref[line_rows(line), :]

    means2, rstds2 = norm_stats(read_h, gm, scal, line_loop(finish_h, (zero, zero)))
    if first:
        save(h1, h1_out)
    activate(read_h, means2, rstds2, row(3), row(4), a2 if first else None)
    if first:
        save(a2, a2_out)
    wait_weights(1)
    conv_tiles(buf, w.at[9 * C : 18 * C], h_ref)

    def finish_y(seg, line, carry):
        value = jnp.where(
            col < scal.lims[seg], read_x(line) + (h_ref[line_rows(line), :] + row(5)), 0.0
        )
        y_ref[line_rows(line), :] = value
        return carry + fold(value)

    def read_y(line):
        return y_ref[line_rows(line), :]

    means3, rstds3 = norm_stats(read_y, gm, scal, line_loop(finish_y, (zero, zero)))

    def third(seg, line, carry):
        normed = (read_y(line) - means3[seg]) * rstds3[seg] * row(6) + row(7)
        z_ref[line_rows(line), :] = jnp.where(col < scal.lims[seg], normed, 0.0).astype(BF16)
        return carry

    line_loop(third, (0, 0))
    if first:
        save(z_ref, z_out)

    def project(tile):
        at = tile_at(tile)
        rows = z_ref[at, :]
        q_ref[at, :] = (dot(rows, w[18 * C : 19 * C, :]) + row(8)).astype(BF16)
        k_ref[at, :] = dot(rows, w[19 * C : 20 * C, :]).astype(BF16)
        v_ref[at, :] = (dot(rows, w[20 * C : 21 * C, :]) + row(9)).astype(BF16)

    tile_loop(project)
    if first:
        for i, pair in enumerate((means1, rstds1, means2, rstds2, means3, rstds3)):
            stats[2 * i : 2 * i + 1, :] = pair[0]
            stats[2 * i + 1 : 2 * i + 2, :] = pair[1]
        stats[12:16, :] = jnp.zeros((4, C), F32)
        for copy in saves:
            copy.wait()
        return
    bias = key_bias(scal)

    def attend(tile):
        at = tile_at(tile)
        prob = probabilities(q_ref[at, :], k_ref, bias(tile)).astype(BF16)
        mixed = dot(prob, v_ref[...]).astype(BF16)
        y_ref[at, :] = y_ref[at, :] + (dot(mixed, w[21 * C : 22 * C, :]) + row(10))

    tile_loop(attend)
    y_ref[PIX : PIX + 8, :] = jnp.zeros((8, C), F32)
    image_to_slots(scatter, y_ref, slots, own_out, oth_out)


def key_bias(scal):
    key = lax.broadcasted_iota(jnp.int32, (1, PIX), 1)
    column = key % 32
    in0 = key < 768
    ok0 = in0 & (column < scal.lims[0])
    ok1 = (~in0) & (column < scal.lims[1])
    large = scal.is_l == 1
    row0 = jnp.where(ok0 | (ok1 & large), 0.0, -1e30).astype(F32)
    row1 = jnp.where(ok1 | (ok0 & large), 0.0, -1e30).astype(F32)
    return lambda tile: jnp.where(tile == 3, row1, row0)


def probabilities(q, k_ref, bias):
    scores = dot_nt(q, k_ref[...]) * (C**-0.5) + bias
    top = jnp.max(scores, axis=1, keepdims=True)
    expo = jnp.exp(scores - top)
    return expo * (1.0 / jnp.sum(expo, axis=1, keepdims=True))


def attend_both_kernel(
    gather,
    scatter,
    flags,
    q,
    k,
    v,
    y,
    z,
    stats,
    small,
    weights,
    *refs,
):
    blocks = refs[:-23]
    own_out, oth_out, dy_out, dy16_out, grads_out, sums_out = refs[-23:-17]
    image, slots, g_ref, o_ref, d_ref, dk_acc, dv_acc, wp, gm, sems = refs[-17:-7]
    loaded = [
        (weights.at[pl.ds(18 * C, 4 * C)], wp),
        (q, refs[-7]),
        (k, refs[-6]),
        (v, refs[-5]),
        (y, refs[-4]),
        (z, refs[-3]),
    ]
    loads = [pltpu.make_async_copy(a, b, sems.at[i]) for i, (a, b) in enumerate(loaded)]
    for load in loads:
        load.start()
    q, k, v, y, z, grads, own_rows = refs[-7:]
    oth_rows = own_rows.at[pl.ds(own_out.shape[0], own_out.shape[0])]
    own_rows = own_rows.at[pl.ds(0, own_out.shape[0])]
    stores = [(own_rows, own_out), (oth_rows, oth_out), (grads, grads_out)]
    stores = [pltpu.make_async_copy(a, b, sems.at[6 + i]) for i, (a, b) in enumerate(stores)]
    scal = Scalars(flags)
    fill_group_matrix(gm)
    bias = key_bias(scal)
    slots_to_image(gather, scal, blocks, slots, g_ref)
    for load in loads[:5]:
        load.wait()
    scaling = C**-0.5
    dk_acc[...] = jnp.zeros(MAP, F32)
    dv_acc[...] = jnp.zeros(MAP, F32)

    def attend(tile):
        at = tile_at(tile)
        q_t = q[at, :]
        prob = probabilities(q_t, k, bias(tile))
        prob16 = prob.astype(BF16)
        mixed = dot(prob16, v[...]).astype(BF16)
        o_ref[at, :] = mixed
        image[at, :] = y[at, :] + (dot(mixed, wp[3 * C : 4 * C, :]) + small[10:11, :])
        d_mixed = dot_nt(g_ref[at, :].astype(BF16), wp[3 * C : 4 * C, :]).astype(BF16)
        d_prob = dot_nt(d_mixed, v[...])
        inner = jnp.sum(prob * d_prob, axis=1, keepdims=True)
        d_score = (prob * (d_prob - inner)).astype(BF16)
        d_ref[at, 0:C] = (scaling * dot(d_score, k[...])).astype(BF16)
        dk_acc[...] += dot_tn(d_score, q_t)
        dv_acc[...] += dot_tn(prob16, d_mixed)

    tile_loop(attend)
    d_ref[:, C : 2 * C] = (scaling * dk_acc[...]).astype(BF16)
    d_ref[:, 2 * C : 3 * C] = dv_acc[...].astype(BF16)
    image[PIX : PIX + 8, :] = jnp.zeros((8, C), F32)
    image_to_slots(scatter, image, slots, own_rows, oth_rows)
    stores[0].start()
    stores[1].start()
    loads[5].wait()
    for part in range(3):
        grads[part * C : (part + 1) * C, :] = dot_tn(z[...], d_ref[:, part * C : (part + 1) * C]).astype(
            BF16
        )
    grads[3 * C : 4 * C, :] = dot_tn(o_ref[...], g_ref[...].astype(BF16)).astype(BF16)
    stores[2].start()
    def back_to_norm(tile):
        at = tile_at(tile)
        acc = dot_nt(d_ref[at, 0:C], wp[0:C, :])
        acc = acc + dot_nt(d_ref[at, C : 2 * C], wp[C : 2 * C, :])
        image[at, :] = acc + dot_nt(d_ref[at, 2 * C : 3 * C], wp[2 * C : 3 * C, :])

    tile_loop(back_to_norm)
    col = columns()
    means = (stats[8:9, :], stats[9:10, :])
    rstds = (stats[10:11, :], stats[11:12, :])
    zero = jnp.zeros((8, C), F32)

    def sums(seg, line, acc):
        at = line_rows(line)
        d_norm = image[at, :]
        unit = (y[at, :] - means[seg]) * rstds[seg]
        d_all = d_ref[at, :].astype(F32)
        return (
            acc[0] + fold(d_norm),
            acc[1] + fold(d_norm * unit),
            acc[2] + fold(d_all[:, 0:C]),
            acc[3] + fold(d_all[:, 2 * C : 3 * C]),
            acc[4] + fold(g_ref[at, :]),
        )

    got = line_loop(sums, ((zero,) * 5, (zero,) * 5), unroll=1)
    got = [[part.sum(axis=0, keepdims=True) for part in seg] for seg in got]
    gain = small[6:7, :]
    ones, cross = group_totals(
        gm, scal, [got[0][0] * gain, got[1][0] * gain, got[0][1] * gain, got[1][1] * gain]
    )
    sums_out[...] = jnp.zeros((16, C), F32)
    for i, part in enumerate((1, 0, 2, 3, 4)):
        sums_out[6 + i : 7 + i, :] = got[0][part] + got[1][part]

    def back(seg, line, carry):
        at = line_rows(line)
        unit = (y[at, :] - means[seg]) * rstds[seg]
        d_in = rstds[seg] * (
            image[at, :] * gain - ones[seg] * scal.inv[seg] - unit * (cross[seg] * scal.inv[seg])
        )
        value = g_ref[at, :] + jnp.where(col < scal.lims[seg], d_in, 0.0)
        dy_out[at, :] = value
        dy16_out[at, :] = value.astype(BF16)
        return carry

    line_loop(back, (0, 0))
    for store in stores:
        store.wait()


def fill_gradient_buffer(buf, scal, grad_ref):
    def body(seg, line, carry):
        store_shifted(buf, scal, seg, line, grad_ref[line_rows(line), :])
        return carry

    line_loop(body, (0, 0))
    fill_halos(buf, scal)


def weight_grad_kernel(conv, split, *refs):
    if not split:
        flags, act, grad, w_out, sums_out, buf, act_t = refs
    else:
        flags, act, grad, more = refs[:4]
        planes, refs = refs[4:8], refs[8:]
        early_out = refs[0] if conv == 1 else None
        sums_out, buf, act_t, rows, sems = refs[conv:]
        kept, sent = planes[:2], planes[2:]
        offset = 2 * C if conv == 1 else 0
        more_at = 9 * C - offset
        load = pltpu.make_async_copy(more, rows.at[pl.ds(more_at, more.shape[0])], sems.at[4])
        load.start()
    scal = Scalars(flags)
    fill_gradient_buffer(buf, scal, grad)
    for tile in range(4):
        at = slice(tile * 256, (tile + 1) * 256)
        act_t[:, at] = act[at, :].T

    def send_out(run):
        plane, core = run // 2, run % 2
        source = rows.at[pl.ds(run * 1408, 1408)]

        @pl.when(scal.core == core)
        def _():
            pltpu.make_async_copy(source, kept[plane], sems.at[run]).start()

        @pl.when(scal.core != core)
        def _():
            pltpu.make_async_copy(source, sent[plane], sems.at[run]).start()

    ready = {0: (3,) if conv == 0 else (2, 3), 1: (2,) if conv == 0 else (1,), 2: (0, 1) if conv == 0 else (0,)}
    for shift in range(3):
        seg0 = slice(shift * 32, shift * 32 + 768)
        seg1 = slice((26 + shift) * 32, (26 + shift) * 32 + 256)
        for part in range(3):
            cols = slice(part * C, (part + 1) * C)
            value = dot(act_t[:, 0:768], buf[seg0, cols]) + dot(act_t[:, 768:1024], buf[seg1, cols])
            tap = 3 * (2 - shift) + (2 - part)
            if not split:
                w_out[tap * C : (tap + 1) * C, :] = value.astype(BF16)
            elif conv == 1 and tap < 2:
                early_out[tap * C : (tap + 1) * C, :] = value.astype(BF16)
            else:
                rows[tap * C - offset : (tap + 1) * C - offset, :] = value.astype(BF16)
        if split:
            if shift == 0:
                load.wait()
            for run in ready[shift]:
                send_out(run)
    zero = jnp.zeros((8, C), F32)
    got = line_loop(
        lambda seg, line, acc: acc + fold(grad[line_rows(line), :].astype(F32)), (zero, zero)
    )
    sums_out[...] = jnp.zeros((16, C), F32)
    sums_out[3 * conv + 2 : 3 * conv + 3, :] = (got[0] + got[1]).sum(axis=0, keepdims=True)
    if split:
        for run in range(4):
            pltpu.make_async_copy(rows.at[pl.ds(run * 1408, 1408)], kept[run // 2], sems.at[run]).wait()


def data_grad_kernel(last, conv, *refs):
    if last:
        scatter, flags, grad, feat, dy, stats, small, weights, own_out, oth_out, sums_out = refs[:11]
        dn, slots, buf, w, gm, sems, feat_v, dy_v = refs[11:]
    else:
        flags, grad, feat, stats, small, weights, grad_out, sums_out = refs[:8]
        dn, buf, w, gm, sems, feat_v = refs[8:]
    copies = [pltpu.make_async_copy(weights.at[pl.ds(conv * 9 * C, 9 * C)], w, sems.at[0])]
    copies.append(pltpu.make_async_copy(feat, feat_v, sems.at[1]))
    if last:
        copies.append(pltpu.make_async_copy(dy, dy_v, sems.at[2]))
        dy = dy_v
    feat = feat_v
    for copy in copies:
        copy.start()
    scal = Scalars(flags)
    fill_group_matrix(gm)
    fill_gradient_buffer(buf, scal, grad)
    copies[0].wait()

    def transposed(tile):
        acc = None
        for shift in range(3):
            for part in range(3):
                tap = 3 * (2 - shift) + (2 - part)
                term = dot_nt(
                    buf[tile_rows(tile, shift), part * C : (part + 1) * C], w[tap * C : (tap + 1) * C, :]
                )
                acc = term if acc is None else acc + term
        dn[tile_at(tile), :] = acc

    tile_loop(transposed)
    for copy in copies[1:]:
        copy.wait()
    base = 4 * conv
    means = (stats[base : base + 1, :], stats[base + 1 : base + 2, :])
    rstds = (stats[base + 2 : base + 3, :], stats[base + 3 : base + 4, :])
    gain, shift_row = small[3 * conv : 3 * conv + 1, :], small[3 * conv + 1 : 3 * conv + 2, :]
    col = columns()
    zero = jnp.zeros((8, C), F32)

    def sums(seg, line, acc):
        at = line_rows(line)
        unit = (feat[at, :].astype(F32) - means[seg]) * rstds[seg]
        value = dn[at, :] * swish_slope(unit * gain + shift_row)
        value = jnp.where(col < scal.lims[seg], value, 0.0)
        dn[at, :] = value
        return (acc[0] + fold(value), acc[1] + fold(value * unit))

    got = line_loop(sums, ((zero, zero), (zero, zero)))
    got = [[part.sum(axis=0, keepdims=True) for part in seg] for seg in got]
    ones, cross = group_totals(
        gm, scal, [got[0][0] * gain, got[1][0] * gain, got[0][1] * gain, got[1][1] * gain]
    )
    sums_out[...] = jnp.zeros((16, C), F32)
    sums_out[3 * conv : 3 * conv + 1, :] = got[0][1] + got[1][1]
    sums_out[3 * conv + 1 : 3 * conv + 2, :] = got[0][0] + got[1][0]

    def back(seg, line, carry):
        at = line_rows(line)
        unit = (feat[at, :].astype(F32) - means[seg]) * rstds[seg]
        value = rstds[seg] * (
            dn[at, :] * gain - ones[seg] * scal.inv[seg] - unit * (cross[seg] * scal.inv[seg])
        )
        value = jnp.where(col < scal.lims[seg], value, 0.0)
        if last:
            dn[at, :] = value + dy[at, :]
        else:
            grad_out[at, :] = value.astype(BF16)
        return carry

    line_loop(back, (0, 0))
    if last:
        dn[PIX : PIX + 8, :] = jnp.zeros((8, C), F32)
        image_to_slots(scatter, dn, slots, own_out, oth_out)


SMEM = pl.BlockSpec(memory_space=pltpu.SMEM)
VMEM = pl.BlockSpec(memory_space=pltpu.VMEM)
HBM = pl.BlockSpec(memory_space=pltpu.HBM)


def call(kernel, name, in_specs, outs, scratch, flops, args, out_specs=None, limit=None):
    moved = sum(int(np.prod(a.shape)) * a.dtype.itemsize for a in args)
    moved += sum(int(np.prod(s)) * jnp.dtype(d).itemsize for s, d in outs)
    out_specs = out_specs or [VMEM] * len(outs)
    held = [(a.shape, a.dtype) for a, spec in zip(args, in_specs) if spec is VMEM]
    held += [out for out, spec in zip(outs, out_specs) if spec is VMEM]
    held += [(s.shape, s.dtype) for s in scratch if s.memory_space == pltpu.VMEM]
    used = sum(int(np.prod(s)) * jnp.dtype(d).itemsize for s, d in held)
    return pl.pallas_call(
        kernel,
        name=name,
        out_shape=[jax.ShapeDtypeStruct(s, d) for s, d in outs],
        in_specs=in_specs,
        out_specs=out_specs,
        scratch_shapes=scratch,
        compiler_params=pltpu.CompilerParams(vmem_limit_bytes=limit or used + VMEM_MARGIN),
        cost_estimate=pl.CostEstimate(flops=int(flops), bytes_accessed=moved, transcendentals=0),
    )(*args)


MAP, SLOT_PAD = (PIX, C), 8
MICROSECOND = 1_100_000_000
BUF = pltpu.VMEM((BUF_LINES * 32, 3 * C), BF16)


def run_features(first, plan, tables, x, pieces, parts, table):
    gather, scatter, flags = tables
    slot_rows = plan.n_band * plan.piece
    count = len(pieces)
    scratch = [
        pltpu.VMEM((slot_rows + SLOT_PAD, C), F32),
        pltpu.VMEM(MAP, F32),
        pltpu.VMEM(MAP, F32),
        pltpu.VMEM(MAP, BF16),
        BUF,
        pltpu.VMEM((22 * C, C), BF16),
        pltpu.VMEM((C, C), BF16),
        pltpu.SemaphoreType.DMA((len(parts) * count + 1,)),
        pltpu.VMEM((16, C), BF16),
    ]
    if first:
        outs = [
            (MAP, BF16),
            (MAP, BF16),
            (MAP, F32),
            (MAP, BF16),
            (MAP, F32),
            (MAP, BF16),
            (MAP, BF16),
            (MAP, BF16),
            (MAP, BF16),
            ((16, C), F32),
            ((16, C), F32),
            ((22 * C, C), BF16),
        ]
        return call(
            functools.partial(features_kernel, True, len(x), count, parts),
            "features_first",
            [SMEM] * 3 + [VMEM] * len(x) + [HBM] * count,
            outs,
            scratch
            + [
                pltpu.VMEM(MAP, BF16),
                pltpu.VMEM(MAP, F32),
                pltpu.VMEM(MAP, BF16),
                pltpu.VMEM(MAP, BF16),
                pltpu.SemaphoreType.DMA((6,)),
            ],
            26 * MICROSECOND,
            (gather, flags, table, *x, *pieces),
            out_specs=[HBM] * 4 + [VMEM, HBM] + [VMEM] * 5 + [HBM],
            limit=VMEM_MOST,
        )
    return call(
        functools.partial(features_kernel, False, 0, count, parts),
        "forward_again",
        [SMEM] * 3 + [VMEM] * 2 + [HBM] * count,
        [((slot_rows // 2, C), BF16)] * 2,
        scratch
        + [
            pltpu.VMEM((16, C), F32),
            pltpu.VMEM((PIX + 8, C), F32),
            pltpu.VMEM(MAP, BF16),
            pltpu.VMEM(MAP, BF16),
            pltpu.VMEM(MAP, BF16),
        ],
        28 * MICROSECOND,
        (scatter, flags, table, *x, *pieces),
        limit=VMEM_MOST,
    )


def run_attend_both(plan, tables, q, k, v, y, z, blocks, stats, small, weights):
    gather, scatter, flags = tables
    slot_rows = plan.n_band * plan.piece
    return call(
        attend_both_kernel,
        "attend_both",
        [SMEM] * 3 + [HBM] * 5 + [VMEM] * 2 + [HBM] + [VMEM] * len(blocks),
        [
            ((slot_rows // 2, C), BF16),
            ((slot_rows // 2, C), BF16),
            (MAP, F32),
            (MAP, BF16),
            ((4 * C, C), BF16),
            ((16, C), F32),
        ],
        [
            pltpu.VMEM((PIX + 8, C), F32),
            pltpu.VMEM((slot_rows + SLOT_PAD, C), F32),
            pltpu.VMEM(MAP, F32),
            pltpu.VMEM(MAP, BF16),
            pltpu.VMEM((PIX, 3 * C), BF16),
            pltpu.VMEM(MAP, F32),
            pltpu.VMEM(MAP, F32),
            pltpu.VMEM((4 * C, C), BF16),
            pltpu.VMEM((C, C), BF16),
            pltpu.SemaphoreType.DMA((9,)),
            pltpu.VMEM(MAP, BF16),
            pltpu.VMEM(MAP, BF16),
            pltpu.VMEM(MAP, BF16),
            pltpu.VMEM(MAP, F32),
            pltpu.VMEM(MAP, BF16),
            pltpu.VMEM((4 * C, C), BF16),
            pltpu.VMEM((slot_rows, C), BF16),
        ],
        24 * MICROSECOND,
        (gather, scatter, flags, q, k, v, y, z, stats, small, weights, *blocks),
        out_specs=[HBM] * 2 + [VMEM] * 2 + [HBM, VMEM],
        limit=VMEM_MOST,
    )


def run_weight_grad(tables, conv, act, grad, more=None):
    scratch = [BUF, pltpu.VMEM((C, PIX), BF16)]
    name = "weight_grad_one" if conv == 0 else "weight_grad_two"
    if more is None:
        return call(
            functools.partial(weight_grad_kernel, conv, False),
            name,
            [SMEM, VMEM, VMEM],
            [((9 * C, C), BF16), ((16, C), F32)],
            scratch,
            9 * MICROSECOND,
            (tables[2], act, grad),
        )
    early = [((2 * C, C), BF16)] if conv == 1 else []
    return call(
        functools.partial(weight_grad_kernel, conv, True),
        name,
        [SMEM, VMEM, VMEM, HBM],
        [((1408, C), BF16)] * 4 + early + [((16, C), F32)],
        scratch + [pltpu.VMEM((5632, C), BF16), pltpu.SemaphoreType.DMA((5,))],
        9 * MICROSECOND,
        (tables[2], act, grad, more),
        out_specs=[HBM] * 4 + [VMEM] * len(early) + [VMEM],
        limit=VMEM_MOST,
    )


def run_data_grad(tables, conv, grad, feat, stats, small, weights, dy=None, half=None):
    last = dy is not None
    scratch = [BUF, pltpu.VMEM((9 * C, C), BF16), pltpu.VMEM((C, C), BF16), pltpu.SemaphoreType.DMA((3,))]
    scratch.append(pltpu.VMEM(MAP, feat.dtype))
    if last:
        outs = [((half, C), BF16)] * 2
        scratch = [pltpu.VMEM((PIX + 8, C), F32), pltpu.VMEM((2 * half, C), F32)] + scratch
        scratch.append(pltpu.VMEM(MAP, F32))
        args = (tables[1], tables[2], grad, feat, dy, stats, small, weights)
        specs = [SMEM, SMEM, VMEM, HBM, HBM, VMEM, VMEM, HBM]
    else:
        outs = [(MAP, BF16)]
        scratch = [pltpu.VMEM(MAP, F32)] + scratch
        args = (tables[2], grad, feat, stats, small, weights)
        specs = [SMEM, VMEM, HBM, VMEM, VMEM, HBM]
    return call(
        functools.partial(data_grad_kernel, last, conv),
        "data_grad_one" if conv == 0 else "data_grad_two",
        specs,
        outs + [((16, C), F32)],
        scratch,
        12 * MICROSECOND,
        args,
        limit=VMEM_MOST,
    )


def z_shift(value, nz, k):
    return lax.ppermute(value, "band", [(2 * z + c, 2 * ((z + k) % nz) + c) for z in range(nz) for c in range(2)])


def core_swap(value, n_band):
    return lax.ppermute(value, "band", [(b, b ^ 1) for b in range(n_band)])


def stage(values):
    return lax.optimization_barrier(values)


def pack_slots(plan, arrays):
    flat = [a.reshape(a.shape[0], -1, C) for a in arrays]
    blocks = []
    for chip in range(plan.n_chip):
        parts = []
        for c in range(2):
            h = plan.holders[2 * chip + c]
            mine = [flat[m][h[name]] for m, name in ((2, "l"), (1, "m"), (0, "s")) if name in h]
            if c == 1:
                used = plan.sizes[2 * chip] + plan.sizes[2 * chip + 1]
                if used < plan.block:
                    parts.append(jnp.zeros((plan.block - used, C), BF16))
            parts += mine
        blocks.append(jnp.concatenate(parts, axis=0))
    return jnp.stack(blocks)


def chip_blocks(plan, position, arrays):
    z, nz = position // 2, plan.n_chip
    sent = pack_slots(plan, arrays)
    return [lax.dynamic_index_in_dim(sent, (z + k) % nz, 0, keepdims=False) for k in range(nz)]


def to_chips(plan, blocks):
    return [blocks[0]] + [z_shift(blocks[k], plan.n_chip, k) for k in range(1, plan.n_chip)]


def to_cores(plan, received):
    return [*received, *[core_swap(block, plan.n_band) for block in received]]


def merge_cores(plan, position, own, got):
    core, nz, slack = position % 2, plan.n_chip, plan.block - plan.piece
    own, got = own.reshape(nz, plan.piece, C), got.reshape(nz, plan.piece, C)
    first, second = jnp.where(core == 0, own, got), jnp.where(core == 0, got, own)
    return jnp.pad(first, ((0, 0), (0, slack), (0, 0))) + jnp.pad(second, ((0, 0), (slack, 0), (0, 0)))


def from_chips(plan, blocks):
    return [blocks[0]] + [z_shift(blocks[k], plan.n_chip, -k) for k in range(1, plan.n_chip)]


def to_bands(plan, position, received):
    z, nz, slack = position // 2, plan.n_chip, plan.block - plan.piece
    received = jnp.stack(received)
    images = [[None] * plan.n_s, [None] * plan.n_m, [None] * plan.n_l]
    for b, h in enumerate(plan.holders):
        chip = b // 2
        if not h:
            continue
        block = lax.dynamic_index_in_dim(received, (chip - z) % nz, 0, keepdims=False)
        at = plan.offs[b] + (slack if b % 2 else 0)
        for member, name, size in ((2, "l", plan.r_l), (1, "m", plan.r_m), (0, "s", plan.r_s)):
            if name in h:
                images[member][h[name]] = block[at : at + size]
                at += size
    sides = (plan.side_s, plan.side_m, plan.side_l)
    return [
        jnp.stack(images[m]).reshape(len(images[m]), -1, sides[m], C) for m in range(3)
    ]


class Place:
    def __init__(self):
        self.n_band, self.n_img = lax.axis_size("band"), lax.axis_size("img")
        self.count = self.n_band * self.n_img
        self.position, self.img = lax.axis_index("band"), lax.axis_index("img")
        self.owner = self.position * self.n_img + self.img
        self.z, self.core = self.position // 2, self.position % 2
        self.y, self.x = self.img // 2, self.img % 2
        self.planes = self.n_band == 8 and self.n_img == 4


def over_core(value):
    return core_swap(value, lax.axis_size("band"))


def over_x(value):
    return lax.ppermute(value, "img", [(i, i ^ 1) for i in range(4)])


def over_y(value):
    return lax.ppermute(value, "img", [(i, i ^ 2) for i in range(4)])


def along_z(value, pairs):
    return lax.ppermute(value, "band", [(2 * a + c, 2 * b + c) for a, b in pairs for c in range(2)])


def over_corner(value):
    return lax.ppermute(value, "img", [(i, i ^ 3) for i in range(4)])


class Gather:
    def __init__(self, block):
        self.block = block

    def beside(self):
        return [self.block, over_x(self.block), over_y(self.block)]

    def first(self, got=None):
        block, x0, y0 = got or self.beside()
        return [block, x0, y0, over_corner(block), z_shift(block, 4, 1), z_shift(block, 4, 3)]

    def second(self, values):
        block, x0, y0, d0, up, down = values
        across = z_shift(block, 4, 2)
        return values + [over_x(up), over_y(up), over_x(down), over_y(down), across]

    def third(self, values):
        d0, up, down, x1, y1, x3, y3, across = values[3:]
        return values + [over_x(across), over_y(across), z_shift(d0, 4, 2), over_y(x1), over_x(y3)]

    def others(self, values, count):
        return [over_core(value) for value in values[:count]]

    def pieces(self, values, others):
        def ordered(v):
            block, x0, y0, d0, up, down, x1, y1, x3, y3, across, x2, y2, d2, c1, c3 = v
            return [block, x0, y0, d0, up, x1, y1, c1, across, x2, y2, d2, down, x3, y3, c3]

        return ordered(values) + ordered(others)


GATHERED = [(side, k, flip) for side in range(2) for k in (0, 1, 2, 3) for flip in range(4)]


def gather_table(here, block_rows):
    side, k, flip = np.array(GATHERED, np.int32).T
    core, z, img = here.core ^ side, (here.z - k) % 4, here.img ^ flip
    last = (core == 1) & (z == 3) & (img == 3)
    rows = jnp.stack(block_rows(z, 4 * core + img), axis=1).reshape(-1)
    return jnp.concatenate([rows, jnp.argmax(last)[None]]).astype(jnp.int32)


def part(value, axis, index):
    return lax.dynamic_index_in_dim(value, index, axis, keepdims=False)


def add_part(kept, got, axis, index):
    both = [part(value.reshape(2, 2, 352, C), axis, index).astype(F32) for value in (kept, got)]
    return (both[0] + both[1]).astype(BF16)


def halves_to_send(here, kept, got):
    return add_part(kept[0], got[0], 1, 1 - here.x), add_part(kept[1], got[1], 0, 1 - here.y)


def send_halves(a, b):
    return over_x(a), over_y(b)


def add_halves(here, kept, got, got_a, got_b):
    a = add_part(kept[0], got[0], 1, here.x).astype(F32) + got_a.astype(F32)
    b = add_part(kept[1], got[1], 0, here.y).astype(F32) + got_b.astype(F32)
    return a.astype(BF16), b.astype(BF16)


def quarters_to_send(here, a, b):
    return part(a, 0, 1 - here.y), part(b, 0, 1 - here.x)


def send_quarters(a, b):
    return over_y(a), over_x(b)


def add_quarters(here, a, b, got_a, got_b):
    return (
        part(a, 0, here.y).astype(F32) + got_a.astype(F32),
        part(b, 0, here.x).astype(F32) + got_b.astype(F32),
    )


def by_plane(low_planes, first, second):
    halves = [first[:176], second[:176], first[176:], second[176:]]
    return jnp.stack(halves if low_planes else halves[2:] + halves[:2])


def send_planes(here, planes, more=None):
    planes16 = planes.astype(BF16)
    sent = [part(planes16, 0, (here.z + k) % 4) for k in (1, 3, 2)]
    if more is not None:
        sent = [jnp.concatenate([value, more.astype(BF16)], axis=0) for value in sent]
    return [z_shift(value, 4, k) for value, k in zip(sent, (1, 3, 2))]


def add_planes(here, planes, got, more=None):
    total = part(planes, 0, here.z)
    if more is not None:
        total = jnp.concatenate([total, more], axis=0)
    for value in got:
        total = total + value.astype(F32)
    return total


def over_two_planes(value):
    return along_z(value, [(0, 2), (2, 0), (1, 3), (3, 1)])


def sum_over_plane(value):
    value = value + over_core(value)
    return (value + over_x(value)) + (over_y(value) + over_corner(value))


def adam(params, first, second, grad, step_count, rate):
    new_first = 0.5 * first + 0.5 * grad
    new_second = 0.9 * second + 0.1 * grad * grad
    update = (
        rate
        * (new_first / (1.0 - jnp.power(0.5, step_count)))
        / (jnp.sqrt(new_second / (1.0 - jnp.power(0.9, step_count))) + ADAM_EPSILON)
    )
    return update, new_first, new_second


def body(
    x_small,
    x_medium,
    x_large,
    cot_small,
    cot_medium,
    cot_large,
    band_rows,
    params,
    first_moment,
    second_moment,
    step,
    rate,
):
    here = Place()
    n_band, position = here.n_band, here.position
    plan = Plan([x_small.shape, x_medium.shape, x_large.shape], n_band)
    tables = make_tables(plan, band_rows, position)
    half = n_band // 2 * plan.piece
    rows, count = params.shape[0], here.count
    step_count, step_rate = step[0].astype(F32), rate[0]
    last = count - 1
    singles = 22 * C - last * rows

    images, cots = (x_small, x_medium, x_large), (cot_small, cot_medium, cot_large)
    if here.planes:
        shard16 = params.astype(BF16)
        before = lax.ppermute(shard16[rows - count :], AXES, [(o, o + 1) for o in range(last)])

        def aligned(head, shard, size):
            both = jnp.concatenate([head, shard], axis=0)
            return lax.dynamic_slice_in_dim(both, count - here.owner, size, 0)

        gather = Gather(jnp.concatenate([aligned(before, shard16, rows - 1), shard16[singles : singles + 16]], axis=0))
        x_got = to_chips(plan, chip_blocks(plan, position, images))
        values, x_got, band_rows, cots = stage((gather.beside(), x_got, band_rows, cots))
        tables = make_tables(plan, band_rows, position)
        cot_sent = chip_blocks(plan, position, cots)
        table = gather_table(here, lambda z, place: [(8 * z + place) * 22])
        values, x_blocks, cot_sent, tables, table = stage(
            (gather.first(values), to_cores(plan, x_got), cot_sent, tables, table)
        )
        state = (params, first_moment, second_moment)
        far = [lax.dynamic_slice_in_dim(rows_of, 176 - here.owner, 176, 0).astype(BF16) for rows_of in state]
        head = jnp.concatenate([rows_of[rows - count :] for rows_of in state], axis=1)
        near = [rows_of[:176] for rows_of in state]
        single_state = [rows_of[singles : singles + 16] for rows_of in state]
        table_again = gather_table(
            here,
            lambda z, place: [
                (8 * (z & 1) + place) * 22 + jnp.where(z < 2, 0, 11),
                (8 * (z | 2) + place) * 22 + jnp.where(z < 2, 11, 0),
            ],
        )
        values, far, head, near, single_state, table_again = stage(
            (gather.second(values), jnp.concatenate(far, axis=1), head, near, single_state, table_again)
        )
        values, others = stage((gather.third(values), gather.others(values, 4)))
        cot_sent, values = stage((cot_sent, values))
        cot_got = to_chips(plan, cot_sent)
        pieces, parts = gather.pieces(values, others + gather.others(values[4:], 12)), ((0, rows - 1),)
        pieces, x_blocks = stage((pieces, x_blocks))
    else:
        pieces, parts = [lax.all_gather(params.astype(BF16), AXES, axis=0, tiled=True)], ((0, rows),)
        table = jnp.zeros((2,), jnp.int32)
        tables = make_tables(plan, band_rows, position)
        x_blocks = to_cores(plan, to_chips(plan, chip_blocks(plan, position, images)))
        cot_got = to_chips(plan, chip_blocks(plan, position, cots))
    x_img, a1, h1, a2, y, z, q, k, v, stats, small, weights = run_features(
        True, plan, tables, x_blocks, pieces, parts, table
    )
    cot_got, y = stage((cot_got, y))
    cot_blocks = to_cores(plan, cot_got)
    if here.planes:
        cot_blocks, far, head = stage((cot_blocks, far, head))
        far = over_two_planes(far)
        before = lax.ppermute(head, AXES, [(o, o + 1) for o in range(last)])
    out_own, out_oth, dy, dy16, g_proj, sums3 = run_attend_both(
        plan, tables, q, k, v, y, z, cot_blocks, stats, small, weights
    )
    if here.planes:

        def stepped(state, grad):
            update, _, _ = adam(*state, grad, step_count, step_rate)
            return (state[0] - update).astype(BF16)

        dy16, far, before, out_oth = stage((dy16, far, before, out_oth))
        out_got = over_core(out_oth)
        *kept, early, sums_b2 = run_weight_grad(tables, 1, a2, dy16, g_proj)
        kept, sent = kept[:2], kept[2:]
        dy16, kept, sent, out_got = stage((dy16, kept, sent, out_got))
        got = [over_core(value) for value in sent]
        out_got = from_chips(plan, merge_cores(plan, position, out_own, out_got))
        dh1, sums_n2 = run_data_grad(tables, 1, dy16, h1, stats, small, weights)
        dh1, kept, got = stage((dh1, kept, got))
        halves = send_halves(*halves_to_send(here, kept, got))
        high = kept, got
        *kept, sums_b1 = run_weight_grad(tables, 0, a1, dh1, early)
        kept, sent = kept[:2], kept[2:]
        kept, sent, high, halves, out_got = stage((kept, sent, high, halves, out_got))
        got = [over_core(value) for value in sent]
        high = add_halves(here, *high, *halves)
        quarters = send_quarters(*quarters_to_send(here, *high))
        low = kept, got
        low, halves, high, quarters, dh1 = stage((low, halves_to_send(here, *low), high, quarters, dh1))
        halves = send_halves(*halves)
        high = by_plane(False, *add_quarters(here, *high, *quarters))
        high, dh1 = stage((high, dh1))
        high_got = send_planes(here, high)
        dx_own, dx_oth, sums_n1 = run_data_grad(
            tables, 0, dh1, x_img, stats, small, weights, dy=dy, half=out_own.shape[0]
        )
        low, halves, high, high_got, sums_n1 = stage((low, halves, high, high_got, sums_n1))
        low = add_halves(here, *low, *halves)
        low, low_sent, sums_n1 = stage((low, quarters_to_send(here, *low), sums_n1))
        quarters = send_quarters(*low_sent)
        small_sum = sum_over_plane(sums_n1 + sums_b1 + sums_n2 + sums_b2 + sums3)
        low, quarters, small_sum = stage((low, quarters, small_sum))
        low = by_plane(True, *add_quarters(here, *low, *quarters))
        low_got = send_planes(here, low, small_sum)
        low, low_got, before, far, high, high_got = stage((low, low_got, before, far, high, high_got))
        low, high = add_planes(here, low, low_got, small_sum), add_planes(here, high, high_got)
        low, small_sum = low[:176], low[176:]
        own = [
            aligned(before[:, i * C : (i + 1) * C], rows_of, 176) for i, rows_of in enumerate(near)
        ]
        far = [far[:, i * C : (i + 1) * C].astype(F32) for i in range(3)]
        first_two = here.z < 2
        block = [
            stepped([jnp.where(first_two, a, b) for a, b in zip(own, far)], low),
            stepped([jnp.where(first_two, b, a) for a, b in zip(own, far)], high),
            stepped(single_state, small_sum),
        ]
        gather = Gather(jnp.concatenate(block, axis=0))
        values, dx_got = stage((gather.first(), over_core(dx_oth)))
        dx_sent = merge_cores(plan, position, dx_own, dx_got)
        values, others, dx_sent, first_out = stage(
            (gather.second(values), gather.others(values, 4), dx_sent, to_bands(plan, position, out_got))
        )
        values, more = stage((gather.third(values), gather.others(values[4:], 6)))
        pieces = gather.pieces(values, others + more + gather.others(values[10:], 6))
        pieces, dx_sent = stage((pieces, dx_sent))
        dx_got = from_chips(plan, dx_sent)
        far = over_two_planes(jnp.where(here.z < 2, high, low).astype(BF16))
        table = table_again
        parts = ((0, 176), (176, 176))
    else:
        out_got = from_chips(plan, merge_cores(plan, position, out_own, over_core(out_oth)))
        g_w2, sums_b2 = run_weight_grad(tables, 1, a2, dy16)
        dh1, sums_n2 = run_data_grad(tables, 1, dy16, h1, stats, small, weights)
        g_w1, sums_b1 = run_weight_grad(tables, 0, a1, dh1)
        dx_own, dx_oth, sums_n1 = run_data_grad(
            tables, 0, dh1, x_img, stats, small, weights, dy=dy, half=out_own.shape[0]
        )
        dx_got = from_chips(plan, merge_cores(plan, position, dx_own, over_core(dx_oth)))
        small_rows = sums_n1 + sums_b1 + sums_n2 + sums_b2 + sums3
        full = jnp.concatenate([g_w1, g_w2, g_proj, small_rows.astype(BF16)], axis=0)
        full = jnp.pad(full, ((0, rows * count - full.shape[0]), (0, 0)))
        grad = lax.psum_scatter(full, AXES, scatter_dimension=0, tiled=True).astype(F32)
        weight_update, new_first, new_second = adam(
            params, first_moment, second_moment, grad, step_count, step_rate
        )
        pieces = [lax.all_gather((params - weight_update).astype(BF16), AXES, axis=0, tiled=True)]
    again_own, again_oth = run_features(False, plan, tables, (x_img, stats), pieces, parts, table)
    if here.planes:
        again_own, again_oth, dx_got, far = stage((again_own, again_oth, dx_got, far))
    again = from_chips(plan, merge_cores(plan, position, again_own, over_core(again_oth)))
    if here.planes:
        mine = jnp.concatenate([jnp.where(here.z < 2, low, high), far.astype(F32)], axis=0)
        follow = lax.ppermute(mine[:count], AXES, [(o, o - 1) for o in range(1, count)])
        follow, dx_got = stage((follow, dx_got))
        follow = jnp.where(here.owner == last, jnp.pad(small_sum, ((0, count - 16), (0, 0))), follow)
        grad = lax.dynamic_slice_in_dim(jnp.concatenate([mine, follow], axis=0), here.owner, rows, 0)
        weight_update, new_first, new_second = adam(
            params, first_moment, second_moment, grad, step_count, step_rate
        )
    else:
        first_out = to_bands(plan, position, out_got)
    input_grads = to_bands(plan, position, dx_got)
    second_out = to_bands(plan, position, again)
    return (*first_out, *second_out, *input_grads, weight_update, new_first, new_second)


def solution(mesh):
    image = P("img", "band", None, None)
    shard = P(("band", "img"), None)
    return jax.shard_map(
        body,
        mesh=mesh,
        in_specs=(image,) * 6 + (P(),) + (shard,) * 3 + (P(), P()),
        out_specs=(image,) * 9 + (shard,) * 3,
        check_vma=False,
    )
```

```python
import functools

import jax
import jax.numpy as jnp
import numpy as np
from jax import lax
from jax.experimental import pallas as pl
from jax.experimental.pallas import tpu as pltpu
from jax.sharding import PartitionSpec as P

GROUPS = 32
EPSILON = 1e-05
ADAM_EPSILON = 1e-08
C = 512
AXES = ("band", "img")
VMEM_MARGIN = 6 * 1024 * 1024
VMEM_MOST = 58 * 1024 * 1024
F32, BF16 = jnp.float32, jnp.bfloat16

PIX = 1024
SEG_LINES = ((0, 24), (24, 32))
BUF_LINES = 36


class Plan:
    def __init__(self, shapes, n_band):
        (self.n_s, self.cap_s, self.side_s, _), (self.n_m, self.cap_m, self.side_m, _), (
            self.n_l,
            self.cap_l,
            self.side_l,
            _,
        ) = shapes
        assert (self.side_s, self.side_m, self.side_l) == (16, 24, 32)
        self.n_band = n_band
        self.n_chip = n_band // 2
        self.r_s, self.r_m, self.r_l = (
            self.cap_s * self.side_s,
            self.cap_m * self.side_m,
            self.cap_l * self.side_l,
        )
        holders = [dict() for _ in range(n_band)]
        for i in range(self.n_l):
            holders[2 * i]["l"] = i
        free = [b for b in range(n_band) if "l" not in holders[b]]
        for i in range(self.n_m):
            holders[free[i]]["m"] = i
        spots = [b for b in free if b >= 2 * self.n_l]
        for i in range(self.n_s):
            holders[spots[i]]["s"] = i
        self.holders = holders
        self.sizes = [
            (self.r_l if "l" in h else 0)
            + (self.r_m if "m" in h else 0)
            + (self.r_s if "s" in h else 0)
            for h in holders
        ]
        self.block = max(self.sizes[2 * j] + self.sizes[2 * j + 1] for j in range(self.n_chip))
        self.piece = max(self.sizes)
        self.offs = [0 if b % 2 == 0 else self.piece - self.sizes[b] for b in range(n_band)]
        self.is_l = np.array([int("l" in h) for h in holders], np.int32)
        self.has_m = np.array([int("m" in h) for h in holders], np.int32)
        self.has_s = np.array([int("s" in h) for h in holders], np.int32)
        self.off = np.array(self.offs, np.int32)


def pick(table, index):
    return lax.dynamic_index_in_dim(jnp.asarray(table), index, 0, keepdims=False)


def make_tables(plan, band_rows, position):
    nz = plan.n_chip
    z, core = position // 2, position % 2
    is_l, has_m, has_s, off = (pick(t, position) for t in (plan.is_l, plan.has_m, plan.has_s, plan.off))
    starts = jnp.cumsum(band_rows, axis=1) - band_rows
    zero_in = plan.n_band * plan.piece // 8

    def band_of(member, rows):
        return jnp.sum((starts[member][None, :] <= rows[:, None]).astype(jnp.int32), axis=1) - 1

    def place(member, rows):
        band = band_of(member, rows)
        onehot = band[:, None] == jnp.arange(plan.n_band)[None, :]
        start = jnp.sum(jnp.where(onehot, starts[member][None, :], 0), axis=1)
        k = (z - band // 2) % nz
        pos = jnp.where(band % 2 == core, k, nz + k)
        return pos * plan.piece + off, rows - start

    q = np.arange(128)
    base, r = place(2, jnp.asarray(q // 4, jnp.int32))
    src_l = (base + r * 32) // 8 + jnp.asarray(q % 4, jnp.int32)
    base, r = place(1, jnp.asarray(np.minimum(q // 4, 23), jnp.int32))
    src_m = (base + r * 24) // 8 + jnp.asarray(q % 4, jnp.int32)
    ok_m = jnp.asarray((q < 96) & (q % 4 < 3)) & (has_m == 1)
    line = np.clip((q - 96) // 4, 0, 7)
    base, r = place(0, jnp.asarray(line + 8 * (q % 4 // 2), jnp.int32))
    src_s = (base + has_m * plan.r_m + r * 16) // 8 + jnp.asarray(q % 2, jnp.int32)
    ok_s = jnp.asarray(q >= 96) & (has_s == 1)
    gather = jnp.where(
        is_l == 1, src_l, jnp.where(ok_m, src_m, jnp.where(ok_s, src_s, zero_in))
    ).astype(jnp.int32)

    per = plan.piece // 8
    p, t = np.divmod(np.arange(plan.n_band * per), per)
    k = jnp.asarray(p % nz, jnp.int32)
    c_src = jnp.where(jnp.asarray(p < nz), core, 1 - core)
    band = 2 * ((z - k) % nz) + c_src
    onehot = band[:, None] == jnp.arange(plan.n_band)[None, :]

    def of_band(row):
        return jnp.sum(jnp.where(onehot, row[None, :], 0), axis=1)

    within = jnp.asarray(t * 8, jnp.int32) - off
    wl = jnp.maximum(within, 0)
    r = wl // 32
    ok_l = (within >= 0) & (r < of_band(band_rows[2]))
    out_l = (of_band(starts[2]) + r) * 4 + wl % 32 // 8
    r = wl // 24
    in_m = (has_m == 1) & (wl < plan.r_m)
    ok_m = (within >= 0) & in_m & (r < of_band(band_rows[1]))
    out_m = (of_band(starts[1]) + r) * 4 + wl % 24 // 8
    ws = jnp.maximum(wl - has_m * plan.r_m, 0)
    r = ws // 16
    h = of_band(starts[0]) + r
    ok_s = (within >= 0) & (has_s == 1) & ~in_m & (r < of_band(band_rows[0]))
    out_s = 96 + (h % 8) * 4 + (h // 8) * 2 + ws % 16 // 8
    scatter = jnp.where(
        is_l == 1,
        jnp.where(ok_l, out_l, 128),
        jnp.where(ok_m, out_m, jnp.where(ok_s, out_s, 128)),
    ).astype(jnp.int32)
    flags = jnp.stack(
        [
            is_l,
            jnp.where(is_l == 1, 32, 24 * has_m),
            jnp.where(is_l == 1, 32, 32 * has_s),
            jnp.where(is_l == 1, 0, 16),
            core,
        ]
    ).astype(jnp.int32)
    return gather, scatter, flags


class Scalars:
    def __init__(self, flags):
        self.is_l = flags[0]
        self.lims = (flags[1], flags[2])
        self.split = flags[3]
        self.core = flags[4]
        self.l_f = flags[0].astype(F32)
        large = flags[0] == 1
        self.inv = (
            jnp.where(large, 1.0 / (1024 * 16), 1.0 / (576 * 16)).astype(F32),
            jnp.where(large, 1.0 / (1024 * 16), 1.0 / (256 * 16)).astype(F32),
        )


def dot(a, b):
    return jnp.dot(a, b, preferred_element_type=F32)


def dot_nt(a, b):
    return lax.dot_general(a, b, (((1,), (1,)), ((), ())), preferred_element_type=F32)


def dot_tn(a, b):
    return lax.dot_general(a, b, (((0,), (0,)), ((), ())), preferred_element_type=F32)


def line_rows(line):
    return pl.ds(pl.multiple_of(line * 32, 32), 32)


def line_loop(body, carries, unroll=2):
    results = []
    for seg, (low, high) in enumerate(SEG_LINES):
        results.append(
            lax.fori_loop(
                low, high, lambda line, carry, seg=seg: body(seg, line, carry), carries[seg], unroll=unroll
            )
        )
    return results


def fold(value):
    return value.reshape(4, 8, C).sum(axis=0)


def columns():
    return lax.broadcasted_iota(jnp.int32, (32, C), 0)


def fill_group_matrix(gm_ref):
    row = lax.broadcasted_iota(jnp.int32, (C, C), 0) // (C // GROUPS)
    col = lax.broadcasted_iota(jnp.int32, (C, C), 1) // (C // GROUPS)
    gm_ref[...] = (row == col).astype(F32).astype(BF16)


def group_totals(gm_ref, scal, per_seg):
    stacked = jnp.concatenate(list(per_seg) + [jnp.zeros((8 - len(per_seg), C), F32)], axis=0)
    hi = stacked.astype(BF16)
    rest = stacked - hi.astype(F32)
    mid = rest.astype(BF16)
    low = (rest - mid.astype(F32)).astype(BF16)
    both = dot(jnp.concatenate([hi, mid, low, jnp.zeros((8, C), BF16)], axis=0), gm_ref[...])
    total = both[0:8] + both[8:16] + both[16:24]
    out = []
    for i in range(0, len(per_seg), 2):
        first, second = total[i : i + 1], total[i + 1 : i + 2]
        out.append((first + scal.l_f * second, second + scal.l_f * first))
    return out


def norm_stats(read, gm_ref, scal, sums=None):
    zero = jnp.zeros((8, C), F32)
    if sums is None:
        sums = line_loop(lambda seg, line, acc: acc + fold(read(line)), (zero, zero))
    sums = [s.sum(axis=0, keepdims=True) for s in sums]
    (totals,) = group_totals(gm_ref, scal, sums)
    means = [totals[seg] * scal.inv[seg] for seg in range(2)]
    col = columns()

    def squares(seg, line, acc):
        dev = jnp.where(col < scal.lims[seg], read(line) - means[seg], 0.0)
        return acc + fold(dev * dev)

    sums = line_loop(squares, (zero, zero))
    sums = [s.sum(axis=0, keepdims=True) for s in sums]
    (totals,) = group_totals(gm_ref, scal, sums)
    rstds = [lax.rsqrt(totals[seg] * scal.inv[seg] + EPSILON) for seg in range(2)]
    return means, rstds


def store_shifted(buf_ref, scal, seg, line, value16):
    col = columns()
    value = value16.astype(F32)
    keep_left, keep_right = col != 0, col != 31
    if seg == 1:
        keep_left &= col != scal.split
        keep_right &= col != scal.split - 1
    left = jnp.where(keep_left, pltpu.roll(value, 1, 0), 0.0).astype(BF16)
    right = jnp.where(keep_right, pltpu.roll(value, 31, 0), 0.0).astype(BF16)
    at = line_rows(line + (1 if seg == 0 else 3))
    buf_ref[at, 0:C] = left
    buf_ref[at, C : 2 * C] = value16
    buf_ref[at, 2 * C : 3 * C] = right


def fill_halos(buf_ref, scal):
    zero = jnp.zeros((32, 3 * C), BF16)
    buf_ref[0:32, :] = zero
    buf_ref[25 * 32 : 26 * 32, :] = zero
    buf_ref[26 * 32 : 27 * 32, :] = zero
    buf_ref[35 * 32 : 36 * 32, :] = zero

    @pl.when(scal.is_l == 1)
    def _():
        buf_ref[25 * 32 : 26 * 32, :] = buf_ref[27 * 32 : 28 * 32, :]
        buf_ref[26 * 32 : 27 * 32, :] = buf_ref[24 * 32 : 25 * 32, :]

    @pl.when(scal.is_l == 0)
    def _():
        buf_ref[26 * 32 + 16 : 27 * 32, :] = buf_ref[34 * 32 : 34 * 32 + 16, :]
        buf_ref[35 * 32 : 35 * 32 + 16, :] = buf_ref[27 * 32 + 16 : 28 * 32, :]


def tile_at(tile):
    return pl.ds(pl.multiple_of(tile * 256, 256), 256)


def tile_rows(tile, shift):
    line = 8 * tile + jnp.where(tile == 3, 2, 0) + shift
    return pl.ds(pl.multiple_of(line * 32, 32), 256)


def tile_loop(body):
    def step(tile, carry):
        body(tile)
        return carry

    lax.fori_loop(0, 4, step, 0, unroll=2)


def conv_tiles(buf_ref, w_ref, out_ref):
    def body(tile):
        acc = None
        for shift in range(3):
            term = dot(buf_ref[tile_rows(tile, shift), :], w_ref[shift * 3 * C : (shift + 1) * 3 * C, :])
            acc = term if acc is None else acc + term
        out_ref[tile_at(tile), :] = acc

    tile_loop(body)


def gather_pieces(table_ref, src_ref, dst_ref, count):
    def step(i, carry):
        at = pl.multiple_of(table_ref[i] * 8, 8)
        dst_ref[pl.ds(pl.multiple_of(i * 8, 8), 8), :] = src_ref[pl.ds(at, 8), :]
        return carry

    lax.fori_loop(0, count, step, 0, unroll=4)


def slots_to_image(table_ref, scal, blocks, slots_ref, image_ref):
    piece = (slots_ref.shape[0] - 8) // len(blocks)
    start = pl.multiple_of((blocks[0].shape[0] - piece) * scal.core, 16)
    for i, block in enumerate(blocks):
        slots_ref[i * piece : (i + 1) * piece, :] = block[pl.ds(start, piece), :].astype(F32)
    slots_ref[len(blocks) * piece :, :] = jnp.zeros((8, C), F32)
    gather_pieces(table_ref, slots_ref, image_ref, 128)


def image_to_slots(table_ref, image_ref, slots_ref, own_ref, oth_ref):
    half = own_ref.shape[0]
    gather_pieces(table_ref, image_ref, slots_ref, 2 * half // 8)
    own_ref[...] = slots_ref[0:half, :].astype(BF16)
    oth_ref[...] = slots_ref[half : 2 * half, :].astype(BF16)


def swish_slope(value):
    sigma = jax.nn.sigmoid(value)
    return sigma * (1.0 + value * (1.0 - sigma))


def load_weights(pieces, parts, table, w, small16, sems):
    last = len(parts) * len(pieces)
    if len(pieces) == 1:
        copies = [[pltpu.make_async_copy(pieces[0].at[pl.ds(0, 22 * C)], w, sems.at[0])]]
        copy = pltpu.make_async_copy(pieces[0].at[pl.ds(22 * C, 16)], small16, sems.at[1])
        copy.start()
        copies[0][0].start()
        copy.wait()
    else:
        for i, piece in enumerate(pieces):

            @pl.when(table[last] == i)
            def _():
                pltpu.make_async_copy(
                    piece.at[pl.ds(parts[-1][0] + parts[-1][1], 16)], small16, sems.at[last]
                ).start()

        copies = []
        for p, (start, count) in enumerate(parts):
            copies.append([])
            for i, piece in enumerate(pieces):
                e = i * len(parts) + p
                at = pl.multiple_of(table[e] * 16, 16)
                copy = pltpu.make_async_copy(
                    piece.at[pl.ds(start, count)], w.at[pl.ds(at, count)], sems.at[e]
                )
                copy.start()
                copies[p].append(copy)
        pltpu.make_async_copy(pieces[0].at[pl.ds(0, 16)], small16, sems.at[last]).wait()

    def wait(p):
        if p < len(copies):
            for copy in copies[p]:
                copy.wait()

    return wait


def features_kernel(first, sources, count, parts, *refs):
    if first:
        gather, flags, table = refs[:3]
        blocks, refs = refs[3 : 3 + sources], refs[3 + sources :]
        pieces, refs = refs[:count], refs[count:]
        x_out, a1_out, h1_out, a2_out, y_ref, z_out, q_ref, k_ref, v_ref, stats, small, w_out = refs[:12]
        slots, x_ref, h_ref, z_ref, buf, w, gm, sems, small16, a1, h1, a2, x16, out_sems = refs[12:]
    else:
        scatter, flags, table, x_in, stats = refs[:5]
        pieces, refs = refs[5 : 5 + count], refs[5 + count :]
        own_out, oth_out = refs[:2]
        slots, x_ref, h_ref, z_ref, buf, w, gm, sems, small16, small, y_ref, q_ref, k_ref, v_ref = refs[2:]
    wait_weights = load_weights(pieces, parts, table, w, small16, sems)
    scal = Scalars(flags)
    fill_group_matrix(gm)
    small[...] = small16[...].astype(F32)
    col = columns()
    saves = []

    def save(value, out):
        if first:
            copy = pltpu.make_async_copy(value, out, out_sems.at[len(saves)])
            copy.start()
            saves.append(copy)

    def row(i):
        return small[i : i + 1, :]

    def activate(read, means, rstds, gain, shift, keep):
        def body(seg, line, carry):
            normed = (read(line) - means[seg]) * rstds[seg] * gain + shift
            act = jnp.where(col < scal.lims[seg], normed * jax.nn.sigmoid(normed), 0.0).astype(BF16)
            if keep is not None:
                keep[line_rows(line), :] = act
            store_shifted(buf, scal, seg, line, act)
            return carry

        line_loop(body, (0, 0))
        fill_halos(buf, scal)

    def read_x(line):
        return x_ref[line_rows(line), :]

    if first:
        slots_to_image(gather, scal, blocks, slots, x_ref)
        means1, rstds1 = norm_stats(read_x, gm, scal)

        def keep_x(seg, line, carry):
            x16[line_rows(line), :] = read_x(line).astype(BF16)
            return carry

        line_loop(keep_x, (0, 0))
        save(x16, x_out)
    else:

        def widen_x(seg, line, carry):
            x_ref[line_rows(line), :] = x_in[line_rows(line), :].astype(F32)
            return carry

        line_loop(widen_x, (0, 0))
        means1, rstds1 = [stats[0:1, :], stats[1:2, :]], [stats[2:3, :], stats[3:4, :]]
    activate(read_x, means1, rstds1, row(0), row(1), a1 if first else None)
    if first:
        save(a1, a1_out)
    wait_weights(0)
    if first:
        save(w, w_out)

    conv_tiles(buf, w.at[0 : 9 * C], h_ref)

    def finish_h(seg, line, carry):
        value = jnp.where(col < scal.lims[seg], h_ref[line_rows(line), :] + row(2), 0.0)
        h_ref[line_rows(line), :] = value
        if first:
            h1[line_rows(line), :] = value
        return carry + fold(value)

    zero = jnp.zeros((8, C), F32)

    def read_h(line):
        return h_ref[line_rows(line), :]

    means2, rstds2 = norm_stats(read_h, gm, scal, line_loop(finish_h, (zero, zero)))
    if first:
        save(h1, h1_out)
    activate(read_h, means2, rstds2, row(3), row(4), a2 if first else None)
    if first:
        save(a2, a2_out)
    wait_weights(1)
    conv_tiles(buf, w.at[9 * C : 18 * C], h_ref)

    def finish_y(seg, line, carry):
        value = jnp.where(
            col < scal.lims[seg], read_x(line) + (h_ref[line_rows(line), :] + row(5)), 0.0
        )
        y_ref[line_rows(line), :] = value
        return carry + fold(value)

    def read_y(line):
        return y_ref[line_rows(line), :]

    means3, rstds3 = norm_stats(read_y, gm, scal, line_loop(finish_y, (zero, zero)))

    def third(seg, line, carry):
        normed = (read_y(line) - means3[seg]) * rstds3[seg] * row(6) + row(7)
        z_ref[line_rows(line), :] = jnp.where(col < scal.lims[seg], normed, 0.0).astype(BF16)
        return carry

    line_loop(third, (0, 0))
    if first:
        save(z_ref, z_out)

    def project(tile):
        at = tile_at(tile)
        rows = z_ref[at, :]
        q_ref[at, :] = (dot(rows, w[18 * C : 19 * C, :]) + row(8)).astype(BF16)
        k_ref[at, :] = dot(rows, w[19 * C : 20 * C, :]).astype(BF16)
        v_ref[at, :] = (dot(rows, w[20 * C : 21 * C, :]) + row(9)).astype(BF16)

    tile_loop(project)
    if first:
        for i, pair in enumerate((means1, rstds1, means2, rstds2, means3, rstds3)):
            stats[2 * i : 2 * i + 1, :] = pair[0]
            stats[2 * i + 1 : 2 * i + 2, :] = pair[1]
        stats[12:16, :] = jnp.zeros((4, C), F32)
        for copy in saves:
            copy.wait()
        return
    bias = key_bias(scal)

    def attend(tile):
        at = tile_at(tile)
        prob = probabilities(q_ref[at, :], k_ref, bias(tile)).astype(BF16)
        mixed = dot(prob, v_ref[...]).astype(BF16)
        y_ref[at, :] = y_ref[at, :] + (dot(mixed, w[21 * C : 22 * C, :]) + row(10))

    tile_loop(attend)
    y_ref[PIX : PIX + 8, :] = jnp.zeros((8, C), F32)
    image_to_slots(scatter, y_ref, slots, own_out, oth_out)


def key_bias(scal):
    key = lax.broadcasted_iota(jnp.int32, (1, PIX), 1)
    column = key % 32
    in0 = key < 768
    ok0 = in0 & (column < scal.lims[0])
    ok1 = (~in0) & (column < scal.lims[1])
    large = scal.is_l == 1
    row0 = jnp.where(ok0 | (ok1 & large), 0.0, -1e30).astype(F32)
    row1 = jnp.where(ok1 | (ok0 & large), 0.0, -1e30).astype(F32)
    return lambda tile: jnp.where(tile == 3, row1, row0)


def probabilities(q, k_ref, bias):
    scores = dot_nt(q, k_ref[...]) * (C**-0.5) + bias
    top = jnp.max(scores, axis=1, keepdims=True)
    expo = jnp.exp(scores - top)
    return expo * (1.0 / jnp.sum(expo, axis=1, keepdims=True))


def attend_both_kernel(
    gather,
    scatter,
    flags,
    q,
    k,
    v,
    y,
    z,
    stats,
    small,
    weights,
    *refs,
):
    blocks = refs[:-23]
    own_out, oth_out, dy_out, dy16_out, grads_out, sums_out = refs[-23:-17]
    image, slots, g_ref, o_ref, d_ref, dk_acc, dv_acc, wp, gm, sems = refs[-17:-7]
    loaded = [
        (weights.at[pl.ds(18 * C, 4 * C)], wp),
        (q, refs[-7]),
        (k, refs[-6]),
        (v, refs[-5]),
        (y, refs[-4]),
        (z, refs[-3]),
    ]
    loads = [pltpu.make_async_copy(a, b, sems.at[i]) for i, (a, b) in enumerate(loaded)]
    for load in loads:
        load.start()
    q, k, v, y, z, grads, own_rows = refs[-7:]
    oth_rows = own_rows.at[pl.ds(own_out.shape[0], own_out.shape[0])]
    own_rows = own_rows.at[pl.ds(0, own_out.shape[0])]
    stores = [(own_rows, own_out), (oth_rows, oth_out), (grads, grads_out)]
    stores = [pltpu.make_async_copy(a, b, sems.at[6 + i]) for i, (a, b) in enumerate(stores)]
    scal = Scalars(flags)
    fill_group_matrix(gm)
    bias = key_bias(scal)
    slots_to_image(gather, scal, blocks, slots, g_ref)
    for load in loads[:5]:
        load.wait()
    scaling = C**-0.5
    dk_acc[...] = jnp.zeros(MAP, F32)
    dv_acc[...] = jnp.zeros(MAP, F32)

    def attend(tile):
        at = tile_at(tile)
        q_t = q[at, :]
        prob = probabilities(q_t, k, bias(tile))
        prob16 = prob.astype(BF16)
        mixed = dot(prob16, v[...]).astype(BF16)
        o_ref[at, :] = mixed
        image[at, :] = y[at, :] + (dot(mixed, wp[3 * C : 4 * C, :]) + small[10:11, :])
        d_mixed = dot_nt(g_ref[at, :].astype(BF16), wp[3 * C : 4 * C, :]).astype(BF16)
        d_prob = dot_nt(d_mixed, v[...])
        inner = jnp.sum(prob * d_prob, axis=1, keepdims=True)
        d_score = (prob * (d_prob - inner)).astype(BF16)
        d_ref[at, 0:C] = (scaling * dot(d_score, k[...])).astype(BF16)
        dk_acc[...] += dot_tn(d_score, q_t)
        dv_acc[...] += dot_tn(prob16, d_mixed)

    tile_loop(attend)
    d_ref[:, C : 2 * C] = (scaling * dk_acc[...]).astype(BF16)
    d_ref[:, 2 * C : 3 * C] = dv_acc[...].astype(BF16)
    image[PIX : PIX + 8, :] = jnp.zeros((8, C), F32)
    image_to_slots(scatter, image, slots, own_rows, oth_rows)
    stores[0].start()
    stores[1].start()
    loads[5].wait()
    for part in range(3):
        grads[part * C : (part + 1) * C, :] = dot_tn(z[...], d_ref[:, part * C : (part + 1) * C]).astype(
            BF16
        )
    grads[3 * C : 4 * C, :] = dot_tn(o_ref[...], g_ref[...].astype(BF16)).astype(BF16)
    stores[2].start()
    def back_to_norm(tile):
        at = tile_at(tile)
        acc = dot_nt(d_ref[at, 0:C], wp[0:C, :])
        acc = acc + dot_nt(d_ref[at, C : 2 * C], wp[C : 2 * C, :])
        image[at, :] = acc + dot_nt(d_ref[at, 2 * C : 3 * C], wp[2 * C : 3 * C, :])

    tile_loop(back_to_norm)
    col = columns()
    means = (stats[8:9, :], stats[9:10, :])
    rstds = (stats[10:11, :], stats[11:12, :])
    zero = jnp.zeros((8, C), F32)

    def sums(seg, line, acc):
        at = line_rows(line)
        d_norm = image[at, :]
        unit = (y[at, :] - means[seg]) * rstds[seg]
        d_all = d_ref[at, :].astype(F32)
        return (
            acc[0] + fold(d_norm),
            acc[1] + fold(d_norm * unit),
            acc[2] + fold(d_all[:, 0:C]),
            acc[3] + fold(d_all[:, 2 * C : 3 * C]),
            acc[4] + fold(g_ref[at, :]),
        )

    got = line_loop(sums, ((zero,) * 5, (zero,) * 5), unroll=1)
    got = [[part.sum(axis=0, keepdims=True) for part in seg] for seg in got]
    gain = small[6:7, :]
    ones, cross = group_totals(
        gm, scal, [got[0][0] * gain, got[1][0] * gain, got[0][1] * gain, got[1][1] * gain]
    )
    sums_out[...] = jnp.zeros((16, C), F32)
    for i, part in enumerate((1, 0, 2, 3, 4)):
        sums_out[6 + i : 7 + i, :] = got[0][part] + got[1][part]

    def back(seg, line, carry):
        at = line_rows(line)
        unit = (y[at, :] - means[seg]) * rstds[seg]
        d_in = rstds[seg] * (
            image[at, :] * gain - ones[seg] * scal.inv[seg] - unit * (cross[seg] * scal.inv[seg])
        )
        value = g_ref[at, :] + jnp.where(col < scal.lims[seg], d_in, 0.0)
        dy_out[at, :] = value
        dy16_out[at, :] = value.astype(BF16)
        return carry

    line_loop(back, (0, 0))
    for store in stores:
        store.wait()


def fill_gradient_buffer(buf, scal, grad_ref):
    def body(seg, line, carry):
        store_shifted(buf, scal, seg, line, grad_ref[line_rows(line), :])
        return carry

    line_loop(body, (0, 0))
    fill_halos(buf, scal)


def weight_grad_kernel(conv, split, *refs):
    if not split:
        flags, act, grad, w_out, sums_out, buf, act_t = refs
    else:
        flags, act, grad, more = refs[:4]
        planes, refs = refs[4:8], refs[8:]
        early_out = refs[0] if conv == 1 else None
        sums_out, buf, act_t, rows, sems = refs[conv:]
        kept, sent = planes[:2], planes[2:]
        offset = 2 * C if conv == 1 else 0
        more_at = 9 * C - offset
        load = pltpu.make_async_copy(more, rows.at[pl.ds(more_at, more.shape[0])], sems.at[4])
        load.start()
    scal = Scalars(flags)
    fill_gradient_buffer(buf, scal, grad)
    for tile in range(4):
        at = slice(tile * 256, (tile + 1) * 256)
        act_t[:, at] = act[at, :].T

    def send_out(run):
        plane, core = run // 2, run % 2
        source = rows.at[pl.ds(run * 1408, 1408)]

        @pl.when(scal.core == core)
        def _():
            pltpu.make_async_copy(source, kept[plane], sems.at[run]).start()

        @pl.when(scal.core != core)
        def _():
            pltpu.make_async_copy(source, sent[plane], sems.at[run]).start()

    ready = {0: (3,) if conv == 0 else (2, 3), 1: (2,) if conv == 0 else (1,), 2: (0, 1) if conv == 0 else (0,)}
    for shift in range(3):
        seg0 = slice(shift * 32, shift * 32 + 768)
        seg1 = slice((26 + shift) * 32, (26 + shift) * 32 + 256)
        for part in range(3):
            cols = slice(part * C, (part + 1) * C)
            value = dot(act_t[:, 0:768], buf[seg0, cols]) + dot(act_t[:, 768:1024], buf[seg1, cols])
            tap = 3 * (2 - shift) + (2 - part)
            if not split:
                w_out[tap * C : (tap + 1) * C, :] = value.astype(BF16)
            elif conv == 1 and tap < 2:
                early_out[tap * C : (tap + 1) * C, :] = value.astype(BF16)
            else:
                rows[tap * C - offset : (tap + 1) * C - offset, :] = value.astype(BF16)
        if split:
            if shift == 0:
                load.wait()
            for run in ready[shift]:
                send_out(run)
    zero = jnp.zeros((8, C), F32)
    got = line_loop(
        lambda seg, line, acc: acc + fold(grad[line_rows(line), :].astype(F32)), (zero, zero)
    )
    sums_out[...] = jnp.zeros((16, C), F32)
    sums_out[3 * conv + 2 : 3 * conv + 3, :] = (got[0] + got[1]).sum(axis=0, keepdims=True)
    if split:
        for run in range(4):
            pltpu.make_async_copy(rows.at[pl.ds(run * 1408, 1408)], kept[run // 2], sems.at[run]).wait()


def data_grad_kernel(last, conv, *refs):
    if last:
        scatter, flags, grad, feat, dy, stats, small, weights, own_out, oth_out, sums_out = refs[:11]
        dn, slots, buf, w, gm, sems, feat_v, dy_v = refs[11:]
    else:
        flags, grad, feat, stats, small, weights, grad_out, sums_out = refs[:8]
        dn, buf, w, gm, sems, feat_v = refs[8:]
    copies = [pltpu.make_async_copy(weights.at[pl.ds(conv * 9 * C, 9 * C)], w, sems.at[0])]
    copies.append(pltpu.make_async_copy(feat, feat_v, sems.at[1]))
    if last:
        copies.append(pltpu.make_async_copy(dy, dy_v, sems.at[2]))
        dy = dy_v
    feat = feat_v
    for copy in copies:
        copy.start()
    scal = Scalars(flags)
    fill_group_matrix(gm)
    fill_gradient_buffer(buf, scal, grad)
    copies[0].wait()

    def transposed(tile):
        acc = None
        for shift in range(3):
            for part in range(3):
                tap = 3 * (2 - shift) + (2 - part)
                term = dot_nt(
                    buf[tile_rows(tile, shift), part * C : (part + 1) * C], w[tap * C : (tap + 1) * C, :]
                )
                acc = term if acc is None else acc + term
        dn[tile_at(tile), :] = acc

    tile_loop(transposed)
    for copy in copies[1:]:
        copy.wait()
    base = 4 * conv
    means = (stats[base : base + 1, :], stats[base + 1 : base + 2, :])
    rstds = (stats[base + 2 : base + 3, :], stats[base + 3 : base + 4, :])
    gain, shift_row = small[3 * conv : 3 * conv + 1, :], small[3 * conv + 1 : 3 * conv + 2, :]
    col = columns()
    zero = jnp.zeros((8, C), F32)

    def sums(seg, line, acc):
        at = line_rows(line)
        unit = (feat[at, :].astype(F32) - means[seg]) * rstds[seg]
        value = dn[at, :] * swish_slope(unit * gain + shift_row)
        value = jnp.where(col < scal.lims[seg], value, 0.0)
        dn[at, :] = value
        return (acc[0] + fold(value), acc[1] + fold(value * unit))

    got = line_loop(sums, ((zero, zero), (zero, zero)))
    got = [[part.sum(axis=0, keepdims=True) for part in seg] for seg in got]
    ones, cross = group_totals(
        gm, scal, [got[0][0] * gain, got[1][0] * gain, got[0][1] * gain, got[1][1] * gain]
    )
    sums_out[...] = jnp.zeros((16, C), F32)
    sums_out[3 * conv : 3 * conv + 1, :] = got[0][1] + got[1][1]
    sums_out[3 * conv + 1 : 3 * conv + 2, :] = got[0][0] + got[1][0]

    def back(seg, line, carry):
        at = line_rows(line)
        unit = (feat[at, :].astype(F32) - means[seg]) * rstds[seg]
        value = rstds[seg] * (
            dn[at, :] * gain - ones[seg] * scal.inv[seg] - unit * (cross[seg] * scal.inv[seg])
        )
        value = jnp.where(col < scal.lims[seg], value, 0.0)
        if last:
            dn[at, :] = value + dy[at, :]
        else:
            grad_out[at, :] = value.astype(BF16)
        return carry

    line_loop(back, (0, 0))
    if last:
        dn[PIX : PIX + 8, :] = jnp.zeros((8, C), F32)
        image_to_slots(scatter, dn, slots, own_out, oth_out)


SMEM = pl.BlockSpec(memory_space=pltpu.SMEM)
VMEM = pl.BlockSpec(memory_space=pltpu.VMEM)
HBM = pl.BlockSpec(memory_space=pltpu.HBM)


def call(kernel, name, in_specs, outs, scratch, flops, args, out_specs=None, limit=None):
    moved = sum(int(np.prod(a.shape)) * a.dtype.itemsize for a in args)
    moved += sum(int(np.prod(s)) * jnp.dtype(d).itemsize for s, d in outs)
    out_specs = out_specs or [VMEM] * len(outs)
    held = [(a.shape, a.dtype) for a, spec in zip(args, in_specs) if spec is VMEM]
    held += [out for out, spec in zip(outs, out_specs) if spec is VMEM]
    held += [(s.shape, s.dtype) for s in scratch if s.memory_space == pltpu.VMEM]
    used = sum(int(np.prod(s)) * jnp.dtype(d).itemsize for s, d in held)
    return pl.pallas_call(
        kernel,
        name=name,
        out_shape=[jax.ShapeDtypeStruct(s, d) for s, d in outs],
        in_specs=in_specs,
        out_specs=out_specs,
        scratch_shapes=scratch,
        compiler_params=pltpu.CompilerParams(vmem_limit_bytes=limit or used + VMEM_MARGIN),
        cost_estimate=pl.CostEstimate(flops=int(flops), bytes_accessed=moved, transcendentals=0),
    )(*args)


MAP, SLOT_PAD = (PIX, C), 8
MICROSECOND = 1_100_000_000
BUF = pltpu.VMEM((BUF_LINES * 32, 3 * C), BF16)


def run_features(first, plan, tables, x, pieces, parts, table):
    gather, scatter, flags = tables
    slot_rows = plan.n_band * plan.piece
    count = len(pieces)
    scratch = [
        pltpu.VMEM((slot_rows + SLOT_PAD, C), F32),
        pltpu.VMEM(MAP, F32),
        pltpu.VMEM(MAP, F32),
        pltpu.VMEM(MAP, BF16),
        BUF,
        pltpu.VMEM((22 * C, C), BF16),
        pltpu.VMEM((C, C), BF16),
        pltpu.SemaphoreType.DMA((len(parts) * count + 1,)),
        pltpu.VMEM((16, C), BF16),
    ]
    if first:
        outs = [
            (MAP, BF16),
            (MAP, BF16),
            (MAP, F32),
            (MAP, BF16),
            (MAP, F32),
            (MAP, BF16),
            (MAP, BF16),
            (MAP, BF16),
            (MAP, BF16),
            ((16, C), F32),
            ((16, C), F32),
            ((22 * C, C), BF16),
        ]
        return call(
            functools.partial(features_kernel, True, len(x), count, parts),
            "features_first",
            [SMEM] * 3 + [VMEM] * len(x) + [HBM] * count,
            outs,
            scratch
            + [
                pltpu.VMEM(MAP, BF16),
                pltpu.VMEM(MAP, F32),
                pltpu.VMEM(MAP, BF16),
                pltpu.VMEM(MAP, BF16),
                pltpu.SemaphoreType.DMA((6,)),
            ],
            26 * MICROSECOND,
            (gather, flags, table, *x, *pieces),
            out_specs=[HBM] * 4 + [VMEM, HBM] + [VMEM] * 5 + [HBM],
            limit=VMEM_MOST,
        )
    return call(
        functools.partial(features_kernel, False, 0, count, parts),
        "forward_again",
        [SMEM] * 3 + [VMEM] * 2 + [HBM] * count,
        [((slot_rows // 2, C), BF16)] * 2,
        scratch
        + [
            pltpu.VMEM((16, C), F32),
            pltpu.VMEM((PIX + 8, C), F32),
            pltpu.VMEM(MAP, BF16),
            pltpu.VMEM(MAP, BF16),
            pltpu.VMEM(MAP, BF16),
        ],
        28 * MICROSECOND,
        (scatter, flags, table, *x, *pieces),
        limit=VMEM_MOST,
    )


def run_attend_both(plan, tables, q, k, v, y, z, blocks, stats, small, weights):
    gather, scatter, flags = tables
    slot_rows = plan.n_band * plan.piece
    return call(
        attend_both_kernel,
        "attend_both",
        [SMEM] * 3 + [HBM] * 5 + [VMEM] * 2 + [HBM] + [VMEM] * len(blocks),
        [
            ((slot_rows // 2, C), BF16),
            ((slot_rows // 2, C), BF16),
            (MAP, F32),
            (MAP, BF16),
            ((4 * C, C), BF16),
            ((16, C), F32),
        ],
        [
            pltpu.VMEM((PIX + 8, C), F32),
            pltpu.VMEM((slot_rows + SLOT_PAD, C), F32),
            pltpu.VMEM(MAP, F32),
            pltpu.VMEM(MAP, BF16),
            pltpu.VMEM((PIX, 3 * C), BF16),
            pltpu.VMEM(MAP, F32),
            pltpu.VMEM(MAP, F32),
            pltpu.VMEM((4 * C, C), BF16),
            pltpu.VMEM((C, C), BF16),
            pltpu.SemaphoreType.DMA((9,)),
            pltpu.VMEM(MAP, BF16),
            pltpu.VMEM(MAP, BF16),
            pltpu.VMEM(MAP, BF16),
            pltpu.VMEM(MAP, F32),
            pltpu.VMEM(MAP, BF16),
            pltpu.VMEM((4 * C, C), BF16),
            pltpu.VMEM((slot_rows, C), BF16),
        ],
        24 * MICROSECOND,
        (gather, scatter, flags, q, k, v, y, z, stats, small, weights, *blocks),
        out_specs=[HBM] * 2 + [VMEM] * 2 + [HBM, VMEM],
        limit=VMEM_MOST,
    )


def run_weight_grad(tables, conv, act, grad, more=None):
    scratch = [BUF, pltpu.VMEM((C, PIX), BF16)]
    name = "weight_grad_one" if conv == 0 else "weight_grad_two"
    if more is None:
        return call(
            functools.partial(weight_grad_kernel, conv, False),
            name,
            [SMEM, VMEM, VMEM],
            [((9 * C, C), BF16), ((16, C), F32)],
            scratch,
            9 * MICROSECOND,
            (tables[2], act, grad),
        )
    early = [((2 * C, C), BF16)] if conv == 1 else []
    return call(
        functools.partial(weight_grad_kernel, conv, True),
        name,
        [SMEM, VMEM, VMEM, HBM],
        [((1408, C), BF16)] * 4 + early + [((16, C), F32)],
        scratch + [pltpu.VMEM((5632, C), BF16), pltpu.SemaphoreType.DMA((5,))],
        9 * MICROSECOND,
        (tables[2], act, grad, more),
        out_specs=[HBM] * 4 + [VMEM] * len(early) + [VMEM],
        limit=VMEM_MOST,
    )


def run_data_grad(tables, conv, grad, feat, stats, small, weights, dy=None, half=None):
    last = dy is not None
    scratch = [BUF, pltpu.VMEM((9 * C, C), BF16), pltpu.VMEM((C, C), BF16), pltpu.SemaphoreType.DMA((3,))]
    scratch.append(pltpu.VMEM(MAP, feat.dtype))
    if last:
        outs = [((half, C), BF16)] * 2
        scratch = [pltpu.VMEM((PIX + 8, C), F32), pltpu.VMEM((2 * half, C), F32)] + scratch
        scratch.append(pltpu.VMEM(MAP, F32))
        args = (tables[1], tables[2], grad, feat, dy, stats, small, weights)
        specs = [SMEM, SMEM, VMEM, HBM, HBM, VMEM, VMEM, HBM]
    else:
        outs = [(MAP, BF16)]
        scratch = [pltpu.VMEM(MAP, F32)] + scratch
        args = (tables[2], grad, feat, stats, small, weights)
        specs = [SMEM, VMEM, HBM, VMEM, VMEM, HBM]
    return call(
        functools.partial(data_grad_kernel, last, conv),
        "data_grad_one" if conv == 0 else "data_grad_two",
        specs,
        outs + [((16, C), F32)],
        scratch,
        12 * MICROSECOND,
        args,
        limit=VMEM_MOST,
    )


def z_shift(value, nz, k):
    return lax.ppermute(value, "band", [(2 * z + c, 2 * ((z + k) % nz) + c) for z in range(nz) for c in range(2)])


def core_swap(value, n_band):
    return lax.ppermute(value, "band", [(b, b ^ 1) for b in range(n_band)])


def stage(values):
    return lax.optimization_barrier(values)


def pack_slots(plan, arrays):
    flat = [a.reshape(a.shape[0], -1, C) for a in arrays]
    blocks = []
    for chip in range(plan.n_chip):
        parts = []
        for c in range(2):
            h = plan.holders[2 * chip + c]
            mine = [flat[m][h[name]] for m, name in ((2, "l"), (1, "m"), (0, "s")) if name in h]
            if c == 1:
                used = plan.sizes[2 * chip] + plan.sizes[2 * chip + 1]
                if used < plan.block:
                    parts.append(jnp.zeros((plan.block - used, C), BF16))
            parts += mine
        blocks.append(jnp.concatenate(parts, axis=0))
    return jnp.stack(blocks)


def chip_blocks(plan, position, arrays):
    z, nz = position // 2, plan.n_chip
    sent = pack_slots(plan, arrays)
    return [lax.dynamic_index_in_dim(sent, (z + k) % nz, 0, keepdims=False) for k in range(nz)]


def to_chips(plan, blocks):
    return [blocks[0]] + [z_shift(blocks[k], plan.n_chip, k) for k in range(1, plan.n_chip)]


def to_cores(plan, received):
    return [*received, *[core_swap(block, plan.n_band) for block in received]]


def merge_cores(plan, position, own, got):
    core, nz, slack = position % 2, plan.n_chip, plan.block - plan.piece
    own, got = own.reshape(nz, plan.piece, C), got.reshape(nz, plan.piece, C)
    first, second = jnp.where(core == 0, own, got), jnp.where(core == 0, got, own)
    return jnp.pad(first, ((0, 0), (0, slack), (0, 0))) + jnp.pad(second, ((0, 0), (slack, 0), (0, 0)))


def from_chips(plan, blocks):
    return [blocks[0]] + [z_shift(blocks[k], plan.n_chip, -k) for k in range(1, plan.n_chip)]


def to_bands(plan, position, received):
    z, nz, slack = position // 2, plan.n_chip, plan.block - plan.piece
    received = jnp.stack(received)
    images = [[None] * plan.n_s, [None] * plan.n_m, [None] * plan.n_l]
    for b, h in enumerate(plan.holders):
        chip = b // 2
        if not h:
            continue
        block = lax.dynamic_index_in_dim(received, (chip - z) % nz, 0, keepdims=False)
        at = plan.offs[b] + (slack if b % 2 else 0)
        for member, name, size in ((2, "l", plan.r_l), (1, "m", plan.r_m), (0, "s", plan.r_s)):
            if name in h:
                images[member][h[name]] = block[at : at + size]
                at += size
    sides = (plan.side_s, plan.side_m, plan.side_l)
    return [
        jnp.stack(images[m]).reshape(len(images[m]), -1, sides[m], C) for m in range(3)
    ]


class Place:
    def __init__(self):
        self.n_band, self.n_img = lax.axis_size("band"), lax.axis_size("img")
        self.count = self.n_band * self.n_img
        self.position, self.img = lax.axis_index("band"), lax.axis_index("img")
        self.owner = self.position * self.n_img + self.img
        self.z, self.core = self.position // 2, self.position % 2
        self.y, self.x = self.img // 2, self.img % 2
        self.planes = self.n_band == 8 and self.n_img == 4


def over_core(value):
    return core_swap(value, lax.axis_size("band"))


def over_x(value):
    return lax.ppermute(value, "img", [(i, i ^ 1) for i in range(4)])


def over_y(value):
    return lax.ppermute(value, "img", [(i, i ^ 2) for i in range(4)])


def along_z(value, pairs):
    return lax.ppermute(value, "band", [(2 * a + c, 2 * b + c) for a, b in pairs for c in range(2)])


def over_corner(value):
    return lax.ppermute(value, "img", [(i, i ^ 3) for i in range(4)])


class Gather:
    def __init__(self, block):
        self.block = block

    def beside(self):
        return [self.block, over_x(self.block), over_y(self.block)]

    def first(self, got=None):
        block, x0, y0 = got or self.beside()
        return [block, x0, y0, over_corner(block), z_shift(block, 4, 1), z_shift(block, 4, 3)]

    def second(self, values):
        block, x0, y0, d0, up, down = values
        across = z_shift(block, 4, 2)
        return values + [over_x(up), over_y(up), over_x(down), over_y(down), across]

    def third(self, values):
        d0, up, down, x1, y1, x3, y3, across = values[3:]
        return values + [over_x(across), over_y(across), z_shift(d0, 4, 2), over_y(x1), over_x(y3)]

    def others(self, values, count):
        return [over_core(value) for value in values[:count]]

    def pieces(self, values, others):
        def ordered(v):
            block, x0, y0, d0, up, down, x1, y1, x3, y3, across, x2, y2, d2, c1, c3 = v
            return [block, x0, y0, d0, up, x1, y1, c1, across, x2, y2, d2, down, x3, y3, c3]

        return ordered(values) + ordered(others)


GATHERED = [(side, k, flip) for side in range(2) for k in (0, 1, 2, 3) for flip in range(4)]


def gather_table(here, core, block_rows):
    side, k, flip = np.array(GATHERED, np.int32).T
    core, z, img = core ^ side, (here.z - k) % 4, here.img ^ flip
    last = (core == 1) & (z == 3) & (img == 3)
    rows = jnp.stack(block_rows(z, 4 * core + img), axis=1).reshape(-1)
    return jnp.concatenate([rows, jnp.argmax(last)[None]]).astype(jnp.int32)


def part(value, axis, index):
    return lax.dynamic_index_in_dim(value, index, axis, keepdims=False)


def add_part(kept, got, axis, index):
    both = [part(value.reshape(2, 2, 352, C), axis, index) for value in (kept, got)]
    return both[0] + both[1]


def halves_to_send(here, kept, got):
    return add_part(kept[0], got[0], 1, 1 - here.x), add_part(kept[1], got[1], 0, 1 - here.y)


def send_halves(a, b):
    return over_x(a), over_y(b)


def add_halves(here, kept, got, got_a, got_b):
    a = add_part(kept[0], got[0], 1, here.x) + got_a
    b = add_part(kept[1], got[1], 0, here.y) + got_b
    return a, b


def quarters_to_send(here, a, b):
    return part(a, 0, 1 - here.y), part(b, 0, 1 - here.x)


def send_quarters(a, b):
    return over_y(a), over_x(b)


def add_quarters(here, a, b, got_a, got_b):
    return (
        part(a, 0, here.y).astype(F32) + got_a.astype(F32),
        part(b, 0, here.x).astype(F32) + got_b.astype(F32),
    )


def by_plane(low_planes, first, second):
    halves = [first[:176], second[:176], first[176:], second[176:]]
    return jnp.stack(halves if low_planes else halves[2:] + halves[:2])


def send_planes(here, planes, more=None):
    planes16 = planes.astype(BF16)
    sent = [part(planes16, 0, (here.z + k) % 4) for k in (1, 3, 2)]
    if more is not None:
        sent = [jnp.concatenate([value, more.astype(BF16)], axis=0) for value in sent]
    return [z_shift(value, 4, k) for value, k in zip(sent, (1, 3, 2))]


def add_planes(here, planes, got, more=None):
    total = part(planes, 0, here.z)
    if more is not None:
        total = jnp.concatenate([total, more], axis=0)
    for value in got:
        total = total + value.astype(F32)
    return total


def over_two_planes(value):
    return along_z(value, [(0, 2), (2, 0), (1, 3), (3, 1)])


def sum_over_img(value):
    return (value + over_x(value)) + (over_y(value) + over_corner(value))


def adam(params, first, second, grad, step_count, rate):
    new_first = 0.5 * first + 0.5 * grad
    new_second = 0.9 * second + 0.1 * grad * grad
    update = (
        rate
        * (new_first / (1.0 - jnp.power(0.5, step_count)))
        / (jnp.sqrt(new_second / (1.0 - jnp.power(0.9, step_count))) + ADAM_EPSILON)
    )
    return update, new_first, new_second


def body(
    x_small,
    x_medium,
    x_large,
    cot_small,
    cot_medium,
    cot_large,
    band_rows,
    params,
    first_moment,
    second_moment,
    step,
    rate,
):
    here = Place()
    n_band, position = here.n_band, here.position
    plan = Plan([x_small.shape, x_medium.shape, x_large.shape], n_band)
    tables = make_tables(plan, band_rows, position)
    half = n_band // 2 * plan.piece
    rows, count = params.shape[0], here.count
    step_count, step_rate = step[0].astype(F32), rate[0]
    last = count - 1
    singles = 22 * C - last * rows

    images, cots = (x_small, x_medium, x_large), (cot_small, cot_medium, cot_large)
    if here.planes:
        shard16 = params.astype(BF16)
        before = lax.ppermute(shard16[rows - count :], AXES, [(o, o + 1) for o in range(last)])

        def aligned(head, shard, size):
            both = jnp.concatenate([head, shard], axis=0)
            return lax.dynamic_slice_in_dim(both, count - here.owner, size, 0)

        gather = Gather(jnp.concatenate([aligned(before, shard16, rows - 1), shard16[singles : singles + 16]], axis=0))
        x_got = to_chips(plan, chip_blocks(plan, position, images))
        values = gather.beside()
        values[1], later, core, band_rows = stage((values[1], position, here.core, band_rows))
        tables = make_tables(plan, band_rows, later)
        values, x_got, tables, core, cots, params, first_moment, second_moment = stage(
            (values, x_got, tables, core, cots, params, first_moment, second_moment)
        )
        values = gather.first(values)
        values[3], core, later, cots = stage((values[3], core, position, cots))
        cot_sent = chip_blocks(plan, later, cots)
        table = gather_table(here, core, lambda z, place: [(8 * z + place) * 22])
        values, x_blocks, cot_sent, table = stage((values, to_cores(plan, x_got), cot_sent, table))
        values = gather.second(values)
        values[6], params, first_moment, second_moment, later = stage(
            (values[6], params, first_moment, second_moment, here.owner)
        )
        state = (params, first_moment, second_moment)
        far = [lax.dynamic_slice_in_dim(rows_of, 176 - later, 176, 0).astype(BF16) for rows_of in state]
        head = jnp.concatenate([rows_of[rows - count :] for rows_of in state], axis=1)
        near = [rows_of[:176] for rows_of in state]
        single_state = [rows_of[singles : singles + 16] for rows_of in state]
        table_again = gather_table(
            here,
            core,
            lambda z, place: [
                (8 * (z & 1) + place) * 22 + jnp.where(z < 2, 0, 11),
                (8 * (z | 2) + place) * 22 + jnp.where(z < 2, 11, 0),
            ],
        )
        values, others, far, head, near, single_state, table_again = stage(
            (
                values,
                gather.others(values, 4),
                jnp.concatenate(far, axis=1),
                head,
                near,
                single_state,
                table_again,
            )
        )
        values, more = stage((gather.third(values), gather.others(values[4:], 6)))
        cot_sent, values = stage((cot_sent, values))
        cot_got = to_chips(plan, cot_sent)
        pieces, parts = gather.pieces(values, others + more + gather.others(values[10:], 6)), ((0, rows - 1),)
        pieces, x_blocks = stage((pieces, x_blocks))
    else:
        pieces, parts = [lax.all_gather(params.astype(BF16), AXES, axis=0, tiled=True)], ((0, rows),)
        table = jnp.zeros((2,), jnp.int32)
        tables = make_tables(plan, band_rows, position)
        x_blocks = to_cores(plan, to_chips(plan, chip_blocks(plan, position, images)))
        cot_got = to_chips(plan, chip_blocks(plan, position, cots))
    x_img, a1, h1, a2, y, z, q, k, v, stats, small, weights = run_features(
        True, plan, tables, x_blocks, pieces, parts, table
    )
    cot_got, y = stage((cot_got, y))
    cot_blocks = to_cores(plan, cot_got)
    if here.planes:
        cot_blocks, far, head = stage((cot_blocks, far, head))
        far = over_two_planes(far)
        before = lax.ppermute(head, AXES, [(o, o + 1) for o in range(last)])
    out_own, out_oth, dy, dy16, g_proj, sums3 = run_attend_both(
        plan, tables, q, k, v, y, z, cot_blocks, stats, small, weights
    )
    if here.planes:

        def stepped(state, grad):
            update, _, _ = adam(*state, grad, step_count, step_rate)
            return (state[0] - update).astype(BF16)

        dy16, far, before, out_oth = stage((dy16, far, before, out_oth))
        out_got = over_core(out_oth)
        *kept, early, sums_b2 = run_weight_grad(tables, 1, a2, dy16, g_proj)
        kept, sent = kept[:2], kept[2:]
        dy16, kept, sent, out_got = stage((dy16, kept, sent, out_got))
        got = [over_core(value) for value in sent]
        out_got = from_chips(plan, merge_cores(plan, position, out_own, out_got))
        dy16, kept, got, halves = stage((dy16, kept, got, halves_to_send(here, kept, got)))
        halves = send_halves(*halves)
        dh1, sums_n2 = run_data_grad(tables, 1, dy16, h1, stats, small, weights)
        dh1, kept, got, halves = stage((dh1, kept, got, halves))
        high = kept, got
        *kept, sums_b1 = run_weight_grad(tables, 0, a1, dh1, early)
        kept, sent = kept[:2], kept[2:]
        kept, sent, high, halves, out_got = stage((kept, sent, high, halves, out_got))
        got = [over_core(value) for value in sent]
        high = add_halves(here, *high, *halves)
        quarters = send_quarters(*quarters_to_send(here, *high))
        low = kept, got
        low, halves, high, quarters, dh1 = stage((low, halves_to_send(here, *low), high, quarters, dh1))
        halves = send_halves(*halves)
        high = by_plane(False, *add_quarters(here, *high, *quarters))
        high, dh1 = stage((high, dh1))
        high_got = send_planes(here, high)
        dx_own, dx_oth, sums_n1 = run_data_grad(
            tables, 0, dh1, x_img, stats, small, weights, dy=dy, half=out_own.shape[0]
        )
        low, halves, high, high_got, sums_n1 = stage((low, halves, high, high_got, sums_n1))
        low = add_halves(here, *low, *halves)
        sums = sums_n1 + sums_b1 + sums_n2 + sums_b2 + sums3
        low, low_sent, sums = stage((low, quarters_to_send(here, *low), sums + over_core(sums)))
        quarters = send_quarters(*low_sent)
        small_sum = sum_over_img(sums)
        low, quarters, small_sum = stage((low, quarters, small_sum))
        low = by_plane(True, *add_quarters(here, *low, *quarters))
        low_got = send_planes(here, low, small_sum)
        low, low_got, before, far, high, high_got = stage((low, low_got, before, far, high, high_got))
        low, high = add_planes(here, low, low_got, small_sum), add_planes(here, high, high_got)
        low, small_sum = low[:176], low[176:]
        own = [
            aligned(before[:, i * C : (i + 1) * C], rows_of, 176) for i, rows_of in enumerate(near)
        ]
        far = [far[:, i * C : (i + 1) * C].astype(F32) for i in range(3)]
        first_two = here.z < 2
        block = [
            stepped([jnp.where(first_two, a, b) for a, b in zip(own, far)], low),
            stepped([jnp.where(first_two, b, a) for a, b in zip(own, far)], high),
            stepped(single_state, small_sum),
        ]
        gather = Gather(jnp.concatenate(block, axis=0))
        values, dx_got = stage((gather.first(), over_core(dx_oth)))
        dx_sent = merge_cores(plan, position, dx_own, dx_got)
        values, others, dx_sent, first_out = stage(
            (gather.second(values), gather.others(values, 4), dx_sent, to_bands(plan, position, out_got))
        )
        values, more = stage((gather.third(values), gather.others(values[4:], 6)))
        pieces = gather.pieces(values, others + more + gather.others(values[10:], 6))
        pieces, dx_sent = stage((pieces, dx_sent))
        dx_got = from_chips(plan, dx_sent)
        far = over_two_planes(jnp.where(here.z < 2, high, low).astype(BF16))
        table = table_again
        parts = ((0, 176), (176, 176))
    else:
        out_got = from_chips(plan, merge_cores(plan, position, out_own, over_core(out_oth)))
        g_w2, sums_b2 = run_weight_grad(tables, 1, a2, dy16)
        dh1, sums_n2 = run_data_grad(tables, 1, dy16, h1, stats, small, weights)
        g_w1, sums_b1 = run_weight_grad(tables, 0, a1, dh1)
        dx_own, dx_oth, sums_n1 = run_data_grad(
            tables, 0, dh1, x_img, stats, small, weights, dy=dy, half=out_own.shape[0]
        )
        dx_got = from_chips(plan, merge_cores(plan, position, dx_own, over_core(dx_oth)))
        small_rows = sums_n1 + sums_b1 + sums_n2 + sums_b2 + sums3
        full = jnp.concatenate([g_w1, g_w2, g_proj, small_rows.astype(BF16)], axis=0)
        full = jnp.pad(full, ((0, rows * count - full.shape[0]), (0, 0)))
        grad = lax.psum_scatter(full, AXES, scatter_dimension=0, tiled=True).astype(F32)
        weight_update, new_first, new_second = adam(
            params, first_moment, second_moment, grad, step_count, step_rate
        )
        pieces = [lax.all_gather((params - weight_update).astype(BF16), AXES, axis=0, tiled=True)]
    again_own, again_oth = run_features(False, plan, tables, (x_img, stats), pieces, parts, table)
    if here.planes:
        again_own, again_oth, dx_got, far = stage((again_own, again_oth, dx_got, far))
    again = from_chips(plan, merge_cores(plan, position, again_own, over_core(again_oth)))
    if here.planes:
        mine = jnp.concatenate([jnp.where(here.z < 2, low, high), far.astype(F32)], axis=0)
        follow = lax.ppermute(mine[:count], AXES, [(o, o - 1) for o in range(1, count)])
        follow, dx_got = stage((follow, dx_got))
        follow = jnp.where(here.owner == last, jnp.pad(small_sum, ((0, count - 16), (0, 0))), follow)
        grad = lax.dynamic_slice_in_dim(jnp.concatenate([mine, follow], axis=0), here.owner, rows, 0)
        weight_update, new_first, new_second = adam(
            params, first_moment, second_moment, grad, step_count, step_rate
        )
    else:
        first_out = to_bands(plan, position, out_got)
    input_grads = to_bands(plan, position, dx_got)
    second_out = to_bands(plan, position, again)
    return (*first_out, *second_out, *input_grads, weight_update, new_first, new_second)


def solution(mesh):
    image = P("img", "band", None, None)
    shard = P(("band", "img"), None)
    return jax.shard_map(
        body,
        mesh=mesh,
        in_specs=(image,) * 6 + (P(),) + (shard,) * 3 + (P(), P()),
        out_specs=(image,) * 9 + (shard,) * 3,
        check_vma=False,
    )
```

```python
import functools

import jax
import jax.numpy as jnp
import numpy as np
from jax import lax
from jax.experimental import pallas as pl
from jax.experimental.pallas import tpu as pltpu
from jax.sharding import PartitionSpec as P

GROUPS = 32
EPSILON = 1e-05
ADAM_EPSILON = 1e-08
C = 512
AXES = ("band", "img")
VMEM_MARGIN = 6 * 1024 * 1024
VMEM_MOST = 58 * 1024 * 1024
F32, BF16 = jnp.float32, jnp.bfloat16

PIX = 1024
SEG_LINES = ((0, 24), (24, 32))
BUF_LINES = 36


class Plan:
    def __init__(self, shapes, n_band):
        (self.n_s, self.cap_s, self.side_s, _), (self.n_m, self.cap_m, self.side_m, _), (
            self.n_l,
            self.cap_l,
            self.side_l,
            _,
        ) = shapes
        assert (self.side_s, self.side_m, self.side_l) == (16, 24, 32)
        self.n_band = n_band
        self.n_chip = n_band // 2
        self.r_s, self.r_m, self.r_l = (
            self.cap_s * self.side_s,
            self.cap_m * self.side_m,
            self.cap_l * self.side_l,
        )
        holders = [dict() for _ in range(n_band)]
        for i in range(self.n_l):
            holders[2 * i]["l"] = i
        free = [b for b in range(n_band) if "l" not in holders[b]]
        for i in range(self.n_m):
            holders[free[i]]["m"] = i
        spots = [b for b in free if b >= 2 * self.n_l]
        for i in range(self.n_s):
            holders[spots[i]]["s"] = i
        self.holders = holders
        self.sizes = [
            (self.r_l if "l" in h else 0)
            + (self.r_m if "m" in h else 0)
            + (self.r_s if "s" in h else 0)
            for h in holders
        ]
        self.block = max(self.sizes[2 * j] + self.sizes[2 * j + 1] for j in range(self.n_chip))
        self.piece = max(self.sizes)
        self.offs = [0 if b % 2 == 0 else self.piece - self.sizes[b] for b in range(n_band)]
        self.is_l = np.array([int("l" in h) for h in holders], np.int32)
        self.has_m = np.array([int("m" in h) for h in holders], np.int32)
        self.has_s = np.array([int("s" in h) for h in holders], np.int32)
        self.off = np.array(self.offs, np.int32)


def pick(table, index):
    return lax.dynamic_index_in_dim(jnp.asarray(table), index, 0, keepdims=False)


def make_tables(plan, band_rows, position):
    nz = plan.n_chip
    z, core = position // 2, position % 2
    is_l, has_m, has_s, off = (pick(t, position) for t in (plan.is_l, plan.has_m, plan.has_s, plan.off))
    starts = jnp.cumsum(band_rows, axis=1) - band_rows
    zero_in = plan.n_band * plan.piece // 8

    def band_of(member, rows):
        return jnp.sum((starts[member][None, :] <= rows[:, None]).astype(jnp.int32), axis=1) - 1

    def place(member, rows):
        band = band_of(member, rows)
        onehot = band[:, None] == jnp.arange(plan.n_band)[None, :]
        start = jnp.sum(jnp.where(onehot, starts[member][None, :], 0), axis=1)
        k = (z - band // 2) % nz
        pos = jnp.where(band % 2 == core, k, nz + k)
        return pos * plan.piece + off, rows - start

    q = np.arange(128)
    base, r = place(2, jnp.asarray(q // 4, jnp.int32))
    src_l = (base + r * 32) // 8 + jnp.asarray(q % 4, jnp.int32)
    base, r = place(1, jnp.asarray(np.minimum(q // 4, 23), jnp.int32))
    src_m = (base + r * 24) // 8 + jnp.asarray(q % 4, jnp.int32)
    ok_m = jnp.asarray((q < 96) & (q % 4 < 3)) & (has_m == 1)
    line = np.clip((q - 96) // 4, 0, 7)
    base, r = place(0, jnp.asarray(line + 8 * (q % 4 // 2), jnp.int32))
    src_s = (base + has_m * plan.r_m + r * 16) // 8 + jnp.asarray(q % 2, jnp.int32)
    ok_s = jnp.asarray(q >= 96) & (has_s == 1)
    gather = jnp.where(
        is_l == 1, src_l, jnp.where(ok_m, src_m, jnp.where(ok_s, src_s, zero_in))
    ).astype(jnp.int32)

    per = plan.piece // 8
    p, t = np.divmod(np.arange(plan.n_band * per), per)
    k = jnp.asarray(p % nz, jnp.int32)
    c_src = jnp.where(jnp.asarray(p < nz), core, 1 - core)
    band = 2 * ((z - k) % nz) + c_src
    onehot = band[:, None] == jnp.arange(plan.n_band)[None, :]

    def of_band(row):
        return jnp.sum(jnp.where(onehot, row[None, :], 0), axis=1)

    within = jnp.asarray(t * 8, jnp.int32) - off
    wl = jnp.maximum(within, 0)
    r = wl // 32
    ok_l = (within >= 0) & (r < of_band(band_rows[2]))
    out_l = (of_band(starts[2]) + r) * 4 + wl % 32 // 8
    r = wl // 24
    in_m = (has_m == 1) & (wl < plan.r_m)
    ok_m = (within >= 0) & in_m & (r < of_band(band_rows[1]))
    out_m = (of_band(starts[1]) + r) * 4 + wl % 24 // 8
    ws = jnp.maximum(wl - has_m * plan.r_m, 0)
    r = ws // 16
    h = of_band(starts[0]) + r
    ok_s = (within >= 0) & (has_s == 1) & ~in_m & (r < of_band(band_rows[0]))
    out_s = 96 + (h % 8) * 4 + (h // 8) * 2 + ws % 16 // 8
    scatter = jnp.where(
        is_l == 1,
        jnp.where(ok_l, out_l, 128),
        jnp.where(ok_m, out_m, jnp.where(ok_s, out_s, 128)),
    ).astype(jnp.int32)
    flags = jnp.stack(
        [
            is_l,
            jnp.where(is_l == 1, 32, 24 * has_m),
            jnp.where(is_l == 1, 32, 32 * has_s),
            jnp.where(is_l == 1, 0, 16),
            core,
        ]
    ).astype(jnp.int32)
    return gather, scatter, flags


class Scalars:
    def __init__(self, flags):
        self.is_l = flags[0]
        self.lims = (flags[1], flags[2])
        self.split = flags[3]
        self.core = flags[4]
        self.l_f = flags[0].astype(F32)
        large = flags[0] == 1
        self.inv = (
            jnp.where(large, 1.0 / (1024 * 16), 1.0 / (576 * 16)).astype(F32),
            jnp.where(large, 1.0 / (1024 * 16), 1.0 / (256 * 16)).astype(F32),
        )


def dot(a, b):
    return jnp.dot(a, b, preferred_element_type=F32)


def dot_nt(a, b):
    return lax.dot_general(a, b, (((1,), (1,)), ((), ())), preferred_element_type=F32)


def dot_tn(a, b):
    return lax.dot_general(a, b, (((0,), (0,)), ((), ())), preferred_element_type=F32)


def line_rows(line):
    return pl.ds(pl.multiple_of(line * 32, 32), 32)


def line_loop(body, carries, unroll=2):
    results = []
    for seg, (low, high) in enumerate(SEG_LINES):
        results.append(
            lax.fori_loop(
                low, high, lambda line, carry, seg=seg: body(seg, line, carry), carries[seg], unroll=unroll
            )
        )
    return results


def fold(value):
    return value.reshape(4, 8, C).sum(axis=0)


def columns():
    return lax.broadcasted_iota(jnp.int32, (32, C), 0)


def fill_group_matrix(gm_ref):
    row = lax.broadcasted_iota(jnp.int32, (C, C), 0) // (C // GROUPS)
    col = lax.broadcasted_iota(jnp.int32, (C, C), 1) // (C // GROUPS)
    gm_ref[...] = (row == col).astype(F32).astype(BF16)


def group_totals(gm_ref, scal, per_seg):
    stacked = jnp.concatenate(list(per_seg) + [jnp.zeros((8 - len(per_seg), C), F32)], axis=0)
    hi = stacked.astype(BF16)
    rest = stacked - hi.astype(F32)
    mid = rest.astype(BF16)
    low = (rest - mid.astype(F32)).astype(BF16)
    both = dot(jnp.concatenate([hi, mid, low, jnp.zeros((8, C), BF16)], axis=0), gm_ref[...])
    total = both[0:8] + both[8:16] + both[16:24]
    out = []
    for i in range(0, len(per_seg), 2):
        first, second = total[i : i + 1], total[i + 1 : i + 2]
        out.append((first + scal.l_f * second, second + scal.l_f * first))
    return out


def norm_stats(read, gm_ref, scal, sums=None):
    zero = jnp.zeros((8, C), F32)
    if sums is None:
        sums = line_loop(lambda seg, line, acc: acc + fold(read(line)), (zero, zero))
    sums = [s.sum(axis=0, keepdims=True) for s in sums]
    (totals,) = group_totals(gm_ref, scal, sums)
    means = [totals[seg] * scal.inv[seg] for seg in range(2)]
    col = columns()

    def squares(seg, line, acc):
        dev = jnp.where(col < scal.lims[seg], read(line) - means[seg], 0.0)
        return acc + fold(dev * dev)

    sums = line_loop(squares, (zero, zero))
    sums = [s.sum(axis=0, keepdims=True) for s in sums]
    (totals,) = group_totals(gm_ref, scal, sums)
    rstds = [lax.rsqrt(totals[seg] * scal.inv[seg] + EPSILON) for seg in range(2)]
    return means, rstds


def store_shifted(buf_ref, scal, seg, line, value16):
    col = columns()
    value = value16.astype(F32)
    keep_left, keep_right = col != 0, col != 31
    if seg == 1:
        keep_left &= col != scal.split
        keep_right &= col != scal.split - 1
    left = jnp.where(keep_left, pltpu.roll(value, 1, 0), 0.0).astype(BF16)
    right = jnp.where(keep_right, pltpu.roll(value, 31, 0), 0.0).astype(BF16)
    at = line_rows(line + (1 if seg == 0 else 3))
    buf_ref[at, 0:C] = left
    buf_ref[at, C : 2 * C] = value16
    buf_ref[at, 2 * C : 3 * C] = right


def fill_halos(buf_ref, scal):
    zero = jnp.zeros((32, 3 * C), BF16)
    buf_ref[0:32, :] = zero
    buf_ref[25 * 32 : 26 * 32, :] = zero
    buf_ref[26 * 32 : 27 * 32, :] = zero
    buf_ref[35 * 32 : 36 * 32, :] = zero

    @pl.when(scal.is_l == 1)
    def _():
        buf_ref[25 * 32 : 26 * 32, :] = buf_ref[27 * 32 : 28 * 32, :]
        buf_ref[26 * 32 : 27 * 32, :] = buf_ref[24 * 32 : 25 * 32, :]

    @pl.when(scal.is_l == 0)
    def _():
        buf_ref[26 * 32 + 16 : 27 * 32, :] = buf_ref[34 * 32 : 34 * 32 + 16, :]
        buf_ref[35 * 32 : 35 * 32 + 16, :] = buf_ref[27 * 32 + 16 : 28 * 32, :]


def tile_at(tile):
    return pl.ds(pl.multiple_of(tile * 256, 256), 256)


def tile_rows(tile, shift):
    line = 8 * tile + jnp.where(tile == 3, 2, 0) + shift
    return pl.ds(pl.multiple_of(line * 32, 32), 256)


def tile_loop(body):
    def step(tile, carry):
        body(tile)
        return carry

    lax.fori_loop(0, 4, step, 0, unroll=2)


def conv_tiles(buf_ref, w_ref, out_ref):
    def body(tile):
        acc = None
        for shift in range(3):
            term = dot(buf_ref[tile_rows(tile, shift), :], w_ref[shift * 3 * C : (shift + 1) * 3 * C, :])
            acc = term if acc is None else acc + term
        out_ref[tile_at(tile), :] = acc

    tile_loop(body)


def gather_pieces(table_ref, src_ref, dst_ref, count):
    def step(i, carry):
        at = pl.multiple_of(table_ref[i] * 8, 8)
        dst_ref[pl.ds(pl.multiple_of(i * 8, 8), 8), :] = src_ref[pl.ds(at, 8), :]
        return carry

    lax.fori_loop(0, count, step, 0, unroll=4)


def slots_to_image(table_ref, scal, blocks, slots_ref, image_ref):
    piece = (slots_ref.shape[0] - 8) // len(blocks)
    start = pl.multiple_of((blocks[0].shape[0] - piece) * scal.core, 16)
    for i, block in enumerate(blocks):
        slots_ref[i * piece : (i + 1) * piece, :] = block[pl.ds(start, piece), :].astype(F32)
    slots_ref[len(blocks) * piece :, :] = jnp.zeros((8, C), F32)
    gather_pieces(table_ref, slots_ref, image_ref, 128)


def image_to_slots(table_ref, image_ref, slots_ref, own_ref, oth_ref):
    half = own_ref.shape[0]
    gather_pieces(table_ref, image_ref, slots_ref, 2 * half // 8)
    own_ref[...] = slots_ref[0:half, :].astype(BF16)
    oth_ref[...] = slots_ref[half : 2 * half, :].astype(BF16)


def swish_slope(value):
    sigma = jax.nn.sigmoid(value)
    return sigma * (1.0 + value * (1.0 - sigma))


def load_weights(pieces, parts, table, w, small16, sems):
    last = len(parts) * len(pieces)
    if len(pieces) == 1:
        copies = [[pltpu.make_async_copy(pieces[0].at[pl.ds(0, 22 * C)], w, sems.at[0])]]
        copy = pltpu.make_async_copy(pieces[0].at[pl.ds(22 * C, 16)], small16, sems.at[1])
        copy.start()
        copies[0][0].start()
        copy.wait()
    else:
        for i, piece in enumerate(pieces):

            @pl.when(table[last] == i)
            def _():
                pltpu.make_async_copy(
                    piece.at[pl.ds(parts[-1][0] + parts[-1][1], 16)], small16, sems.at[last]
                ).start()

        copies = []
        for p, (start, count) in enumerate(parts):
            copies.append([])
            for i, piece in enumerate(pieces):
                e = i * len(parts) + p
                at = pl.multiple_of(table[e] * 16, 16)
                copy = pltpu.make_async_copy(
                    piece.at[pl.ds(start, count)], w.at[pl.ds(at, count)], sems.at[e]
                )
                copy.start()
                copies[p].append(copy)
        pltpu.make_async_copy(pieces[0].at[pl.ds(0, 16)], small16, sems.at[last]).wait()

    def wait(p):
        if p < len(copies):
            for copy in copies[p]:
                copy.wait()

    return wait


def features_kernel(first, sources, count, parts, *refs):
    if first:
        gather, flags, table = refs[:3]
        blocks, refs = refs[3 : 3 + sources], refs[3 + sources :]
        pieces, refs = refs[:count], refs[count:]
        x_out, a1_out, h1_out, a2_out, y_ref, z_out, q_ref, k_ref, v_ref, stats, small, w_out = refs[:12]
        slots, x_ref, h_ref, z_ref, buf, w, gm, sems, small16, a1, h1, a2, x16, out_sems = refs[12:]
    else:
        scatter, flags, table, x_in, stats = refs[:5]
        pieces, refs = refs[5 : 5 + count], refs[5 + count :]
        own_out, oth_out = refs[:2]
        slots, x_ref, h_ref, z_ref, buf, w, gm, sems, small16, small, y_ref, q_ref, k_ref, v_ref = refs[2:]
    wait_weights = load_weights(pieces, parts, table, w, small16, sems)
    scal = Scalars(flags)
    fill_group_matrix(gm)
    small[...] = small16[...].astype(F32)
    col = columns()
    saves = []

    def save(value, out):
        if first:
            copy = pltpu.make_async_copy(value, out, out_sems.at[len(saves)])
            copy.start()
            saves.append(copy)

    def row(i):
        return small[i : i + 1, :]

    def activate(read, means, rstds, gain, shift, keep):
        def body(seg, line, carry):
            normed = (read(line) - means[seg]) * rstds[seg] * gain + shift
            act = jnp.where(col < scal.lims[seg], normed * jax.nn.sigmoid(normed), 0.0).astype(BF16)
            if keep is not None:
                keep[line_rows(line), :] = act
            store_shifted(buf, scal, seg, line, act)
            return carry

        line_loop(body, (0, 0))
        fill_halos(buf, scal)

    def read_x(line):
        return x_ref[line_rows(line), :]

    if first:
        slots_to_image(gather, scal, blocks, slots, x_ref)
        means1, rstds1 = norm_stats(read_x, gm, scal)

        def keep_x(seg, line, carry):
            x16[line_rows(line), :] = read_x(line).astype(BF16)
            return carry

        line_loop(keep_x, (0, 0))
        save(x16, x_out)
    else:

        def widen_x(seg, line, carry):
            x_ref[line_rows(line), :] = x_in[line_rows(line), :].astype(F32)
            return carry

        line_loop(widen_x, (0, 0))
        means1, rstds1 = [stats[0:1, :], stats[1:2, :]], [stats[2:3, :], stats[3:4, :]]
    activate(read_x, means1, rstds1, row(0), row(1), a1 if first else None)
    if first:
        save(a1, a1_out)
    wait_weights(0)
    if first:
        save(w, w_out)

    conv_tiles(buf, w.at[0 : 9 * C], h_ref)

    def finish_h(seg, line, carry):
        value = jnp.where(col < scal.lims[seg], h_ref[line_rows(line), :] + row(2), 0.0)
        h_ref[line_rows(line), :] = value
        if first:
            h1[line_rows(line), :] = value
        return carry + fold(value)

    zero = jnp.zeros((8, C), F32)

    def read_h(line):
        return h_ref[line_rows(line), :]

    means2, rstds2 = norm_stats(read_h, gm, scal, line_loop(finish_h, (zero, zero)))
    if first:
        save(h1, h1_out)
    activate(read_h, means2, rstds2, row(3), row(4), a2 if first else None)
    if first:
        save(a2, a2_out)
    wait_weights(1)
    conv_tiles(buf, w.at[9 * C : 18 * C], h_ref)

    def finish_y(seg, line, carry):
        value = jnp.where(
            col < scal.lims[seg], read_x(line) + (h_ref[line_rows(line), :] + row(5)), 0.0
        )
        y_ref[line_rows(line), :] = value
        return carry + fold(value)

    def read_y(line):
        return y_ref[line_rows(line), :]

    means3, rstds3 = norm_stats(read_y, gm, scal, line_loop(finish_y, (zero, zero)))

    def third(seg, line, carry):
        normed = (read_y(line) - means3[seg]) * rstds3[seg] * row(6) + row(7)
        z_ref[line_rows(line), :] = jnp.where(col < scal.lims[seg], normed, 0.0).astype(BF16)
        return carry

    line_loop(third, (0, 0))
    if first:
        save(z_ref, z_out)

    def project(tile):
        at = tile_at(tile)
        rows = z_ref[at, :]
        q_ref[at, :] = (dot(rows, w[18 * C : 19 * C, :]) + row(8)).astype(BF16)
        k_ref[at, :] = dot(rows, w[19 * C : 20 * C, :]).astype(BF16)
        v_ref[at, :] = (dot(rows, w[20 * C : 21 * C, :]) + row(9)).astype(BF16)

    tile_loop(project)
    if first:
        for i, pair in enumerate((means1, rstds1, means2, rstds2, means3, rstds3)):
            stats[2 * i : 2 * i + 1, :] = pair[0]
            stats[2 * i + 1 : 2 * i + 2, :] = pair[1]
        stats[12:16, :] = jnp.zeros((4, C), F32)
        for copy in saves:
            copy.wait()
        return
    bias = key_bias(scal)

    def attend(tile):
        at = tile_at(tile)
        prob = probabilities(q_ref[at, :], k_ref, bias(tile)).astype(BF16)
        mixed = dot(prob, v_ref[...]).astype(BF16)
        y_ref[at, :] = y_ref[at, :] + (dot(mixed, w[21 * C : 22 * C, :]) + row(10))

    tile_loop(attend)
    y_ref[PIX : PIX + 8, :] = jnp.zeros((8, C), F32)
    image_to_slots(scatter, y_ref, slots, own_out, oth_out)


def key_bias(scal):
    key = lax.broadcasted_iota(jnp.int32, (1, PIX), 1)
    column = key % 32
    in0 = key < 768
    ok0 = in0 & (column < scal.lims[0])
    ok1 = (~in0) & (column < scal.lims[1])
    large = scal.is_l == 1
    row0 = jnp.where(ok0 | (ok1 & large), 0.0, -1e30).astype(F32)
    row1 = jnp.where(ok1 | (ok0 & large), 0.0, -1e30).astype(F32)
    return lambda tile: jnp.where(tile == 3, row1, row0)


def probabilities(q, k_ref, bias):
    scores = dot_nt(q, k_ref[...]) * (C**-0.5) + bias
    top = jnp.max(scores, axis=1, keepdims=True)
    expo = jnp.exp(scores - top)
    return expo * (1.0 / jnp.sum(expo, axis=1, keepdims=True))


def attend_both_kernel(
    gather,
    scatter,
    flags,
    q,
    k,
    v,
    y,
    z,
    stats,
    small,
    weights,
    *refs,
):
    blocks = refs[:-23]
    own_out, oth_out, dy_out, dy16_out, grads_out, sums_out = refs[-23:-17]
    image, slots, g_ref, o_ref, d_ref, dk_acc, dv_acc, wp, gm, sems = refs[-17:-7]
    loaded = [
        (weights.at[pl.ds(18 * C, 4 * C)], wp),
        (q, refs[-7]),
        (k, refs[-6]),
        (v, refs[-5]),
        (y, refs[-4]),
        (z, refs[-3]),
    ]
    loads = [pltpu.make_async_copy(a, b, sems.at[i]) for i, (a, b) in enumerate(loaded)]
    for load in loads:
        load.start()
    q, k, v, y, z, grads, own_rows = refs[-7:]
    oth_rows = own_rows.at[pl.ds(own_out.shape[0], own_out.shape[0])]
    own_rows = own_rows.at[pl.ds(0, own_out.shape[0])]
    stores = [(own_rows, own_out), (oth_rows, oth_out), (grads, grads_out)]
    stores = [pltpu.make_async_copy(a, b, sems.at[6 + i]) for i, (a, b) in enumerate(stores)]
    scal = Scalars(flags)
    fill_group_matrix(gm)
    bias = key_bias(scal)
    slots_to_image(gather, scal, blocks, slots, g_ref)
    for load in loads[:5]:
        load.wait()
    scaling = C**-0.5
    dk_acc[...] = jnp.zeros(MAP, F32)
    dv_acc[...] = jnp.zeros(MAP, F32)

    def attend(tile):
        at = tile_at(tile)
        q_t = q[at, :]
        prob = probabilities(q_t, k, bias(tile))
        prob16 = prob.astype(BF16)
        mixed = dot(prob16, v[...]).astype(BF16)
        o_ref[at, :] = mixed
        image[at, :] = y[at, :] + (dot(mixed, wp[3 * C : 4 * C, :]) + small[10:11, :])
        d_mixed = dot_nt(g_ref[at, :].astype(BF16), wp[3 * C : 4 * C, :]).astype(BF16)
        d_prob = dot_nt(d_mixed, v[...])
        inner = jnp.sum(prob * d_prob, axis=1, keepdims=True)
        d_score = (prob * (d_prob - inner)).astype(BF16)
        d_ref[at, 0:C] = (scaling * dot(d_score, k[...])).astype(BF16)
        dk_acc[...] += dot_tn(d_score, q_t)
        dv_acc[...] += dot_tn(prob16, d_mixed)

    tile_loop(attend)
    d_ref[:, C : 2 * C] = (scaling * dk_acc[...]).astype(BF16)
    d_ref[:, 2 * C : 3 * C] = dv_acc[...].astype(BF16)
    image[PIX : PIX + 8, :] = jnp.zeros((8, C), F32)
    image_to_slots(scatter, image, slots, own_rows, oth_rows)
    stores[0].start()
    stores[1].start()
    loads[5].wait()
    for part in range(3):
        grads[part * C : (part + 1) * C, :] = dot_tn(z[...], d_ref[:, part * C : (part + 1) * C]).astype(
            BF16
        )
    grads[3 * C : 4 * C, :] = dot_tn(o_ref[...], g_ref[...].astype(BF16)).astype(BF16)
    stores[2].start()
    def back_to_norm(tile):
        at = tile_at(tile)
        acc = dot_nt(d_ref[at, 0:C], wp[0:C, :])
        acc = acc + dot_nt(d_ref[at, C : 2 * C], wp[C : 2 * C, :])
        image[at, :] = acc + dot_nt(d_ref[at, 2 * C : 3 * C], wp[2 * C : 3 * C, :])

    tile_loop(back_to_norm)
    col = columns()
    means = (stats[8:9, :], stats[9:10, :])
    rstds = (stats[10:11, :], stats[11:12, :])
    zero = jnp.zeros((8, C), F32)

    def sums(seg, line, acc):
        at = line_rows(line)
        d_norm = image[at, :]
        unit = (y[at, :] - means[seg]) * rstds[seg]
        d_all = d_ref[at, :].astype(F32)
        return (
            acc[0] + fold(d_norm),
            acc[1] + fold(d_norm * unit),
            acc[2] + fold(d_all[:, 0:C]),
            acc[3] + fold(d_all[:, 2 * C : 3 * C]),
            acc[4] + fold(g_ref[at, :]),
        )

    got = line_loop(sums, ((zero,) * 5, (zero,) * 5), unroll=1)
    got = [[part.sum(axis=0, keepdims=True) for part in seg] for seg in got]
    gain = small[6:7, :]
    ones, cross = group_totals(
        gm, scal, [got[0][0] * gain, got[1][0] * gain, got[0][1] * gain, got[1][1] * gain]
    )
    sums_out[...] = jnp.zeros((16, C), F32)
    for i, part in enumerate((1, 0, 2, 3, 4)):
        sums_out[6 + i : 7 + i, :] = got[0][part] + got[1][part]

    def back(seg, line, carry):
        at = line_rows(line)
        unit = (y[at, :] - means[seg]) * rstds[seg]
        d_in = rstds[seg] * (
            image[at, :] * gain - ones[seg] * scal.inv[seg] - unit * (cross[seg] * scal.inv[seg])
        )
        value = g_ref[at, :] + jnp.where(col < scal.lims[seg], d_in, 0.0)
        dy_out[at, :] = value
        dy16_out[at, :] = value.astype(BF16)
        return carry

    line_loop(back, (0, 0))
    for store in stores:
        store.wait()


def fill_gradient_buffer(buf, scal, grad_ref):
    def body(seg, line, carry):
        store_shifted(buf, scal, seg, line, grad_ref[line_rows(line), :])
        return carry

    line_loop(body, (0, 0))
    fill_halos(buf, scal)


def weight_grad_kernel(conv, split, *refs):
    if not split:
        flags, act, grad, w_out, sums_out, buf, act_t = refs
    else:
        flags, act, grad, more = refs[:4]
        planes, refs = refs[4:8], refs[8:]
        early_out = refs[0] if conv == 1 else None
        sums_out, buf, act_t, rows, sems = refs[conv:]
        kept, sent = planes[:2], planes[2:]
        offset = 2 * C if conv == 1 else 0
        more_at = 9 * C - offset
        load = pltpu.make_async_copy(more, rows.at[pl.ds(more_at, more.shape[0])], sems.at[4])
        load.start()
    scal = Scalars(flags)
    fill_gradient_buffer(buf, scal, grad)
    for tile in range(4):
        at = slice(tile * 256, (tile + 1) * 256)
        act_t[:, at] = act[at, :].T

    def send_out(run):
        plane, core = run // 2, run % 2
        source = rows.at[pl.ds(run * 1408, 1408)]

        @pl.when(scal.core == core)
        def _():
            pltpu.make_async_copy(source, kept[plane], sems.at[run]).start()

        @pl.when(scal.core != core)
        def _():
            pltpu.make_async_copy(source, sent[plane], sems.at[run]).start()

    ready = {0: (3,) if conv == 0 else (2, 3), 1: (2,) if conv == 0 else (1,), 2: (0, 1) if conv == 0 else (0,)}
    for shift in range(3):
        seg0 = slice(shift * 32, shift * 32 + 768)
        seg1 = slice((26 + shift) * 32, (26 + shift) * 32 + 256)
        for part in range(3):
            cols = slice(part * C, (part + 1) * C)
            value = dot(act_t[:, 0:768], buf[seg0, cols]) + dot(act_t[:, 768:1024], buf[seg1, cols])
            tap = 3 * (2 - shift) + (2 - part)
            if not split:
                w_out[tap * C : (tap + 1) * C, :] = value.astype(BF16)
            elif conv == 1 and tap < 2:
                early_out[tap * C : (tap + 1) * C, :] = value.astype(BF16)
            else:
                rows[tap * C - offset : (tap + 1) * C - offset, :] = value.astype(BF16)
        if split:
            if shift == 0:
                load.wait()
            for run in ready[shift]:
                send_out(run)
    zero = jnp.zeros((8, C), F32)
    got = line_loop(
        lambda seg, line, acc: acc + fold(grad[line_rows(line), :].astype(F32)), (zero, zero)
    )
    sums_out[...] = jnp.zeros((16, C), F32)
    sums_out[3 * conv + 2 : 3 * conv + 3, :] = (got[0] + got[1]).sum(axis=0, keepdims=True)
    if split:
        for run in range(4):
            pltpu.make_async_copy(rows.at[pl.ds(run * 1408, 1408)], kept[run // 2], sems.at[run]).wait()


def data_grad_kernel(last, conv, *refs):
    if last:
        scatter, flags, grad, feat, dy, stats, small, weights, own_out, oth_out, sums_out = refs[:11]
        dn, slots, buf, w, gm, sems, feat_v, dy_v = refs[11:]
    else:
        flags, grad, feat, stats, small, weights, grad_out, sums_out = refs[:8]
        dn, buf, w, gm, sems, feat_v = refs[8:]
    copies = [pltpu.make_async_copy(weights.at[pl.ds(conv * 9 * C, 9 * C)], w, sems.at[0])]
    copies.append(pltpu.make_async_copy(feat, feat_v, sems.at[1]))
    if last:
        copies.append(pltpu.make_async_copy(dy, dy_v, sems.at[2]))
        dy = dy_v
    feat = feat_v
    for copy in copies:
        copy.start()
    scal = Scalars(flags)
    fill_group_matrix(gm)
    fill_gradient_buffer(buf, scal, grad)
    copies[0].wait()

    def transposed(tile):
        acc = None
        for shift in range(3):
            for part in range(3):
                tap = 3 * (2 - shift) + (2 - part)
                term = dot_nt(
                    buf[tile_rows(tile, shift), part * C : (part + 1) * C], w[tap * C : (tap + 1) * C, :]
                )
                acc = term if acc is None else acc + term
        dn[tile_at(tile), :] = acc

    tile_loop(transposed)
    for copy in copies[1:]:
        copy.wait()
    base = 4 * conv
    means = (stats[base : base + 1, :], stats[base + 1 : base + 2, :])
    rstds = (stats[base + 2 : base + 3, :], stats[base + 3 : base + 4, :])
    gain, shift_row = small[3 * conv : 3 * conv + 1, :], small[3 * conv + 1 : 3 * conv + 2, :]
    col = columns()
    zero = jnp.zeros((8, C), F32)

    def sums(seg, line, acc):
        at = line_rows(line)
        unit = (feat[at, :].astype(F32) - means[seg]) * rstds[seg]
        value = dn[at, :] * swish_slope(unit * gain + shift_row)
        value = jnp.where(col < scal.lims[seg], value, 0.0)
        dn[at, :] = value
        return (acc[0] + fold(value), acc[1] + fold(value * unit))

    got = line_loop(sums, ((zero, zero), (zero, zero)))
    got = [[part.sum(axis=0, keepdims=True) for part in seg] for seg in got]
    ones, cross = group_totals(
        gm, scal, [got[0][0] * gain, got[1][0] * gain, got[0][1] * gain, got[1][1] * gain]
    )
    sums_out[...] = jnp.zeros((16, C), F32)
    sums_out[3 * conv : 3 * conv + 1, :] = got[0][1] + got[1][1]
    sums_out[3 * conv + 1 : 3 * conv + 2, :] = got[0][0] + got[1][0]

    def back(seg, line, carry):
        at = line_rows(line)
        unit = (feat[at, :].astype(F32) - means[seg]) * rstds[seg]
        value = rstds[seg] * (
            dn[at, :] * gain - ones[seg] * scal.inv[seg] - unit * (cross[seg] * scal.inv[seg])
        )
        value = jnp.where(col < scal.lims[seg], value, 0.0)
        if last:
            dn[at, :] = value + dy[at, :]
        else:
            grad_out[at, :] = value.astype(BF16)
        return carry

    line_loop(back, (0, 0))
    if last:
        dn[PIX : PIX + 8, :] = jnp.zeros((8, C), F32)
        image_to_slots(scatter, dn, slots, own_out, oth_out)


SMEM = pl.BlockSpec(memory_space=pltpu.SMEM)
VMEM = pl.BlockSpec(memory_space=pltpu.VMEM)
HBM = pl.BlockSpec(memory_space=pltpu.HBM)


def call(kernel, name, in_specs, outs, scratch, flops, args, out_specs=None, limit=None):
    moved = sum(int(np.prod(a.shape)) * a.dtype.itemsize for a in args)
    moved += sum(int(np.prod(s)) * jnp.dtype(d).itemsize for s, d in outs)
    out_specs = out_specs or [VMEM] * len(outs)
    held = [(a.shape, a.dtype) for a, spec in zip(args, in_specs) if spec is VMEM]
    held += [out for out, spec in zip(outs, out_specs) if spec is VMEM]
    held += [(s.shape, s.dtype) for s in scratch if s.memory_space == pltpu.VMEM]
    used = sum(int(np.prod(s)) * jnp.dtype(d).itemsize for s, d in held)
    return pl.pallas_call(
        kernel,
        name=name,
        out_shape=[jax.ShapeDtypeStruct(s, d) for s, d in outs],
        in_specs=in_specs,
        out_specs=out_specs,
        scratch_shapes=scratch,
        compiler_params=pltpu.CompilerParams(vmem_limit_bytes=limit or used + VMEM_MARGIN),
        cost_estimate=pl.CostEstimate(flops=int(flops), bytes_accessed=moved, transcendentals=0),
    )(*args)


MAP, SLOT_PAD = (PIX, C), 8
MICROSECOND = 1_100_000_000
BUF = pltpu.VMEM((BUF_LINES * 32, 3 * C), BF16)


def run_features(first, plan, tables, x, pieces, parts, table):
    gather, scatter, flags = tables
    slot_rows = plan.n_band * plan.piece
    count = len(pieces)
    scratch = [
        pltpu.VMEM((slot_rows + SLOT_PAD, C), F32),
        pltpu.VMEM(MAP, F32),
        pltpu.VMEM(MAP, F32),
        pltpu.VMEM(MAP, BF16),
        BUF,
        pltpu.VMEM((22 * C, C), BF16),
        pltpu.VMEM((C, C), BF16),
        pltpu.SemaphoreType.DMA((len(parts) * count + 1,)),
        pltpu.VMEM((16, C), BF16),
    ]
    if first:
        outs = [
            (MAP, BF16),
            (MAP, BF16),
            (MAP, F32),
            (MAP, BF16),
            (MAP, F32),
            (MAP, BF16),
            (MAP, BF16),
            (MAP, BF16),
            (MAP, BF16),
            ((16, C), F32),
            ((16, C), F32),
            ((22 * C, C), BF16),
        ]
        return call(
            functools.partial(features_kernel, True, len(x), count, parts),
            "features_first",
            [SMEM] * 3 + [VMEM] * len(x) + [HBM] * count,
            outs,
            scratch
            + [
                pltpu.VMEM(MAP, BF16),
                pltpu.VMEM(MAP, F32),
                pltpu.VMEM(MAP, BF16),
                pltpu.VMEM(MAP, BF16),
                pltpu.SemaphoreType.DMA((6,)),
            ],
            26 * MICROSECOND,
            (gather, flags, table, *x, *pieces),
            out_specs=[HBM] * 4 + [VMEM, HBM] + [VMEM] * 5 + [HBM],
            limit=VMEM_MOST,
        )
    return call(
        functools.partial(features_kernel, False, 0, count, parts),
        "forward_again",
        [SMEM] * 3 + [VMEM] * 2 + [HBM] * count,
        [((slot_rows // 2, C), BF16)] * 2,
        scratch
        + [
            pltpu.VMEM((16, C), F32),
            pltpu.VMEM((PIX + 8, C), F32),
            pltpu.VMEM(MAP, BF16),
            pltpu.VMEM(MAP, BF16),
            pltpu.VMEM(MAP, BF16),
        ],
        28 * MICROSECOND,
        (scatter, flags, table, *x, *pieces),
        limit=VMEM_MOST,
    )


def run_attend_both(plan, tables, q, k, v, y, z, blocks, stats, small, weights):
    gather, scatter, flags = tables
    slot_rows = plan.n_band * plan.piece
    return call(
        attend_both_kernel,
        "attend_both",
        [SMEM] * 3 + [HBM] * 5 + [VMEM] * 2 + [HBM] + [VMEM] * len(blocks),
        [
            ((slot_rows // 2, C), BF16),
            ((slot_rows // 2, C), BF16),
            (MAP, F32),
            (MAP, BF16),
            ((4 * C, C), BF16),
            ((16, C), F32),
        ],
        [
            pltpu.VMEM((PIX + 8, C), F32),
            pltpu.VMEM((slot_rows + SLOT_PAD, C), F32),
            pltpu.VMEM(MAP, F32),
            pltpu.VMEM(MAP, BF16),
            pltpu.VMEM((PIX, 3 * C), BF16),
            pltpu.VMEM(MAP, F32),
            pltpu.VMEM(MAP, F32),
            pltpu.VMEM((4 * C, C), BF16),
            pltpu.VMEM((C, C), BF16),
            pltpu.SemaphoreType.DMA((9,)),
            pltpu.VMEM(MAP, BF16),
            pltpu.VMEM(MAP, BF16),
            pltpu.VMEM(MAP, BF16),
            pltpu.VMEM(MAP, F32),
            pltpu.VMEM(MAP, BF16),
            pltpu.VMEM((4 * C, C), BF16),
            pltpu.VMEM((slot_rows, C), BF16),
        ],
        24 * MICROSECOND,
        (gather, scatter, flags, q, k, v, y, z, stats, small, weights, *blocks),
        out_specs=[HBM] * 2 + [VMEM] * 2 + [HBM, VMEM],
        limit=VMEM_MOST,
    )


def run_weight_grad(tables, conv, act, grad, more=None):
    scratch = [BUF, pltpu.VMEM((C, PIX), BF16)]
    name = "weight_grad_one" if conv == 0 else "weight_grad_two"
    if more is None:
        return call(
            functools.partial(weight_grad_kernel, conv, False),
            name,
            [SMEM, VMEM, VMEM],
            [((9 * C, C), BF16), ((16, C), F32)],
            scratch,
            9 * MICROSECOND,
            (tables[2], act, grad),
        )
    early = [((2 * C, C), BF16)] if conv == 1 else []
    return call(
        functools.partial(weight_grad_kernel, conv, True),
        name,
        [SMEM, VMEM, VMEM, HBM],
        [((1408, C), BF16)] * 4 + early + [((16, C), F32)],
        scratch + [pltpu.VMEM((5632, C), BF16), pltpu.SemaphoreType.DMA((5,))],
        9 * MICROSECOND,
        (tables[2], act, grad, more),
        out_specs=[HBM] * 4 + [VMEM] * len(early) + [VMEM],
        limit=VMEM_MOST,
    )


def run_data_grad(tables, conv, grad, feat, stats, small, weights, dy=None, half=None):
    last = dy is not None
    scratch = [BUF, pltpu.VMEM((9 * C, C), BF16), pltpu.VMEM((C, C), BF16), pltpu.SemaphoreType.DMA((3,))]
    scratch.append(pltpu.VMEM(MAP, feat.dtype))
    if last:
        outs = [((half, C), BF16)] * 2
        scratch = [pltpu.VMEM((PIX + 8, C), F32), pltpu.VMEM((2 * half, C), F32)] + scratch
        scratch.append(pltpu.VMEM(MAP, F32))
        args = (tables[1], tables[2], grad, feat, dy, stats, small, weights)
        specs = [SMEM, SMEM, VMEM, HBM, HBM, VMEM, VMEM, HBM]
    else:
        outs = [(MAP, BF16)]
        scratch = [pltpu.VMEM(MAP, F32)] + scratch
        args = (tables[2], grad, feat, stats, small, weights)
        specs = [SMEM, VMEM, HBM, VMEM, VMEM, HBM]
    return call(
        functools.partial(data_grad_kernel, last, conv),
        "data_grad_one" if conv == 0 else "data_grad_two",
        specs,
        outs + [((16, C), F32)],
        scratch,
        12 * MICROSECOND,
        args,
        limit=VMEM_MOST,
    )


def z_shift(value, nz, k):
    return lax.ppermute(value, "band", [(2 * z + c, 2 * ((z + k) % nz) + c) for z in range(nz) for c in range(2)])


def core_swap(value, n_band):
    return lax.ppermute(value, "band", [(b, b ^ 1) for b in range(n_band)])


def stage(values):
    return lax.optimization_barrier(values)


def pack_slots(plan, arrays):
    flat = [a.reshape(a.shape[0], -1, C) for a in arrays]
    blocks = []
    for chip in range(plan.n_chip):
        parts = []
        for c in range(2):
            h = plan.holders[2 * chip + c]
            mine = [flat[m][h[name]] for m, name in ((2, "l"), (1, "m"), (0, "s")) if name in h]
            if c == 1:
                used = plan.sizes[2 * chip] + plan.sizes[2 * chip + 1]
                if used < plan.block:
                    parts.append(jnp.zeros((plan.block - used, C), BF16))
            parts += mine
        blocks.append(jnp.concatenate(parts, axis=0))
    return jnp.stack(blocks)


def chip_blocks(plan, position, arrays):
    z, nz = position // 2, plan.n_chip
    sent = pack_slots(plan, arrays)
    return [lax.dynamic_index_in_dim(sent, (z + k) % nz, 0, keepdims=False) for k in range(nz)]


def to_chips(plan, blocks):
    return [blocks[0]] + [z_shift(blocks[k], plan.n_chip, k) for k in range(1, plan.n_chip)]


def to_cores(plan, received):
    return [*received, *[core_swap(block, plan.n_band) for block in received]]


def merge_cores(plan, position, own, got):
    core, nz, slack = position % 2, plan.n_chip, plan.block - plan.piece
    own, got = own.reshape(nz, plan.piece, C), got.reshape(nz, plan.piece, C)
    first, second = jnp.where(core == 0, own, got), jnp.where(core == 0, got, own)
    return jnp.pad(first, ((0, 0), (0, slack), (0, 0))) + jnp.pad(second, ((0, 0), (slack, 0), (0, 0)))


def from_chips(plan, blocks):
    return [blocks[0]] + [z_shift(blocks[k], plan.n_chip, -k) for k in range(1, plan.n_chip)]


def to_bands(plan, position, received):
    z, nz, slack = position // 2, plan.n_chip, plan.block - plan.piece
    received = jnp.stack(received)
    images = [[None] * plan.n_s, [None] * plan.n_m, [None] * plan.n_l]
    for b, h in enumerate(plan.holders):
        chip = b // 2
        if not h:
            continue
        block = lax.dynamic_index_in_dim(received, (chip - z) % nz, 0, keepdims=False)
        at = plan.offs[b] + (slack if b % 2 else 0)
        for member, name, size in ((2, "l", plan.r_l), (1, "m", plan.r_m), (0, "s", plan.r_s)):
            if name in h:
                images[member][h[name]] = block[at : at + size]
                at += size
    sides = (plan.side_s, plan.side_m, plan.side_l)
    return [
        jnp.stack(images[m]).reshape(len(images[m]), -1, sides[m], C) for m in range(3)
    ]


class Place:
    def __init__(self):
        self.n_band, self.n_img = lax.axis_size("band"), lax.axis_size("img")
        self.count = self.n_band * self.n_img
        self.position, self.img = lax.axis_index("band"), lax.axis_index("img")
        self.owner = self.position * self.n_img + self.img
        self.z, self.core = self.position // 2, self.position % 2
        self.y, self.x = self.img // 2, self.img % 2
        self.planes = self.n_band == 8 and self.n_img == 4


def over_core(value):
    return core_swap(value, lax.axis_size("band"))


def over_x(value):
    return lax.ppermute(value, "img", [(i, i ^ 1) for i in range(4)])


def over_y(value):
    return lax.ppermute(value, "img", [(i, i ^ 2) for i in range(4)])


def along_z(value, pairs):
    return lax.ppermute(value, "band", [(2 * a + c, 2 * b + c) for a, b in pairs for c in range(2)])


def over_corner(value):
    return lax.ppermute(value, "img", [(i, i ^ 3) for i in range(4)])


class Gather:
    def __init__(self, block):
        self.block = block

    def beside(self):
        return [self.block, over_x(self.block), over_y(self.block)]

    def first(self, got=None):
        block, x0, y0 = got or self.beside()
        return [block, x0, y0, over_corner(block), z_shift(block, 4, 1), z_shift(block, 4, 3)]

    def second(self, values):
        block, x0, y0, d0, up, down = values
        across = z_shift(block, 4, 2)
        return values + [over_x(up), over_y(up), over_x(down), over_y(down), across]

    def third(self, values):
        d0, up, down, x1, y1, x3, y3, across = values[3:]
        return values + [over_x(across), over_y(across), z_shift(d0, 4, 2), over_y(x1), over_x(y3)]

    def others(self, values, count):
        return [over_core(value) for value in values[:count]]

    def pieces(self, values, others):
        def ordered(v):
            block, x0, y0, d0, up, down, x1, y1, x3, y3, across, x2, y2, d2, c1, c3 = v
            return [block, x0, y0, d0, up, x1, y1, c1, across, x2, y2, d2, down, x3, y3, c3]

        return ordered(values) + ordered(others)


GATHERED = [(side, k, flip) for side in range(2) for k in (0, 1, 2, 3) for flip in range(4)]


def gather_table(here, core, block_rows):
    side, k, flip = np.array(GATHERED, np.int32).T
    core, z, img = core ^ side, (here.z - k) % 4, here.img ^ flip
    last = (core == 1) & (z == 3) & (img == 3)
    rows = jnp.stack(block_rows(z, 4 * core + img), axis=1).reshape(-1)
    return jnp.concatenate([rows, jnp.argmax(last)[None]]).astype(jnp.int32)


def part(value, axis, index):
    return lax.dynamic_index_in_dim(value, index, axis, keepdims=False)


def add_part(kept, got, axis, index):
    both = [part(value.reshape(2, 2, 352, C), axis, index) for value in (kept, got)]
    return both[0] + both[1]


def halves_to_send(here, kept, got):
    return add_part(kept[0], got[0], 1, 1 - here.x), add_part(kept[1], got[1], 0, 1 - here.y)


def send_halves(a, b):
    return over_x(a), over_y(b)


def add_halves(here, kept, got, got_a, got_b):
    a = add_part(kept[0], got[0], 1, here.x) + got_a
    b = add_part(kept[1], got[1], 0, here.y) + got_b
    return a, b


def quarters_to_send(here, a, b):
    return part(a, 0, 1 - here.y), part(b, 0, 1 - here.x)


def send_quarters(a, b):
    return over_y(a), over_x(b)


def add_quarters(here, a, b, got_a, got_b):
    return (
        part(a, 0, here.y).astype(F32) + got_a.astype(F32),
        part(b, 0, here.x).astype(F32) + got_b.astype(F32),
    )


def by_plane(low_planes, first, second):
    halves = [first[:176], second[:176], first[176:], second[176:]]
    return jnp.stack(halves if low_planes else halves[2:] + halves[:2])


def send_planes(here, planes, more=None):
    planes16 = planes.astype(BF16)
    sent = [part(planes16, 0, (here.z + k) % 4) for k in (1, 3, 2)]
    if more is not None:
        sent = [jnp.concatenate([value, more.astype(BF16)], axis=0) for value in sent]
    return [z_shift(value, 4, k) for value, k in zip(sent, (1, 3, 2))]


def add_planes(here, planes, got, more=None):
    total = part(planes, 0, here.z)
    if more is not None:
        total = jnp.concatenate([total, more], axis=0)
    for value in got:
        total = total + value.astype(F32)
    return total


def over_two_planes(value):
    return along_z(value, [(0, 2), (2, 0), (1, 3), (3, 1)])


def sum_over_img(value):
    return (value + over_x(value)) + (over_y(value) + over_corner(value))


def adam(params, first, second, grad, step_count, rate):
    new_first = 0.5 * first + 0.5 * grad
    new_second = 0.9 * second + 0.1 * grad * grad
    update = (
        rate
        * (new_first / (1.0 - jnp.power(0.5, step_count)))
        / (jnp.sqrt(new_second / (1.0 - jnp.power(0.9, step_count))) + ADAM_EPSILON)
    )
    return update, new_first, new_second


def body(
    x_small,
    x_medium,
    x_large,
    cot_small,
    cot_medium,
    cot_large,
    band_rows,
    params,
    first_moment,
    second_moment,
    step,
    rate,
):
    here = Place()
    n_band, position = here.n_band, here.position
    plan = Plan([x_small.shape, x_medium.shape, x_large.shape], n_band)
    tables = make_tables(plan, band_rows, position)
    half = n_band // 2 * plan.piece
    rows, count = params.shape[0], here.count
    step_count, step_rate = step[0].astype(F32), rate[0]
    last = count - 1
    singles = 22 * C - last * rows

    images, cots = (x_small, x_medium, x_large), (cot_small, cot_medium, cot_large)
    if here.planes:
        shard16 = params.astype(BF16)
        before = lax.ppermute(params[rows - count :].astype(BF16), AXES, [(o, o + 1) for o in range(last)])

        def aligned(head, shard, size):
            both = jnp.concatenate([head, shard], axis=0)
            return lax.dynamic_slice_in_dim(both, count - here.owner, size, 0)

        before, x_sent = stage((before, chip_blocks(plan, position, images)))
        x_got = to_chips(plan, x_sent)
        x_got[1], before, later, core, band_rows = stage((x_got[1], before, position, here.core, band_rows))
        block = aligned(before, shard16, rows - 1)
        gather = Gather(jnp.concatenate([block, shard16[singles : singles + 16]], axis=0))
        values = gather.beside()
        tables = make_tables(plan, band_rows, later)
        values, x_got, tables, core, cots, params, first_moment, second_moment = stage(
            (values, x_got, tables, core, cots, params, first_moment, second_moment)
        )
        values = gather.first(values)
        values[3], core, later, cots = stage((values[3], core, position, cots))
        cot_sent = chip_blocks(plan, later, cots)
        table = gather_table(here, core, lambda z, place: [(8 * z + place) * 22])
        values, x_blocks, cot_sent, table = stage((values, to_cores(plan, x_got), cot_sent, table))
        values = gather.second(values)
        values[6], params, first_moment, second_moment, later = stage(
            (values[6], params, first_moment, second_moment, here.owner)
        )
        state = (params, first_moment, second_moment)
        far = [lax.dynamic_slice_in_dim(rows_of, 176 - later, 176, 0).astype(BF16) for rows_of in state]
        head = jnp.concatenate([rows_of[rows - count :] for rows_of in state], axis=1)
        near = [rows_of[:176] for rows_of in state]
        single_state = [rows_of[singles : singles + 16] for rows_of in state]
        table_again = gather_table(
            here,
            core,
            lambda z, place: [
                (8 * (z & 1) + place) * 22 + jnp.where(z < 2, 0, 11),
                (8 * (z | 2) + place) * 22 + jnp.where(z < 2, 11, 0),
            ],
        )
        values, others, far, head, near, single_state, table_again = stage(
            (
                values,
                gather.others(values, 4),
                jnp.concatenate(far, axis=1),
                head,
                near,
                single_state,
                table_again,
            )
        )
        values, more = stage((gather.third(values), gather.others(values[4:], 6)))
        cot_sent, values = stage((cot_sent, values))
        cot_got = to_chips(plan, cot_sent)
        pieces, parts = gather.pieces(values, others + more + gather.others(values[10:], 6)), ((0, rows - 1),)
        pieces, x_blocks = stage((pieces, x_blocks))
    else:
        pieces, parts = [lax.all_gather(params.astype(BF16), AXES, axis=0, tiled=True)], ((0, rows),)
        table = jnp.zeros((2,), jnp.int32)
        tables = make_tables(plan, band_rows, position)
        x_blocks = to_cores(plan, to_chips(plan, chip_blocks(plan, position, images)))
        cot_got = to_chips(plan, chip_blocks(plan, position, cots))
    x_img, a1, h1, a2, y, z, q, k, v, stats, small, weights = run_features(
        True, plan, tables, x_blocks, pieces, parts, table
    )
    cot_got, y = stage((cot_got, y))
    cot_blocks = to_cores(plan, cot_got)
    if here.planes:
        cot_blocks, far = stage((cot_blocks, far))
        far = over_two_planes(far)
    out_own, out_oth, dy, dy16, g_proj, sums3 = run_attend_both(
        plan, tables, q, k, v, y, z, cot_blocks, stats, small, weights
    )
    if here.planes:

        def stepped(state, grad):
            update, _, _ = adam(*state, grad, step_count, step_rate)
            return (state[0] - update).astype(BF16)

        dy16, far, out_oth = stage((dy16, far, out_oth))
        out_got = over_core(out_oth)
        *kept, early, sums_b2 = run_weight_grad(tables, 1, a2, dy16, g_proj)
        kept, sent = kept[:2], kept[2:]
        dy16, kept, sent, out_got = stage((dy16, kept, sent, out_got))
        got = [over_core(value) for value in sent]
        out_got = from_chips(plan, merge_cores(plan, position, out_own, out_got))
        dy16, kept, got, halves = stage((dy16, kept, got, halves_to_send(here, kept, got)))
        halves = send_halves(*halves)
        dh1, sums_n2 = run_data_grad(tables, 1, dy16, h1, stats, small, weights)
        dh1, kept, got, halves = stage((dh1, kept, got, halves))
        high = kept, got
        *kept, sums_b1 = run_weight_grad(tables, 0, a1, dh1, early)
        kept, sent = kept[:2], kept[2:]
        kept, sent, high, halves, out_got = stage((kept, sent, high, halves, out_got))
        got = [over_core(value) for value in sent]
        high = add_halves(here, *high, *halves)
        quarters = send_quarters(*quarters_to_send(here, *high))
        low = kept, got
        low, halves, high, quarters, dh1 = stage((low, halves_to_send(here, *low), high, quarters, dh1))
        halves = send_halves(*halves)
        high = by_plane(False, *add_quarters(here, *high, *quarters))
        high, dh1 = stage((high, dh1))
        high_got = send_planes(here, high)
        dx_own, dx_oth, sums_n1 = run_data_grad(
            tables, 0, dh1, x_img, stats, small, weights, dy=dy, half=out_own.shape[0]
        )
        low, halves, high, high_got, sums_n1 = stage((low, halves, high, high_got, sums_n1))
        low = add_halves(here, *low, *halves)
        sums = sums_n1 + sums_b1 + sums_n2 + sums_b2 + sums3
        low, low_sent, sums = stage((low, quarters_to_send(here, *low), sums + over_core(sums)))
        quarters = send_quarters(*low_sent)
        small_sum = sum_over_img(sums)
        low, quarters, small_sum, head = stage((low, quarters, small_sum, head))
        before = lax.ppermute(head, AXES, [(o, o + 1) for o in range(last)])
        low = by_plane(True, *add_quarters(here, *low, *quarters))
        low_got = send_planes(here, low, small_sum)
        low, low_got, before, far, high, high_got = stage((low, low_got, before, far, high, high_got))
        low, high = add_planes(here, low, low_got, small_sum), add_planes(here, high, high_got)
        low, small_sum = low[:176], low[176:]
        own = [
            aligned(before[:, i * C : (i + 1) * C], rows_of, 176) for i, rows_of in enumerate(near)
        ]
        far = [far[:, i * C : (i + 1) * C].astype(F32) for i in range(3)]
        first_two = here.z < 2
        block = [
            stepped([jnp.where(first_two, a, b) for a, b in zip(own, far)], low),
            stepped([jnp.where(first_two, b, a) for a, b in zip(own, far)], high),
            stepped(single_state, small_sum),
        ]
        gather = Gather(jnp.concatenate(block, axis=0))
        values, dx_got = stage((gather.first(), over_core(dx_oth)))
        dx_sent = merge_cores(plan, position, dx_own, dx_got)
        values, others, dx_sent, first_out = stage(
            (gather.second(values), gather.others(values, 4), dx_sent, to_bands(plan, position, out_got))
        )
        values, more = stage((gather.third(values), gather.others(values[4:], 6)))
        pieces = gather.pieces(values, others + more + gather.others(values[10:], 6))
        pieces, dx_sent = stage((pieces, dx_sent))
        dx_got = from_chips(plan, dx_sent)
        far = over_two_planes(jnp.where(here.z < 2, high, low).astype(BF16))
        table = table_again
        parts = ((0, 176), (176, 176))
    else:
        out_got = from_chips(plan, merge_cores(plan, position, out_own, over_core(out_oth)))
        g_w2, sums_b2 = run_weight_grad(tables, 1, a2, dy16)
        dh1, sums_n2 = run_data_grad(tables, 1, dy16, h1, stats, small, weights)
        g_w1, sums_b1 = run_weight_grad(tables, 0, a1, dh1)
        dx_own, dx_oth, sums_n1 = run_data_grad(
            tables, 0, dh1, x_img, stats, small, weights, dy=dy, half=out_own.shape[0]
        )
        dx_got = from_chips(plan, merge_cores(plan, position, dx_own, over_core(dx_oth)))
        small_rows = sums_n1 + sums_b1 + sums_n2 + sums_b2 + sums3
        full = jnp.concatenate([g_w1, g_w2, g_proj, small_rows.astype(BF16)], axis=0)
        full = jnp.pad(full, ((0, rows * count - full.shape[0]), (0, 0)))
        grad = lax.psum_scatter(full, AXES, scatter_dimension=0, tiled=True).astype(F32)
        weight_update, new_first, new_second = adam(
            params, first_moment, second_moment, grad, step_count, step_rate
        )
        pieces = [lax.all_gather((params - weight_update).astype(BF16), AXES, axis=0, tiled=True)]
    again_own, again_oth = run_features(False, plan, tables, (x_img, stats), pieces, parts, table)
    if here.planes:
        again_own, again_oth, dx_got, far = stage((again_own, again_oth, dx_got, far))
    again = from_chips(plan, merge_cores(plan, position, again_own, over_core(again_oth)))
    if here.planes:
        mine = jnp.concatenate([jnp.where(here.z < 2, low, high), far.astype(F32)], axis=0)
        follow = lax.ppermute(mine[:count], AXES, [(o, o - 1) for o in range(1, count)])
        follow, dx_got = stage((follow, dx_got))
        follow = jnp.where(here.owner == last, jnp.pad(small_sum, ((0, count - 16), (0, 0))), follow)
        grad = lax.dynamic_slice_in_dim(jnp.concatenate([mine, follow], axis=0), here.owner, rows, 0)
        weight_update, new_first, new_second = adam(
            params, first_moment, second_moment, grad, step_count, step_rate
        )
    else:
        first_out = to_bands(plan, position, out_got)
    input_grads = to_bands(plan, position, dx_got)
    second_out = to_bands(plan, position, again)
    return (*first_out, *second_out, *input_grads, weight_update, new_first, new_second)


def solution(mesh):
    image = P("img", "band", None, None)
    shard = P(("band", "img"), None)
    return jax.shard_map(
        body,
        mesh=mesh,
        in_specs=(image,) * 6 + (P(),) + (shard,) * 3 + (P(), P()),
        out_specs=(image,) * 9 + (shard,) * 3,
        check_vma=False,
    )
```

```python
import functools

import jax
import jax.numpy as jnp
import numpy as np
from jax import lax
from jax.experimental import pallas as pl
from jax.experimental.pallas import tpu as pltpu
from jax.sharding import PartitionSpec as P

GROUPS = 32
EPSILON = 1e-05
ADAM_EPSILON = 1e-08
C = 512
AXES = ("band", "img")
VMEM_MARGIN = 6 * 1024 * 1024
VMEM_MOST = 58 * 1024 * 1024
F32, BF16 = jnp.float32, jnp.bfloat16

PIX = 1024
SEG_LINES = ((0, 24), (24, 32))
BUF_LINES = 36


class Plan:
    def __init__(self, shapes, n_band):
        (self.n_s, self.cap_s, self.side_s, _), (self.n_m, self.cap_m, self.side_m, _), (
            self.n_l,
            self.cap_l,
            self.side_l,
            _,
        ) = shapes
        assert (self.side_s, self.side_m, self.side_l) == (16, 24, 32)
        self.n_band = n_band
        self.n_chip = n_band // 2
        self.r_s, self.r_m, self.r_l = (
            self.cap_s * self.side_s,
            self.cap_m * self.side_m,
            self.cap_l * self.side_l,
        )
        holders = [dict() for _ in range(n_band)]
        for i in range(self.n_l):
            holders[2 * i]["l"] = i
        free = [b for b in range(n_band) if "l" not in holders[b]]
        for i in range(self.n_m):
            holders[free[i]]["m"] = i
        spots = [b for b in free if b >= 2 * self.n_l]
        for i in range(self.n_s):
            holders[spots[i]]["s"] = i
        self.holders = holders
        self.sizes = [
            (self.r_l if "l" in h else 0)
            + (self.r_m if "m" in h else 0)
            + (self.r_s if "s" in h else 0)
            for h in holders
        ]
        self.block = max(self.sizes[2 * j] + self.sizes[2 * j + 1] for j in range(self.n_chip))
        self.piece = max(self.sizes)
        self.offs = [0 if b % 2 == 0 else self.piece - self.sizes[b] for b in range(n_band)]
        rows, flags = [], []
        for b, h in enumerate(holders):
            large, middle, small = int("l" in h), int("m" in h), int("s" in h)
            rows.append([large, middle, small, self.offs[b]])
            flags.append([large, 32 if large else 24 * middle, 32 if large else 32 * small, 16 - 16 * large, b % 2])
        self.rows, self.flags = np.array(rows, np.int32), np.array(flags, np.int32)


def pick(table, index):
    return lax.dynamic_index_in_dim(jnp.asarray(table), index, 0, keepdims=False)


def make_tables(plan, band_rows, position):
    nz = plan.n_chip
    z, core = position // 2, position % 2
    own = pick(plan.rows, position)
    is_l, has_m, has_s, off = own[0], own[1], own[2], own[3]
    starts = jnp.cumsum(band_rows, axis=1) - band_rows
    zero_in = plan.n_band * plan.piece // 8

    def band_of(member, rows):
        return jnp.sum((starts[member][None, :] <= rows[:, None]).astype(jnp.int32), axis=1) - 1

    def place(member, rows):
        band = band_of(member, rows)
        onehot = band[:, None] == jnp.arange(plan.n_band)[None, :]
        start = jnp.sum(jnp.where(onehot, starts[member][None, :], 0), axis=1)
        k = (z - band // 2) % nz
        pos = jnp.where(band % 2 == core, k, nz + k)
        return pos * plan.piece + off, rows - start

    q = np.arange(128)
    base, r = place(2, jnp.asarray(q // 4, jnp.int32))
    src_l = (base + r * 32) // 8 + jnp.asarray(q % 4, jnp.int32)
    base, r = place(1, jnp.asarray(np.minimum(q // 4, 23), jnp.int32))
    src_m = (base + r * 24) // 8 + jnp.asarray(q % 4, jnp.int32)
    ok_m = jnp.asarray((q < 96) & (q % 4 < 3)) & (has_m == 1)
    line = np.clip((q - 96) // 4, 0, 7)
    base, r = place(0, jnp.asarray(line + 8 * (q % 4 // 2), jnp.int32))
    src_s = (base + has_m * plan.r_m + r * 16) // 8 + jnp.asarray(q % 2, jnp.int32)
    ok_s = jnp.asarray(q >= 96) & (has_s == 1)
    gather = jnp.where(
        is_l == 1, src_l, jnp.where(ok_m, src_m, jnp.where(ok_s, src_s, zero_in))
    ).astype(jnp.int32)

    per = plan.piece // 8
    p, t = np.divmod(np.arange(plan.n_band * per), per)
    k = jnp.asarray(p % nz, jnp.int32)
    c_src = jnp.where(jnp.asarray(p < nz), core, 1 - core)
    band = 2 * ((z - k) % nz) + c_src
    onehot = band[:, None] == jnp.arange(plan.n_band)[None, :]

    def of_band(row):
        return jnp.sum(jnp.where(onehot, row[None, :], 0), axis=1)

    within = jnp.asarray(t * 8, jnp.int32) - off
    wl = jnp.maximum(within, 0)
    r = wl // 32
    ok_l = (within >= 0) & (r < of_band(band_rows[2]))
    out_l = (of_band(starts[2]) + r) * 4 + wl % 32 // 8
    r = wl // 24
    in_m = (has_m == 1) & (wl < plan.r_m)
    ok_m = (within >= 0) & in_m & (r < of_band(band_rows[1]))
    out_m = (of_band(starts[1]) + r) * 4 + wl % 24 // 8
    ws = jnp.maximum(wl - has_m * plan.r_m, 0)
    r = ws // 16
    h = of_band(starts[0]) + r
    ok_s = (within >= 0) & (has_s == 1) & ~in_m & (r < of_band(band_rows[0]))
    out_s = 96 + (h % 8) * 4 + (h // 8) * 2 + ws % 16 // 8
    scatter = jnp.where(
        is_l == 1,
        jnp.where(ok_l, out_l, 128),
        jnp.where(ok_m, out_m, jnp.where(ok_s, out_s, 128)),
    ).astype(jnp.int32)
    flags = pick(plan.flags, position)
    return gather, scatter, flags


class Scalars:
    def __init__(self, flags):
        self.is_l = flags[0]
        self.lims = (flags[1], flags[2])
        self.split = flags[3]
        self.core = flags[4]
        self.l_f = flags[0].astype(F32)
        large = flags[0] == 1
        self.inv = (
            jnp.where(large, 1.0 / (1024 * 16), 1.0 / (576 * 16)).astype(F32),
            jnp.where(large, 1.0 / (1024 * 16), 1.0 / (256 * 16)).astype(F32),
        )


def dot(a, b):
    return jnp.dot(a, b, preferred_element_type=F32)


def dot_nt(a, b):
    return lax.dot_general(a, b, (((1,), (1,)), ((), ())), preferred_element_type=F32)


def dot_tn(a, b):
    return lax.dot_general(a, b, (((0,), (0,)), ((), ())), preferred_element_type=F32)


def line_rows(line):
    return pl.ds(pl.multiple_of(line * 32, 32), 32)


def line_loop(body, carries, unroll=2):
    results = []
    for seg, (low, high) in enumerate(SEG_LINES):
        results.append(
            lax.fori_loop(
                low, high, lambda line, carry, seg=seg: body(seg, line, carry), carries[seg], unroll=unroll
            )
        )
    return results


def fold(value):
    return value.reshape(4, 8, C).sum(axis=0)


def columns():
    return lax.broadcasted_iota(jnp.int32, (32, C), 0)


def fill_group_matrix(gm_ref):
    row = lax.broadcasted_iota(jnp.int32, (C, C), 0) // (C // GROUPS)
    col = lax.broadcasted_iota(jnp.int32, (C, C), 1) // (C // GROUPS)
    gm_ref[...] = (row == col).astype(F32).astype(BF16)


def group_totals(gm_ref, scal, per_seg):
    stacked = jnp.concatenate(list(per_seg) + [jnp.zeros((8 - len(per_seg), C), F32)], axis=0)
    hi = stacked.astype(BF16)
    rest = stacked - hi.astype(F32)
    mid = rest.astype(BF16)
    low = (rest - mid.astype(F32)).astype(BF16)
    both = dot(jnp.concatenate([hi, mid, low, jnp.zeros((8, C), BF16)], axis=0), gm_ref[...])
    total = both[0:8] + both[8:16] + both[16:24]
    out = []
    for i in range(0, len(per_seg), 2):
        first, second = total[i : i + 1], total[i + 1 : i + 2]
        out.append((first + scal.l_f * second, second + scal.l_f * first))
    return out


def norm_stats(read, gm_ref, scal, sums=None):
    zero = jnp.zeros((8, C), F32)
    if sums is None:
        sums = line_loop(lambda seg, line, acc: acc + fold(read(line)), (zero, zero))
    sums = [s.sum(axis=0, keepdims=True) for s in sums]
    (totals,) = group_totals(gm_ref, scal, sums)
    means = [totals[seg] * scal.inv[seg] for seg in range(2)]
    col = columns()

    def squares(seg, line, acc):
        dev = jnp.where(col < scal.lims[seg], read(line) - means[seg], 0.0)
        return acc + fold(dev * dev)

    sums = line_loop(squares, (zero, zero))
    sums = [s.sum(axis=0, keepdims=True) for s in sums]
    (totals,) = group_totals(gm_ref, scal, sums)
    rstds = [lax.rsqrt(totals[seg] * scal.inv[seg] + EPSILON) for seg in range(2)]
    return means, rstds


def store_shifted(buf_ref, scal, seg, line, value16):
    col = columns()
    value = value16.astype(F32)
    keep_left, keep_right = col != 0, col != 31
    if seg == 1:
        keep_left &= col != scal.split
        keep_right &= col != scal.split - 1
    left = jnp.where(keep_left, pltpu.roll(value, 1, 0), 0.0).astype(BF16)
    right = jnp.where(keep_right, pltpu.roll(value, 31, 0), 0.0).astype(BF16)
    at = line_rows(line + (1 if seg == 0 else 3))
    buf_ref[at, 0:C] = left
    buf_ref[at, C : 2 * C] = value16
    buf_ref[at, 2 * C : 3 * C] = right


def fill_halos(buf_ref, scal):
    zero = jnp.zeros((32, 3 * C), BF16)
    buf_ref[0:32, :] = zero
    buf_ref[25 * 32 : 26 * 32, :] = zero
    buf_ref[26 * 32 : 27 * 32, :] = zero
    buf_ref[35 * 32 : 36 * 32, :] = zero

    @pl.when(scal.is_l == 1)
    def _():
        buf_ref[25 * 32 : 26 * 32, :] = buf_ref[27 * 32 : 28 * 32, :]
        buf_ref[26 * 32 : 27 * 32, :] = buf_ref[24 * 32 : 25 * 32, :]

    @pl.when(scal.is_l == 0)
    def _():
        buf_ref[26 * 32 + 16 : 27 * 32, :] = buf_ref[34 * 32 : 34 * 32 + 16, :]
        buf_ref[35 * 32 : 35 * 32 + 16, :] = buf_ref[27 * 32 + 16 : 28 * 32, :]


def tile_at(tile):
    return pl.ds(pl.multiple_of(tile * 256, 256), 256)


def tile_rows(tile, shift):
    line = 8 * tile + jnp.where(tile == 3, 2, 0) + shift
    return pl.ds(pl.multiple_of(line * 32, 32), 256)


def tile_loop(body, unroll=2):
    def step(tile, carry):
        body(tile)
        return carry

    lax.fori_loop(0, 4, step, 0, unroll=unroll)


def conv_tiles(buf_ref, w_ref, out_ref):
    def body(tile):
        acc = None
        for shift in range(3):
            term = dot(buf_ref[tile_rows(tile, shift), :], w_ref[shift * 3 * C : (shift + 1) * 3 * C, :])
            acc = term if acc is None else acc + term
        out_ref[tile_at(tile), :] = acc

    tile_loop(body, 4)


def gather_pieces(table_ref, src_ref, dst_ref, count):
    def step(i, carry):
        at = pl.multiple_of(table_ref[i] * 8, 8)
        dst_ref[pl.ds(pl.multiple_of(i * 8, 8), 8), :] = src_ref[pl.ds(at, 8), :]
        return carry

    lax.fori_loop(0, count, step, 0, unroll=4)


def slots_to_image(table_ref, scal, blocks, slots_ref, image_ref):
    piece = (slots_ref.shape[0] - 8) // len(blocks)
    start = pl.multiple_of((blocks[0].shape[0] - piece) * scal.core, 16)
    for i, block in enumerate(blocks):
        slots_ref[i * piece : (i + 1) * piece, :] = block[pl.ds(start, piece), :].astype(F32)
    slots_ref[len(blocks) * piece :, :] = jnp.zeros((8, C), F32)
    gather_pieces(table_ref, slots_ref, image_ref, 128)


def image_to_slots(table_ref, image_ref, slots_ref, own_ref, oth_ref):
    half = own_ref.shape[0]
    gather_pieces(table_ref, image_ref, slots_ref, 2 * half // 8)
    own_ref[...] = slots_ref[0:half, :].astype(BF16)
    oth_ref[...] = slots_ref[half : 2 * half, :].astype(BF16)


def swish_slope(value):
    sigma = jax.nn.sigmoid(value)
    return sigma * (1.0 + value * (1.0 - sigma))


def load_weights(pieces, parts, table, w, small16, sems):
    last = len(parts) * len(pieces)
    if len(pieces) == 1:
        copies = [[pltpu.make_async_copy(pieces[0].at[pl.ds(0, 22 * C)], w, sems.at[0])]]
        copy = pltpu.make_async_copy(pieces[0].at[pl.ds(22 * C, 16)], small16, sems.at[1])
        copy.start()
        copies[0][0].start()
        copy.wait()
    else:
        for i, piece in enumerate(pieces):

            @pl.when(table[last] == i)
            def _():
                pltpu.make_async_copy(
                    piece.at[pl.ds(parts[-1][0] + parts[-1][1], 16)], small16, sems.at[last]
                ).start()

        copies = []
        for p, (start, count) in enumerate(parts):
            copies.append([])
            for i, piece in enumerate(pieces):
                e = i * len(parts) + p
                at = pl.multiple_of(table[e] * 16, 16)
                copy = pltpu.make_async_copy(
                    piece.at[pl.ds(start, count)], w.at[pl.ds(at, count)], sems.at[e]
                )
                copy.start()
                copies[p].append(copy)
        pltpu.make_async_copy(pieces[0].at[pl.ds(0, 16)], small16, sems.at[last]).wait()

    def wait(p):
        if p < len(copies):
            for copy in copies[p]:
                copy.wait()

    return wait


def features_kernel(first, sources, count, parts, *refs):
    if first:
        gather, flags, table = refs[:3]
        blocks, refs = refs[3 : 3 + sources], refs[3 + sources :]
        pieces, refs = refs[:count], refs[count:]
        x_out, a1_out, h1_out, a2_out, y_ref, z_out, q_ref, k_ref, v_ref, stats, small, w_out = refs[:12]
        slots, x_ref, h_ref, z_ref, buf, w, gm, sems, small16, a1, h1, a2, x16, out_sems = refs[12:]
    else:
        scatter, flags, table, x_in, stats = refs[:5]
        pieces, refs = refs[5 : 5 + count], refs[5 + count :]
        own_out, oth_out = refs[:2]
        slots, x_ref, h_ref, z_ref, buf, w, gm, sems, small16, small, y_ref, q_ref, k_ref, v_ref = refs[2:]
    wait_weights = load_weights(pieces, parts, table, w, small16, sems)
    scal = Scalars(flags)
    fill_group_matrix(gm)
    small[...] = small16[...].astype(F32)
    col = columns()
    saves = []

    def save(value, out):
        if first:
            copy = pltpu.make_async_copy(value, out, out_sems.at[len(saves)])
            copy.start()
            saves.append(copy)

    def row(i):
        return small[i : i + 1, :]

    def activate(read, means, rstds, gain, shift, keep):
        def body(seg, line, carry):
            normed = (read(line) - means[seg]) * rstds[seg] * gain + shift
            act = jnp.where(col < scal.lims[seg], normed * jax.nn.sigmoid(normed), 0.0).astype(BF16)
            if keep is not None:
                keep[line_rows(line), :] = act
            store_shifted(buf, scal, seg, line, act)
            return carry

        line_loop(body, (0, 0))
        fill_halos(buf, scal)

    def read_x(line):
        return x_ref[line_rows(line), :]

    if first:
        slots_to_image(gather, scal, blocks, slots, x_ref)
        means1, rstds1 = norm_stats(read_x, gm, scal)

        def keep_x(seg, line, carry):
            x16[line_rows(line), :] = read_x(line).astype(BF16)
            return carry

        line_loop(keep_x, (0, 0))
        save(x16, x_out)
    else:

        def widen_x(seg, line, carry):
            x_ref[line_rows(line), :] = x_in[line_rows(line), :].astype(F32)
            return carry

        line_loop(widen_x, (0, 0))
        means1, rstds1 = [stats[0:1, :], stats[1:2, :]], [stats[2:3, :], stats[3:4, :]]
    activate(read_x, means1, rstds1, row(0), row(1), a1 if first else None)
    if first:
        save(a1, a1_out)
    wait_weights(0)
    if first:
        save(w, w_out)

    conv_tiles(buf, w.at[0 : 9 * C], h_ref)

    def finish_h(seg, line, carry):
        value = jnp.where(col < scal.lims[seg], h_ref[line_rows(line), :] + row(2), 0.0)
        h_ref[line_rows(line), :] = value
        if first:
            h1[line_rows(line), :] = value
        return carry + fold(value)

    zero = jnp.zeros((8, C), F32)

    def read_h(line):
        return h_ref[line_rows(line), :]

    means2, rstds2 = norm_stats(read_h, gm, scal, line_loop(finish_h, (zero, zero)))
    if first:
        save(h1, h1_out)
    activate(read_h, means2, rstds2, row(3), row(4), a2 if first else None)
    if first:
        save(a2, a2_out)
    wait_weights(1)
    conv_tiles(buf, w.at[9 * C : 18 * C], h_ref)

    def finish_y(seg, line, carry):
        value = jnp.where(
            col < scal.lims[seg], read_x(line) + (h_ref[line_rows(line), :] + row(5)), 0.0
        )
        y_ref[line_rows(line), :] = value
        return carry + fold(value)

    def read_y(line):
        return y_ref[line_rows(line), :]

    means3, rstds3 = norm_stats(read_y, gm, scal, line_loop(finish_y, (zero, zero)))

    def third(seg, line, carry):
        normed = (read_y(line) - means3[seg]) * rstds3[seg] * row(6) + row(7)
        z_ref[line_rows(line), :] = jnp.where(col < scal.lims[seg], normed, 0.0).astype(BF16)
        return carry

    line_loop(third, (0, 0))
    if first:
        save(z_ref, z_out)

    def project(tile):
        at = tile_at(tile)
        rows = z_ref[at, :]
        q_ref[at, :] = (dot(rows, w[18 * C : 19 * C, :]) + row(8)).astype(BF16)
        k_ref[at, :] = dot(rows, w[19 * C : 20 * C, :]).astype(BF16)
        v_ref[at, :] = (dot(rows, w[20 * C : 21 * C, :]) + row(9)).astype(BF16)

    tile_loop(project)
    if first:
        for i, pair in enumerate((means1, rstds1, means2, rstds2, means3, rstds3)):
            stats[2 * i : 2 * i + 1, :] = pair[0]
            stats[2 * i + 1 : 2 * i + 2, :] = pair[1]
        stats[12:16, :] = jnp.zeros((4, C), F32)
        for copy in saves:
            copy.wait()
        return
    bias = key_bias(scal)

    def attend(tile):
        at = tile_at(tile)
        prob = probabilities(q_ref[at, :], k_ref, bias(tile)).astype(BF16)
        mixed = dot(prob, v_ref[...]).astype(BF16)
        y_ref[at, :] = y_ref[at, :] + (dot(mixed, w[21 * C : 22 * C, :]) + row(10))

    tile_loop(attend)
    y_ref[PIX : PIX + 8, :] = jnp.zeros((8, C), F32)
    image_to_slots(scatter, y_ref, slots, own_out, oth_out)


def key_bias(scal):
    key = lax.broadcasted_iota(jnp.int32, (1, PIX), 1)
    column = key % 32
    in0 = key < 768
    ok0 = in0 & (column < scal.lims[0])
    ok1 = (~in0) & (column < scal.lims[1])
    large = scal.is_l == 1
    row0 = jnp.where(ok0 | (ok1 & large), 0.0, -1e30).astype(F32)
    row1 = jnp.where(ok1 | (ok0 & large), 0.0, -1e30).astype(F32)
    return lambda tile: jnp.where(tile == 3, row1, row0)


def probabilities(q, k_ref, bias):
    scores = dot_nt(q, k_ref[...]) * (C**-0.5) + bias
    top = jnp.max(scores, axis=1, keepdims=True)
    expo = jnp.exp(scores - top)
    return expo * (1.0 / jnp.sum(expo, axis=1, keepdims=True))


def attend_both_kernel(
    gather,
    scatter,
    flags,
    q,
    k,
    v,
    y,
    z,
    stats,
    small,
    weights,
    *refs,
):
    blocks = refs[:-23]
    own_out, oth_out, dy_out, dy16_out, grads_out, sums_out = refs[-23:-17]
    image, slots, g_ref, o_ref, d_ref, dk_acc, dv_acc, wp, gm, sems = refs[-17:-7]
    loaded = [
        (weights.at[pl.ds(18 * C, 4 * C)], wp),
        (q, refs[-7]),
        (k, refs[-6]),
        (v, refs[-5]),
        (y, refs[-4]),
        (z, refs[-3]),
    ]
    loads = [pltpu.make_async_copy(a, b, sems.at[i]) for i, (a, b) in enumerate(loaded)]
    for load in loads:
        load.start()
    q, k, v, y, z, grads, own_rows = refs[-7:]
    oth_rows = own_rows.at[pl.ds(own_out.shape[0], own_out.shape[0])]
    own_rows = own_rows.at[pl.ds(0, own_out.shape[0])]
    stores = [(own_rows, own_out), (oth_rows, oth_out), (grads, grads_out)]
    stores = [pltpu.make_async_copy(a, b, sems.at[6 + i]) for i, (a, b) in enumerate(stores)]
    scal = Scalars(flags)
    fill_group_matrix(gm)
    bias = key_bias(scal)
    slots_to_image(gather, scal, blocks, slots, g_ref)
    for load in loads[:5]:
        load.wait()
    scaling = C**-0.5
    dk_acc[...] = jnp.zeros(MAP, F32)
    dv_acc[...] = jnp.zeros(MAP, F32)

    def attend(tile):
        at = tile_at(tile)
        q_t = q[at, :]
        prob = probabilities(q_t, k, bias(tile))
        prob16 = prob.astype(BF16)
        mixed = dot(prob16, v[...]).astype(BF16)
        o_ref[at, :] = mixed
        image[at, :] = y[at, :] + (dot(mixed, wp[3 * C : 4 * C, :]) + small[10:11, :])
        d_mixed = dot_nt(g_ref[at, :].astype(BF16), wp[3 * C : 4 * C, :]).astype(BF16)
        d_prob = dot_nt(d_mixed, v[...])
        inner = jnp.sum(prob * d_prob, axis=1, keepdims=True)
        d_score = (prob * (d_prob - inner)).astype(BF16)
        d_ref[at, 0:C] = (scaling * dot(d_score, k[...])).astype(BF16)
        dk_acc[...] += dot_tn(d_score, q_t)
        dv_acc[...] += dot_tn(prob16, d_mixed)

    tile_loop(attend)
    d_ref[:, C : 2 * C] = (scaling * dk_acc[...]).astype(BF16)
    d_ref[:, 2 * C : 3 * C] = dv_acc[...].astype(BF16)
    image[PIX : PIX + 8, :] = jnp.zeros((8, C), F32)
    image_to_slots(scatter, image, slots, own_rows, oth_rows)
    stores[0].start()
    stores[1].start()
    loads[5].wait()
    for part in range(3):
        grads[part * C : (part + 1) * C, :] = dot_tn(z[...], d_ref[:, part * C : (part + 1) * C]).astype(
            BF16
        )
    grads[3 * C : 4 * C, :] = dot_tn(o_ref[...], g_ref[...].astype(BF16)).astype(BF16)
    stores[2].start()
    def back_to_norm(tile):
        at = tile_at(tile)
        acc = dot_nt(d_ref[at, 0:C], wp[0:C, :])
        acc = acc + dot_nt(d_ref[at, C : 2 * C], wp[C : 2 * C, :])
        image[at, :] = acc + dot_nt(d_ref[at, 2 * C : 3 * C], wp[2 * C : 3 * C, :])

    tile_loop(back_to_norm)
    col = columns()
    means = (stats[8:9, :], stats[9:10, :])
    rstds = (stats[10:11, :], stats[11:12, :])
    zero = jnp.zeros((8, C), F32)

    def sums(seg, line, acc):
        at = line_rows(line)
        d_norm = image[at, :]
        unit = (y[at, :] - means[seg]) * rstds[seg]
        d_all = d_ref[at, :].astype(F32)
        return (
            acc[0] + fold(d_norm),
            acc[1] + fold(d_norm * unit),
            acc[2] + fold(d_all[:, 0:C]),
            acc[3] + fold(d_all[:, 2 * C : 3 * C]),
            acc[4] + fold(g_ref[at, :]),
        )

    got = line_loop(sums, ((zero,) * 5, (zero,) * 5), unroll=1)
    got = [[part.sum(axis=0, keepdims=True) for part in seg] for seg in got]
    gain = small[6:7, :]
    ones, cross = group_totals(
        gm, scal, [got[0][0] * gain, got[1][0] * gain, got[0][1] * gain, got[1][1] * gain]
    )
    sums_out[...] = jnp.zeros((16, C), F32)
    for i, part in enumerate((1, 0, 2, 3, 4)):
        sums_out[6 + i : 7 + i, :] = got[0][part] + got[1][part]

    def back(seg, line, carry):
        at = line_rows(line)
        unit = (y[at, :] - means[seg]) * rstds[seg]
        d_in = rstds[seg] * (
            image[at, :] * gain - ones[seg] * scal.inv[seg] - unit * (cross[seg] * scal.inv[seg])
        )
        value = g_ref[at, :] + jnp.where(col < scal.lims[seg], d_in, 0.0)
        dy_out[at, :] = value
        dy16_out[at, :] = value.astype(BF16)
        return carry

    line_loop(back, (0, 0))
    for store in stores:
        store.wait()


def fill_gradient_buffer(buf, scal, grad_ref):
    def body(seg, line, carry):
        store_shifted(buf, scal, seg, line, grad_ref[line_rows(line), :])
        return carry

    line_loop(body, (0, 0))
    fill_halos(buf, scal)


def weight_grad_kernel(conv, split, *refs):
    if not split:
        flags, act, grad, w_out, sums_out, buf, act_t = refs
    else:
        flags, act, grad, more = refs[:4]
        planes, refs = refs[4:8], refs[8:]
        early_out = refs[0] if conv == 1 else None
        sums_out, buf, act_t, rows, sems = refs[conv:]
        kept, sent = planes[:2], planes[2:]
        offset = 2 * C if conv == 1 else 0
        more_at = 9 * C - offset
        load = pltpu.make_async_copy(more, rows.at[pl.ds(more_at, more.shape[0])], sems.at[4])
        load.start()
    scal = Scalars(flags)
    fill_gradient_buffer(buf, scal, grad)
    for tile in range(4):
        at = slice(tile * 256, (tile + 1) * 256)
        act_t[:, at] = act[at, :].T

    def send_out(run):
        plane, core = run // 2, run % 2
        source = rows.at[pl.ds(run * 1408, 1408)]

        @pl.when(scal.core == core)
        def _():
            pltpu.make_async_copy(source, kept[plane], sems.at[run]).start()

        @pl.when(scal.core != core)
        def _():
            pltpu.make_async_copy(source, sent[plane], sems.at[run]).start()

    ready = {0: (3,) if conv == 0 else (2, 3), 1: (2,) if conv == 0 else (1,), 2: (0, 1) if conv == 0 else (0,)}
    for shift in range(3):
        seg0 = slice(shift * 32, shift * 32 + 768)
        seg1 = slice((26 + shift) * 32, (26 + shift) * 32 + 256)
        for part in range(3):
            cols = slice(part * C, (part + 1) * C)
            value = dot(act_t[:, 0:768], buf[seg0, cols]) + dot(act_t[:, 768:1024], buf[seg1, cols])
            tap = 3 * (2 - shift) + (2 - part)
            if not split:
                w_out[tap * C : (tap + 1) * C, :] = value.astype(BF16)
            elif conv == 1 and tap < 2:
                early_out[tap * C : (tap + 1) * C, :] = value.astype(BF16)
            else:
                rows[tap * C - offset : (tap + 1) * C - offset, :] = value.astype(BF16)
        if split:
            if shift == 0:
                load.wait()
            for run in ready[shift]:
                send_out(run)
    zero = jnp.zeros((8, C), F32)
    got = line_loop(
        lambda seg, line, acc: acc + fold(grad[line_rows(line), :].astype(F32)), (zero, zero)
    )
    sums_out[...] = jnp.zeros((16, C), F32)
    sums_out[3 * conv + 2 : 3 * conv + 3, :] = (got[0] + got[1]).sum(axis=0, keepdims=True)
    if split:
        for run in range(4):
            pltpu.make_async_copy(rows.at[pl.ds(run * 1408, 1408)], kept[run // 2], sems.at[run]).wait()


def data_grad_kernel(last, conv, *refs):
    if last:
        scatter, flags, grad, feat, dy, stats, small, weights, own_out, oth_out, sums_out = refs[:11]
        dn, slots, buf, w, gm, sems, feat_v, dy_v = refs[11:]
    else:
        flags, grad, feat, stats, small, weights, grad_out, sums_out = refs[:8]
        dn, buf, w, gm, sems, feat_v = refs[8:]
    copies = [pltpu.make_async_copy(weights.at[pl.ds(conv * 9 * C, 9 * C)], w, sems.at[0])]
    copies.append(pltpu.make_async_copy(feat, feat_v, sems.at[1]))
    if last:
        copies.append(pltpu.make_async_copy(dy, dy_v, sems.at[2]))
        dy = dy_v
    feat = feat_v
    for copy in copies:
        copy.start()
    scal = Scalars(flags)
    fill_group_matrix(gm)
    fill_gradient_buffer(buf, scal, grad)
    copies[0].wait()

    def transposed(tile):
        acc = None
        for shift in range(3):
            for part in range(3):
                tap = 3 * (2 - shift) + (2 - part)
                term = dot_nt(
                    buf[tile_rows(tile, shift), part * C : (part + 1) * C], w[tap * C : (tap + 1) * C, :]
                )
                acc = term if acc is None else acc + term
        dn[tile_at(tile), :] = acc

    tile_loop(transposed)
    for copy in copies[1:]:
        copy.wait()
    base = 4 * conv
    means = (stats[base : base + 1, :], stats[base + 1 : base + 2, :])
    rstds = (stats[base + 2 : base + 3, :], stats[base + 3 : base + 4, :])
    gain, shift_row = small[3 * conv : 3 * conv + 1, :], small[3 * conv + 1 : 3 * conv + 2, :]
    col = columns()
    zero = jnp.zeros((8, C), F32)

    def sums(seg, line, acc):
        at = line_rows(line)
        unit = (feat[at, :].astype(F32) - means[seg]) * rstds[seg]
        value = dn[at, :] * swish_slope(unit * gain + shift_row)
        value = jnp.where(col < scal.lims[seg], value, 0.0)
        dn[at, :] = value
        return (acc[0] + fold(value), acc[1] + fold(value * unit))

    got = line_loop(sums, ((zero, zero), (zero, zero)))
    got = [[part.sum(axis=0, keepdims=True) for part in seg] for seg in got]
    ones, cross = group_totals(
        gm, scal, [got[0][0] * gain, got[1][0] * gain, got[0][1] * gain, got[1][1] * gain]
    )
    sums_out[...] = jnp.zeros((16, C), F32)
    sums_out[3 * conv : 3 * conv + 1, :] = got[0][1] + got[1][1]
    sums_out[3 * conv + 1 : 3 * conv + 2, :] = got[0][0] + got[1][0]

    def back(seg, line, carry):
        at = line_rows(line)
        unit = (feat[at, :].astype(F32) - means[seg]) * rstds[seg]
        value = rstds[seg] * (
            dn[at, :] * gain - ones[seg] * scal.inv[seg] - unit * (cross[seg] * scal.inv[seg])
        )
        value = jnp.where(col < scal.lims[seg], value, 0.0)
        if last:
            dn[at, :] = value + dy[at, :]
        else:
            grad_out[at, :] = value.astype(BF16)
        return carry

    line_loop(back, (0, 0))
    if last:
        dn[PIX : PIX + 8, :] = jnp.zeros((8, C), F32)
        image_to_slots(scatter, dn, slots, own_out, oth_out)


SMEM = pl.BlockSpec(memory_space=pltpu.SMEM)
VMEM = pl.BlockSpec(memory_space=pltpu.VMEM)
HBM = pl.BlockSpec(memory_space=pltpu.HBM)


def call(kernel, name, in_specs, outs, scratch, flops, args, out_specs=None, limit=None):
    moved = sum(int(np.prod(a.shape)) * a.dtype.itemsize for a in args)
    moved += sum(int(np.prod(s)) * jnp.dtype(d).itemsize for s, d in outs)
    out_specs = out_specs or [VMEM] * len(outs)
    held = [(a.shape, a.dtype) for a, spec in zip(args, in_specs) if spec is VMEM]
    held += [out for out, spec in zip(outs, out_specs) if spec is VMEM]
    held += [(s.shape, s.dtype) for s in scratch if s.memory_space == pltpu.VMEM]
    used = sum(int(np.prod(s)) * jnp.dtype(d).itemsize for s, d in held)
    return pl.pallas_call(
        kernel,
        name=name,
        out_shape=[jax.ShapeDtypeStruct(s, d) for s, d in outs],
        in_specs=in_specs,
        out_specs=out_specs,
        scratch_shapes=scratch,
        compiler_params=pltpu.CompilerParams(vmem_limit_bytes=limit or used + VMEM_MARGIN),
        cost_estimate=pl.CostEstimate(flops=int(flops), bytes_accessed=moved, transcendentals=0),
    )(*args)


MAP, SLOT_PAD = (PIX, C), 8
MICROSECOND = 1_100_000_000
BUF = pltpu.VMEM((BUF_LINES * 32, 3 * C), BF16)


def run_features(first, plan, tables, x, pieces, parts, table):
    gather, scatter, flags = tables
    slot_rows = plan.n_band * plan.piece
    count = len(pieces)
    scratch = [
        pltpu.VMEM((slot_rows + SLOT_PAD, C), F32),
        pltpu.VMEM(MAP, F32),
        pltpu.VMEM(MAP, F32),
        pltpu.VMEM(MAP, BF16),
        BUF,
        pltpu.VMEM((22 * C, C), BF16),
        pltpu.VMEM((C, C), BF16),
        pltpu.SemaphoreType.DMA((len(parts) * count + 1,)),
        pltpu.VMEM((16, C), BF16),
    ]
    if first:
        outs = [
            (MAP, BF16),
            (MAP, BF16),
            (MAP, F32),
            (MAP, BF16),
            (MAP, F32),
            (MAP, BF16),
            (MAP, BF16),
            (MAP, BF16),
            (MAP, BF16),
            ((16, C), F32),
            ((16, C), F32),
            ((22 * C, C), BF16),
        ]
        return call(
            functools.partial(features_kernel, True, len(x), count, parts),
            "features_first",
            [SMEM] * 3 + [VMEM] * len(x) + [HBM] * count,
            outs,
            scratch
            + [
                pltpu.VMEM(MAP, BF16),
                pltpu.VMEM(MAP, F32),
                pltpu.VMEM(MAP, BF16),
                pltpu.VMEM(MAP, BF16),
                pltpu.SemaphoreType.DMA((6,)),
            ],
            26 * MICROSECOND,
            (gather, flags, table, *x, *pieces),
            out_specs=[HBM] * 4 + [VMEM, HBM] + [VMEM] * 5 + [HBM],
            limit=VMEM_MOST,
        )
    return call(
        functools.partial(features_kernel, False, 0, count, parts),
        "forward_again",
        [SMEM] * 3 + [VMEM] * 2 + [HBM] * count,
        [((slot_rows // 2, C), BF16)] * 2,
        scratch
        + [
            pltpu.VMEM((16, C), F32),
            pltpu.VMEM((PIX + 8, C), F32),
            pltpu.VMEM(MAP, BF16),
            pltpu.VMEM(MAP, BF16),
            pltpu.VMEM(MAP, BF16),
        ],
        28 * MICROSECOND,
        (scatter, flags, table, *x, *pieces),
        limit=VMEM_MOST,
    )


def run_attend_both(plan, tables, q, k, v, y, z, blocks, stats, small, weights):
    gather, scatter, flags = tables
    slot_rows = plan.n_band * plan.piece
    return call(
        attend_both_kernel,
        "attend_both",
        [SMEM] * 3 + [HBM] * 5 + [VMEM] * 2 + [HBM] + [VMEM] * len(blocks),
        [
            ((slot_rows // 2, C), BF16),
            ((slot_rows // 2, C), BF16),
            (MAP, F32),
            (MAP, BF16),
            ((4 * C, C), BF16),
            ((16, C), F32),
        ],
        [
            pltpu.VMEM((PIX + 8, C), F32),
            pltpu.VMEM((slot_rows + SLOT_PAD, C), F32),
            pltpu.VMEM(MAP, F32),
            pltpu.VMEM(MAP, BF16),
            pltpu.VMEM((PIX, 3 * C), BF16),
            pltpu.VMEM(MAP, F32),
            pltpu.VMEM(MAP, F32),
            pltpu.VMEM((4 * C, C), BF16),
            pltpu.VMEM((C, C), BF16),
            pltpu.SemaphoreType.DMA((9,)),
            pltpu.VMEM(MAP, BF16),
            pltpu.VMEM(MAP, BF16),
            pltpu.VMEM(MAP, BF16),
            pltpu.VMEM(MAP, F32),
            pltpu.VMEM(MAP, BF16),
            pltpu.VMEM((4 * C, C), BF16),
            pltpu.VMEM((slot_rows, C), BF16),
        ],
        24 * MICROSECOND,
        (gather, scatter, flags, q, k, v, y, z, stats, small, weights, *blocks),
        out_specs=[HBM] * 2 + [VMEM] * 2 + [HBM, VMEM],
        limit=VMEM_MOST,
    )


def run_weight_grad(tables, conv, act, grad, more=None):
    scratch = [BUF, pltpu.VMEM((C, PIX), BF16)]
    name = "weight_grad_one" if conv == 0 else "weight_grad_two"
    if more is None:
        return call(
            functools.partial(weight_grad_kernel, conv, False),
            name,
            [SMEM, VMEM, VMEM],
            [((9 * C, C), BF16), ((16, C), F32)],
            scratch,
            9 * MICROSECOND,
            (tables[2], act, grad),
        )
    early = [((2 * C, C), BF16)] if conv == 1 else []
    return call(
        functools.partial(weight_grad_kernel, conv, True),
        name,
        [SMEM, VMEM, VMEM, HBM],
        [((1408, C), BF16)] * 4 + early + [((16, C), F32)],
        scratch + [pltpu.VMEM((5632, C), BF16), pltpu.SemaphoreType.DMA((5,))],
        9 * MICROSECOND,
        (tables[2], act, grad, more),
        out_specs=[HBM] * 4 + [VMEM] * len(early) + [VMEM],
        limit=VMEM_MOST,
    )


def run_data_grad(tables, conv, grad, feat, stats, small, weights, dy=None, half=None):
    last = dy is not None
    scratch = [BUF, pltpu.VMEM((9 * C, C), BF16), pltpu.VMEM((C, C), BF16), pltpu.SemaphoreType.DMA((3,))]
    scratch.append(pltpu.VMEM(MAP, feat.dtype))
    if last:
        outs = [((half, C), BF16)] * 2
        scratch = [pltpu.VMEM((PIX + 8, C), F32), pltpu.VMEM((2 * half, C), F32)] + scratch
        scratch.append(pltpu.VMEM(MAP, F32))
        args = (tables[1], tables[2], grad, feat, dy, stats, small, weights)
        specs = [SMEM, SMEM, VMEM, HBM, HBM, VMEM, VMEM, HBM]
    else:
        outs = [(MAP, BF16)]
        scratch = [pltpu.VMEM(MAP, F32)] + scratch
        args = (tables[2], grad, feat, stats, small, weights)
        specs = [SMEM, VMEM, HBM, VMEM, VMEM, HBM]
    return call(
        functools.partial(data_grad_kernel, last, conv),
        "data_grad_one" if conv == 0 else "data_grad_two",
        specs,
        outs + [((16, C), F32)],
        scratch,
        12 * MICROSECOND,
        args,
        limit=VMEM_MOST,
    )


def z_shift(value, nz, k):
    return lax.ppermute(value, "band", [(2 * z + c, 2 * ((z + k) % nz) + c) for z in range(nz) for c in range(2)])


def core_swap(value, n_band):
    return lax.ppermute(value, "band", [(b, b ^ 1) for b in range(n_band)])


def stage(values):
    return lax.optimization_barrier(values)


def pack_slots(plan, arrays):
    flat = [a.reshape(a.shape[0], -1, C) for a in arrays]
    blocks = []
    for chip in range(plan.n_chip):
        parts = []
        for c in range(2):
            h = plan.holders[2 * chip + c]
            mine = [flat[m][h[name]] for m, name in ((2, "l"), (1, "m"), (0, "s")) if name in h]
            if c == 1:
                used = plan.sizes[2 * chip] + plan.sizes[2 * chip + 1]
                if used < plan.block:
                    parts.append(jnp.zeros((plan.block - used, C), BF16))
            parts += mine
        blocks.append(jnp.concatenate(parts, axis=0))
    return jnp.stack(blocks)


def chip_blocks(plan, position, arrays):
    z, nz = position // 2, plan.n_chip
    sent = pack_slots(plan, arrays)
    return [lax.dynamic_index_in_dim(sent, (z + k) % nz, 0, keepdims=False) for k in range(nz)]


def to_chips(plan, blocks):
    return [blocks[0]] + [z_shift(blocks[k], plan.n_chip, k) for k in range(1, plan.n_chip)]


def to_cores(plan, received):
    return [*received, *[core_swap(block, plan.n_band) for block in received]]


def merge_cores(plan, position, own, got):
    core, nz, slack = position % 2, plan.n_chip, plan.block - plan.piece
    own, got = own.reshape(nz, plan.piece, C), got.reshape(nz, plan.piece, C)
    first, second = jnp.where(core == 0, own, got), jnp.where(core == 0, got, own)
    return jnp.pad(first, ((0, 0), (0, slack), (0, 0))) + jnp.pad(second, ((0, 0), (slack, 0), (0, 0)))


def from_chips(plan, blocks):
    return [blocks[0]] + [z_shift(blocks[k], plan.n_chip, -k) for k in range(1, plan.n_chip)]


def to_bands(plan, position, received):
    z, nz, slack = position // 2, plan.n_chip, plan.block - plan.piece
    received = jnp.stack(received)
    images = [[None] * plan.n_s, [None] * plan.n_m, [None] * plan.n_l]
    for b, h in enumerate(plan.holders):
        chip = b // 2
        if not h:
            continue
        block = lax.dynamic_index_in_dim(received, (chip - z) % nz, 0, keepdims=False)
        at = plan.offs[b] + (slack if b % 2 else 0)
        for member, name, size in ((2, "l", plan.r_l), (1, "m", plan.r_m), (0, "s", plan.r_s)):
            if name in h:
                images[member][h[name]] = block[at : at + size]
                at += size
    sides = (plan.side_s, plan.side_m, plan.side_l)
    return [
        jnp.stack(images[m]).reshape(len(images[m]), -1, sides[m], C) for m in range(3)
    ]


class Place:
    def __init__(self):
        self.n_band, self.n_img = lax.axis_size("band"), lax.axis_size("img")
        self.count = self.n_band * self.n_img
        self.position, self.img = lax.axis_index("band"), lax.axis_index("img")
        self.owner = self.position * self.n_img + self.img
        self.z, self.core = self.position // 2, self.position % 2
        self.y, self.x = self.img // 2, self.img % 2
        self.planes = self.n_band == 8 and self.n_img == 4


def over_core(value):
    return core_swap(value, lax.axis_size("band"))


def over_x(value):
    return lax.ppermute(value, "img", [(i, i ^ 1) for i in range(4)])


def over_y(value):
    return lax.ppermute(value, "img", [(i, i ^ 2) for i in range(4)])


def along_z(value, pairs):
    return lax.ppermute(value, "band", [(2 * a + c, 2 * b + c) for a, b in pairs for c in range(2)])


def over_corner(value):
    return lax.ppermute(value, "img", [(i, i ^ 3) for i in range(4)])


class Gather:
    def __init__(self, block):
        self.block = block

    def beside(self):
        return [self.block, over_x(self.block), over_y(self.block)]

    def first(self, got=None):
        block, x0, y0 = got or self.beside()
        return [block, x0, y0, over_corner(block), z_shift(block, 4, 1), z_shift(block, 4, 3)]

    def second(self, values):
        block, x0, y0, d0, up, down = values
        across = z_shift(block, 4, 2)
        return values + [over_x(up), over_y(up), over_x(down), over_y(down), across]

    def third(self, values):
        d0, up, down, x1, y1, x3, y3, across = values[3:]
        return values + [over_x(across), over_y(across), z_shift(d0, 4, 2), over_y(x1), over_x(y3)]

    def others(self, values, count):
        return [over_core(value) for value in values[:count]]

    def pieces(self, values, others):
        def ordered(v):
            block, x0, y0, d0, up, down, x1, y1, x3, y3, across, x2, y2, d2, c1, c3 = v
            return [block, x0, y0, d0, up, x1, y1, c1, across, x2, y2, d2, down, x3, y3, c3]

        return ordered(values) + ordered(others)


GATHERED = [(side, k, flip) for side in range(2) for k in (0, 1, 2, 3) for flip in range(4)]


def gather_table(here, core, block_rows):
    side, k, flip = np.array(GATHERED, np.int32).T
    core, z, img = core ^ side, (here.z - k) % 4, here.img ^ flip
    last = (core == 1) & (z == 3) & (img == 3)
    rows = jnp.stack(block_rows(z, 4 * core + img), axis=1).reshape(-1)
    return jnp.concatenate([rows, jnp.argmax(last)[None]]).astype(jnp.int32)


def part(value, axis, index):
    return lax.dynamic_index_in_dim(value, index, axis, keepdims=False)


def add_part(kept, got, axis, index):
    both = [part(value.reshape(2, 2, 352, C), axis, index) for value in (kept, got)]
    return both[0] + both[1]


def halves_to_send(here, kept, got):
    return add_part(kept[0], got[0], 1, 1 - here.x), add_part(kept[1], got[1], 0, 1 - here.y)


def send_halves(a, b):
    return over_x(a), over_y(b)


def add_halves(here, kept, got, got_a, got_b):
    a = add_part(kept[0], got[0], 1, here.x) + got_a
    b = add_part(kept[1], got[1], 0, here.y) + got_b
    return a, b


def quarters_to_send(here, a, b):
    return part(a, 0, 1 - here.y), part(b, 0, 1 - here.x)


def send_quarters(a, b):
    return over_y(a), over_x(b)


def add_quarters(here, a, b, got_a, got_b):
    return (
        part(a, 0, here.y).astype(F32) + got_a.astype(F32),
        part(b, 0, here.x).astype(F32) + got_b.astype(F32),
    )


def by_plane(low_planes, first, second):
    halves = [first[:176], second[:176], first[176:], second[176:]]
    return jnp.stack(halves if low_planes else halves[2:] + halves[:2])


def send_planes(here, planes, more=None):
    planes16 = planes.astype(BF16)
    sent = [part(planes16, 0, (here.z + k) % 4) for k in (1, 3, 2)]
    if more is not None:
        sent = [jnp.concatenate([value, more.astype(BF16)], axis=0) for value in sent]
    return [z_shift(value, 4, k) for value, k in zip(sent, (1, 3, 2))]


def add_planes(here, planes, got, more=None):
    total = part(planes, 0, here.z)
    if more is not None:
        total = jnp.concatenate([total, more], axis=0)
    for value in got:
        total = total + value.astype(F32)
    return total


def over_two_planes(value):
    return along_z(value, [(0, 2), (2, 0), (1, 3), (3, 1)])


def sum_over_img(value):
    return (value + over_x(value)) + (over_y(value) + over_corner(value))


def adam(params, first, second, grad, step_count, rate):
    new_first = 0.5 * first + 0.5 * grad
    new_second = 0.9 * second + 0.1 * grad * grad
    update = (
        rate
        * (new_first / (1.0 - jnp.power(0.5, step_count)))
        / (jnp.sqrt(new_second / (1.0 - jnp.power(0.9, step_count))) + ADAM_EPSILON)
    )
    return update, new_first, new_second


def body(
    x_small,
    x_medium,
    x_large,
    cot_small,
    cot_medium,
    cot_large,
    band_rows,
    params,
    first_moment,
    second_moment,
    step,
    rate,
):
    here = Place()
    n_band, position = here.n_band, here.position
    plan = Plan([x_small.shape, x_medium.shape, x_large.shape], n_band)
    tables = make_tables(plan, band_rows, position)
    half = n_band // 2 * plan.piece
    rows, count = params.shape[0], here.count
    step_count, step_rate = step[0].astype(F32), rate[0]
    last = count - 1
    singles = 22 * C - last * rows

    images, cots = (x_small, x_medium, x_large), (cot_small, cot_medium, cot_large)
    if here.planes:
        shard16 = params.astype(BF16)
        before = lax.ppermute(params[rows - count :].astype(BF16), AXES, [(o, o + 1) for o in range(last)])

        def aligned(head, shard, size):
            both = jnp.concatenate([head, shard], axis=0)
            return lax.dynamic_slice_in_dim(both, count - here.owner, size, 0)

        before, x_sent = stage((before, chip_blocks(plan, position, images)))
        x_got = to_chips(plan, x_sent)
        x_got[1], before, later, core, band_rows = stage((x_got[1], before, position, here.core, band_rows))
        block = aligned(before, shard16, rows - 1)
        gather = Gather(jnp.concatenate([block, shard16[singles : singles + 16]], axis=0))
        values = gather.beside()
        tables = make_tables(plan, band_rows, later)
        values, x_got, tables, core, cots, params, first_moment, second_moment = stage(
            (values, x_got, tables, core, cots, params, first_moment, second_moment)
        )
        values = gather.first(values)
        values[3], core, later, cots = stage((values[3], core, position, cots))
        cot_sent = chip_blocks(plan, later, cots)
        table = gather_table(here, core, lambda z, place: [(8 * z + place) * 22])
        values, x_blocks, cot_sent, table = stage((values, to_cores(plan, x_got), cot_sent, table))
        values = gather.second(values)
        values[6], params, first_moment, second_moment, later = stage(
            (values[6], params, first_moment, second_moment, here.owner)
        )
        state = (params, first_moment, second_moment)
        far = [lax.dynamic_slice_in_dim(rows_of, 176 - later, 176, 0).astype(BF16) for rows_of in state]
        head = jnp.concatenate([rows_of[rows - count :] for rows_of in state], axis=1)
        near = [rows_of[:176] for rows_of in state]
        single_state = [rows_of[singles : singles + 16] for rows_of in state]
        table_again = gather_table(
            here,
            core,
            lambda z, place: [
                (8 * (z & 1) + place) * 22 + jnp.where(z < 2, 0, 11),
                (8 * (z | 2) + place) * 22 + jnp.where(z < 2, 11, 0),
            ],
        )
        values, others, far, head, near, single_state, table_again = stage(
            (
                values,
                gather.others(values, 4),
                jnp.concatenate(far, axis=1),
                head,
                near,
                single_state,
                table_again,
            )
        )
        values, more = stage((gather.third(values), gather.others(values[4:], 6)))
        cot_sent, values = stage((cot_sent, values))
        cot_got = to_chips(plan, cot_sent)
        pieces, parts = gather.pieces(values, others + more + gather.others(values[10:], 6)), ((0, rows - 1),)
        pieces, x_blocks = stage((pieces, x_blocks))
    else:
        pieces, parts = [lax.all_gather(params.astype(BF16), AXES, axis=0, tiled=True)], ((0, rows),)
        table = jnp.zeros((2,), jnp.int32)
        tables = make_tables(plan, band_rows, position)
        x_blocks = to_cores(plan, to_chips(plan, chip_blocks(plan, position, images)))
        cot_got = to_chips(plan, chip_blocks(plan, position, cots))
    x_img, a1, h1, a2, y, z, q, k, v, stats, small, weights = run_features(
        True, plan, tables, x_blocks, pieces, parts, table
    )
    cot_got, y = stage((cot_got, y))
    cot_blocks = to_cores(plan, cot_got)
    if here.planes:
        cot_blocks, far = stage((cot_blocks, far))
        far = over_two_planes(far)
    out_own, out_oth, dy, dy16, g_proj, sums3 = run_attend_both(
        plan, tables, q, k, v, y, z, cot_blocks, stats, small, weights
    )
    if here.planes:

        def stepped(state, grad):
            update, _, _ = adam(*state, grad, step_count, step_rate)
            return (state[0] - update).astype(BF16)

        dy16, far, out_oth = stage((dy16, far, out_oth))
        out_got = over_core(out_oth)
        *kept, early, sums_b2 = run_weight_grad(tables, 1, a2, dy16, g_proj)
        kept, sent = kept[:2], kept[2:]
        dy16, kept, sent, out_got = stage((dy16, kept, sent, out_got))
        got = [over_core(value) for value in sent]
        out_got = from_chips(plan, merge_cores(plan, position, out_own, out_got))
        dy16, kept, got, halves = stage((dy16, kept, got, halves_to_send(here, kept, got)))
        halves = send_halves(*halves)
        dh1, sums_n2 = run_data_grad(tables, 1, dy16, h1, stats, small, weights)
        dh1, kept, got, halves = stage((dh1, kept, got, halves))
        high = kept, got
        *kept, sums_b1 = run_weight_grad(tables, 0, a1, dh1, early)
        kept, sent = kept[:2], kept[2:]
        kept, sent, high, halves, out_got = stage((kept, sent, high, halves, out_got))
        got = [over_core(value) for value in sent]
        high = add_halves(here, *high, *halves)
        quarters = send_quarters(*quarters_to_send(here, *high))
        low = kept, got
        low, halves, high, quarters, dh1 = stage((low, halves_to_send(here, *low), high, quarters, dh1))
        halves = send_halves(*halves)
        high = by_plane(False, *add_quarters(here, *high, *quarters))
        high, dh1 = stage((high, dh1))
        high_got = send_planes(here, high)
        dx_own, dx_oth, sums_n1 = run_data_grad(
            tables, 0, dh1, x_img, stats, small, weights, dy=dy, half=out_own.shape[0]
        )
        low, halves, high, high_got, sums_n1 = stage((low, halves, high, high_got, sums_n1))
        low = add_halves(here, *low, *halves)
        sums = sums_n1 + sums_b1 + sums_n2 + sums_b2 + sums3
        low, low_sent, sums = stage((low, quarters_to_send(here, *low), sums + over_core(sums)))
        quarters = send_quarters(*low_sent)
        small_sum = sum_over_img(sums)
        low, quarters, small_sum, head = stage((low, quarters, small_sum, head))
        before = lax.ppermute(head, AXES, [(o, o + 1) for o in range(last)])
        low = by_plane(True, *add_quarters(here, *low, *quarters))
        low_got = send_planes(here, low, small_sum)
        low, low_got, before, far, high, high_got = stage((low, low_got, before, far, high, high_got))
        low, high = add_planes(here, low, low_got, small_sum), add_planes(here, high, high_got)
        low, small_sum = low[:176], low[176:]
        own = [
            aligned(before[:, i * C : (i + 1) * C], rows_of, 176) for i, rows_of in enumerate(near)
        ]
        far = [far[:, i * C : (i + 1) * C].astype(F32) for i in range(3)]
        first_two = here.z < 2
        block = [
            stepped([jnp.where(first_two, a, b) for a, b in zip(own, far)], low),
            stepped([jnp.where(first_two, b, a) for a, b in zip(own, far)], high),
            stepped(single_state, small_sum),
        ]
        gather = Gather(jnp.concatenate(block, axis=0))
        values, dx_got = stage((gather.first(), over_core(dx_oth)))
        dx_sent = merge_cores(plan, position, dx_own, dx_got)
        values, others, dx_sent, first_out = stage(
            (gather.second(values), gather.others(values, 4), dx_sent, to_bands(plan, position, out_got))
        )
        values, more = stage((gather.third(values), gather.others(values[4:], 6)))
        pieces = gather.pieces(values, others + more + gather.others(values[10:], 6))
        pieces, dx_sent = stage((pieces, dx_sent))
        dx_got = from_chips(plan, dx_sent)
        far = over_two_planes(jnp.where(here.z < 2, high, low).astype(BF16))
        table = table_again
        parts = ((0, 176), (176, 176))
    else:
        out_got = from_chips(plan, merge_cores(plan, position, out_own, over_core(out_oth)))
        g_w2, sums_b2 = run_weight_grad(tables, 1, a2, dy16)
        dh1, sums_n2 = run_data_grad(tables, 1, dy16, h1, stats, small, weights)
        g_w1, sums_b1 = run_weight_grad(tables, 0, a1, dh1)
        dx_own, dx_oth, sums_n1 = run_data_grad(
            tables, 0, dh1, x_img, stats, small, weights, dy=dy, half=out_own.shape[0]
        )
        dx_got = from_chips(plan, merge_cores(plan, position, dx_own, over_core(dx_oth)))
        small_rows = sums_n1 + sums_b1 + sums_n2 + sums_b2 + sums3
        full = jnp.concatenate([g_w1, g_w2, g_proj, small_rows.astype(BF16)], axis=0)
        full = jnp.pad(full, ((0, rows * count - full.shape[0]), (0, 0)))
        grad = lax.psum_scatter(full, AXES, scatter_dimension=0, tiled=True).astype(F32)
        weight_update, new_first, new_second = adam(
            params, first_moment, second_moment, grad, step_count, step_rate
        )
        pieces = [lax.all_gather((params - weight_update).astype(BF16), AXES, axis=0, tiled=True)]
    again_own, again_oth = run_features(False, plan, tables, (x_img, stats), pieces, parts, table)
    if here.planes:
        again_own, again_oth, dx_got, far = stage((again_own, again_oth, dx_got, far))
    again = from_chips(plan, merge_cores(plan, position, again_own, over_core(again_oth)))
    if here.planes:
        mine = jnp.concatenate([jnp.where(here.z < 2, low, high), far.astype(F32)], axis=0)
        follow = lax.ppermute(mine[:count], AXES, [(o, o - 1) for o in range(1, count)])
        follow, dx_got = stage((follow, dx_got))
        follow = jnp.where(here.owner == last, jnp.pad(small_sum, ((0, count - 16), (0, 0))), follow)
        grad = lax.dynamic_slice_in_dim(jnp.concatenate([mine, follow], axis=0), here.owner, rows, 0)
        weight_update, new_first, new_second = adam(
            params, first_moment, second_moment, grad, step_count, step_rate
        )
    else:
        first_out = to_bands(plan, position, out_got)
    input_grads = to_bands(plan, position, dx_got)
    second_out = to_bands(plan, position, again)
    return (*first_out, *second_out, *input_grads, weight_update, new_first, new_second)


def solution(mesh):
    image = P("img", "band", None, None)
    shard = P(("band", "img"), None)
    return jax.shard_map(
        body,
        mesh=mesh,
        in_specs=(image,) * 6 + (P(),) + (shard,) * 3 + (P(), P()),
        out_specs=(image,) * 9 + (shard,) * 3,
        check_vma=False,
    )
```
